128 devices in a mesh: inst: 16 (over z, x), tile: 8 (over y, core).
Axes of the slice: x: 4, y: 4, z: 4, core: 2. Of those that a mesh axis runs over, the one named last changes fastest.
Arguments:
- obs_values: bfloat16 [262144, 128], P(('inst', 'tile')), may hold values from -6 to 6
- obs_instrument: int32 [262144], P(('inst', 'tile')), may hold values from 0 to 15
- obs_target: int32 [262144, 1], P(('inst', 'tile')), may hold values from 0 to 127; in each aligned block of 2048 rows (0 to 2047, 2048 to 4095, ...) at most 32 rows name the same one
- obs_cell: int32 [262144], P(('inst', 'tile')), may hold values from 0 to 1023
- inst_bias: float32 [16, 128], replicated, may hold values from -5 to 5
- kernel: float32 [9, 128], replicated, may hold values from 0.1 to 1
- w_in: bfloat16 [128, 1024], replicated, may hold values from -0.5 to 0.5
- norm_gain: float32 [1024], replicated, may hold values from 0.1 to 1.9
- w_up: bfloat16 [1024, 1024], replicated, may hold values from -0.1875 to 0.1875
- w_down: bfloat16 [1024, 1024], replicated, may hold values from -0.1875 to 0.1875
- cotangent: bfloat16 [256, 512, 1024], P('tile', 'inst'), may hold values from -6 to 6
Outputs:
- predicted_field: bfloat16 [256, 512, 1024], P('tile', 'inst')
- grad_w_in: float32 [128, 1024], replicated
- grad_w_up: float32 [1024, 1024], replicated
- grad_w_down: float32 [1024, 1024], replicated
- grad_gain: float32 [1024], replicated
- filter_matrix_derivative: float32 [9, 128], replicated
- sensor_offset_derivative: float32 [16, 128], replicated
The draws below stay inside these ranges and needn't reach their ends.
Inputs may be any that keep to these rules, and one draw needn't show every extreme that they name: `obs_target`: among the rows of one device no tile is named by more than 32 rows, a bound that some block reaches.
All inputs are finite; a program needn't handle non-finite values.
Results may differ from the reference program's by a relative error of at most 0.008.
Values may be sent and summed in bfloat16 or wider, within the bound.
A program may use at most 128 MiB of HBM per device.

```python
import math
import jax
import jax.numpy as jnp
import numpy as np
from jax import lax

C = 128
TRUNK_FEATURES = 1024
INSTR = 16
LAT_DEV = 32
LON_DEV = 32
OBS_DEV = 2048
CAP = 32
OBS = 262144
PARALLEL_ROWS = 256
MERIDIAN_COLUMNS = 512
N_INST = 16
N_TILE = 8


def place_ends(entries, rng, least, high):
    dims = entries.shape
    index_at = [jax.random.randint(jax.random.fold_in(rng, axis), (), 0, dims[axis]) for axis in range(len(dims))]
    entries = entries.at[tuple(index_at)].set(least)
    longest = dims.index(max(dims))
    index_at[longest] = (index_at[longest] + 1) % dims[longest]
    return entries.at[tuple(index_at)].set(high)


def steps_of(key, shape, pieces, low, top_value):
    loudness, own = 1.0, jax.random.fold_in(key, 6)
    for dim, shards_of in pieces:
        heights = jnp.exp(jax.random.uniform(jax.random.fold_in(own, dim), (shards_of,), jnp.float32, low / len(pieces), top_value / len(pieces)))
        loudness = loudness * jnp.repeat(heights, shape[dim] // shards_of).reshape([-1 if axis == dim else 1 for axis in range(len(shape))])
    return loudness


def shared_out(own_key, own, number, rows, number_of, top, bound, skew):
    ranking = jax.random.permutation(own_key, number_of)
    packed, ordinary = shares(number_of, rows * top, bound, skew, True), shares(number_of, rows * top, bound, skew, False)
    places = jnp.arange(number_of)

    def named(sizes, offset_by):
        used = int((sizes > 0).sum())
        fixed = max(1, used // 4)
        passed = fixed + (places - fixed + offset_by * (used - fixed)) % max(1, number_of - fixed)
        return jnp.zeros((number_of,), jnp.int32).at[ranking[jnp.where(places < fixed, places, passed)]].set(jnp.asarray(sizes, jnp.int32))

    sizes = jnp.where(number % 4 == 0, named(packed, number // 4), named(ordinary, number - number // 4 - 1))
    mixed = jax.random.permutation(jax.random.fold_in(own, 3), number_of)
    giver, sink = mixed[0:number_of // 2 * 2:2], mixed[1:number_of // 2 * 2:2]
    margin = jnp.minimum(sizes[giver] - 1, bound - sizes[sink]) // 2
    margin = jnp.where((giver == ranking[0]) | (sink == ranking[0]) | (sizes[sink] == 0), 0, jnp.maximum(margin, 0))
    passed = jax.random.randint(jax.random.fold_in(own, 4), (number_of // 2,), 0, 1 << 20) % (margin + 1)
    sizes = sizes.at[giver].add(-passed).at[sink].add(passed)
    labels = jnp.searchsorted(jnp.cumsum(sizes), jnp.arange(rows * top), side="right").astype(jnp.int32)
    grid = labels.reshape(top, rows).T
    grid = grid[jax.random.permutation(jax.random.fold_in(own, 1), rows)]
    offset_by = jax.random.randint(jax.random.fold_in(own, 2), (rows, 1), 0, top)
    return jnp.take_along_axis(grid, (jnp.arange(top)[None, :] + offset_by) % top, axis=1)


def shares(amount, total, reach, lean, full):
    loads = [(1 << 20) // math.isqrt(grade ** lean) + 1 for grade in range(1, amount + 1)]
    largest = reach if full else min(reach, max(-(-total // amount), total * loads[0] // sum(loads)))
    least = 1 if total - largest >= amount - 1 else 0
    given, spare = [largest] + [least] * (amount - 1), total - largest - least * (amount - 1)
    while spare > 0:
        free = [i for i in range(1, amount) if given[i] < largest] or [i for i in range(1, amount) if given[i] < reach]
        whole, left = sum([loads[i] for i in free]), spare
        for i in free:
            extra = min(reach - given[i], max(1, left * loads[i] // whole), spare)
            given[i] = given[i] + extra
            spare = spare - extra
    return np.array(given)


def bell_draw(own_key, dims, width, limit, shards=(), held_as=jnp.bfloat16):
    loudness = steps_of(own_key, dims, shards, -0.22, 0.18) if shards else 1.0
    array = jax.random.normal(own_key, dims, jnp.float32) * width * loudness
    return jnp.minimum(jnp.maximum(array, -limit), limit).astype(held_as)


def setup_inputs(seed: int = 0) -> dict:
    streams_of = jax.random.split(jax.random.key(seed), 12)
    obs_values = bell_draw(streams_of[0], (OBS, C), 1.0, 6.0, ((0, 128),))
    obs_instrument = place_ends(jax.random.randint(streams_of[1], (OBS,), 0, INSTR), jax.random.fold_in(streams_of[1], 1), 0, INSTR - 1).astype(jnp.int32)
    obs_target_keys = jax.random.split(jax.random.fold_in(streams_of[2], 1), OBS // OBS_DEV)
    obs_target_turns = jax.random.permutation(jax.random.fold_in(streams_of[2], 3), OBS // OBS_DEV)
    obs_target = jax.vmap(lambda own, number: shared_out(jax.random.fold_in(streams_of[2], 2), own, number, OBS_DEV, N_INST * N_TILE, 1, CAP, 2))(obs_target_keys, obs_target_turns).reshape((OBS, 1))
    obs_cell = place_ends(jax.random.randint(streams_of[3], (OBS,), 0, LAT_DEV * LON_DEV), jax.random.fold_in(streams_of[3], 1), 0, (LAT_DEV * LON_DEV) - 1).astype(jnp.int32)
    inst_bias = bell_draw(streams_of[4], (INSTR, C), 1.0, 5.0, (), jnp.float32)
    kernel = jnp.clip(jnp.exp(jax.random.uniform(streams_of[5], (9, C), jnp.float32, math.log(0.1), math.log(1.0))), 0.1, 1.0)
    w_in = bell_draw(streams_of[6], (C, TRUNK_FEATURES), C ** -0.5, 0.5)
    norm_gain = jnp.clip(1.0 + 0.18 * jax.random.normal(streams_of[7], (TRUNK_FEATURES,), jnp.float32), 0.1, 1.9)
    w_up = bell_draw(streams_of[8], (TRUNK_FEATURES, TRUNK_FEATURES), TRUNK_FEATURES ** -0.5, 0.1875)
    w_down = bell_draw(streams_of[9], (TRUNK_FEATURES, TRUNK_FEATURES), TRUNK_FEATURES ** -0.5, 0.1875)
    cotangent = bell_draw(streams_of[10], (PARALLEL_ROWS, MERIDIAN_COLUMNS, TRUNK_FEATURES), 1.0, 6.0, ((0, 8), (1, 16)))
    return dict(obs_values=obs_values, obs_instrument=obs_instrument, obs_target=obs_target, obs_cell=obs_cell, inst_bias=inst_bias, kernel=kernel, w_in=w_in, norm_gain=norm_gain, w_up=w_up, w_down=w_down, cotangent=cotangent)


offsets = [(a, b) for a in (-1, 0, 1) for b in (-1, 0, 1)]

def shifted(padded, a, b):
    return padded[1 + a:1 + a + PARALLEL_ROWS, 1 + b:1 + b + MERIDIAN_COLUMNS]

def unshifted(padded, a, b):
    return padded[1 - a:1 - a + PARALLEL_ROWS, 1 - b:1 - b + MERIDIAN_COLUMNS]

def reference(obs_values, obs_instrument, obs_target, obs_cell, inst_bias, kernel, w_in, norm_gain, w_up, w_down, cotangent):
    feat = (obs_values.astype(jnp.float32) + inst_bias[obs_instrument]).astype(jnp.bfloat16)
    dest = obs_target[:, 0]
    lat_idx = dest % N_TILE * LAT_DEV + obs_cell // LON_DEV
    lon_idx = dest // N_TILE * LON_DEV + obs_cell % LON_DEV
    flat = (lat_idx * MERIDIAN_COLUMNS + lon_idx).astype(jnp.int32)
    sums = jax.ops.segment_sum(feat.astype(jnp.float32), flat, PARALLEL_ROWS * MERIDIAN_COLUMNS).reshape(PARALLEL_ROWS, MERIDIAN_COLUMNS, C)
    counts = jax.ops.segment_sum(jnp.ones((OBS,), jnp.float32), flat, PARALLEL_ROWS * MERIDIAN_COLUMNS).reshape(PARALLEL_ROWS, MERIDIAN_COLUMNS, 1)
    psums = jnp.pad(sums, ((1, 1), (1, 1), (0, 0)))
    pcounts = jnp.pad(counts, ((1, 1), (1, 1), (0, 0)))
    spread = jnp.zeros((PARALLEL_ROWS, MERIDIAN_COLUMNS, C), jnp.float32)
    density = jnp.zeros((PARALLEL_ROWS, MERIDIAN_COLUMNS, C), jnp.float32)
    for j, (a, b) in enumerate(offsets):
        spread = spread + kernel[j] * shifted(psums, a, b)
        density = density + kernel[j] * shifted(pcounts, a, b)
    enc32 = spread / (1.0 + density)
    enc = enc32.astype(jnp.bfloat16).reshape(-1, C)
    scale = 1.0 / (PARALLEL_ROWS * MERIDIAN_COLUMNS) ** 0.5
    dyb = (cotangent.astype(jnp.float32) * scale).astype(jnp.bfloat16).reshape(-1, TRUNK_FEATURES)
    blocks = N_INST * N_TILE
    rows = LAT_DEV * LON_DEV

    def inner(left, right):
        return lax.dot_general(left, right, (((0,), (0,)), ((), ())), preferred_element_type=jnp.float32)

    def along(left, right):
        return lax.dot_general(left, right, (((1,), (1,)), ((), ())), preferred_element_type=jnp.float32)

    def step(carry, block):
        enc_b, dy_b = block
        h0 = jnp.dot(enc_b, w_in, preferred_element_type=jnp.float32)
        rinv = lax.rsqrt(lax.optimization_barrier(jnp.mean(h0 * h0, axis=-1, keepdims=True)) + 1e-06)
        u = (h0 * rinv * norm_gain).astype(jnp.bfloat16)
        act = jnp.dot(u, w_up, preferred_element_type=jnp.float32)
        gl, gelu_back = jax.vjp(jax.nn.gelu, act)
        g = gl.astype(jnp.bfloat16)
        y = (h0 + jnp.dot(g, w_down, preferred_element_type=jnp.float32)).astype(jnp.bfloat16)
        gw_down = inner(g, dy_b)
        dact = gelu_back(along(dy_b, w_down))[0].astype(jnp.bfloat16)
        gw_up = inner(u, dact)
        du = along(dact, w_up)
        g_gain = lax.optimization_barrier(jnp.sum(du * h0 * rinv, axis=0))
        t = du * norm_gain
        dh = (rinv * t - h0 * rinv ** 3 * lax.optimization_barrier(jnp.mean(t * h0, axis=-1, keepdims=True)) + dy_b.astype(jnp.float32)).astype(jnp.bfloat16)
        gw_in = inner(enc_b, dh)
        denc = along(dh, w_in)
        new = (carry[0] + gw_in, carry[1] + gw_up, carry[2] + gw_down, carry[3] + g_gain)
        return (new, (y, denc))
    init = (jnp.zeros((C, TRUNK_FEATURES), jnp.float32), jnp.zeros((TRUNK_FEATURES, TRUNK_FEATURES), jnp.float32), jnp.zeros((TRUNK_FEATURES, TRUNK_FEATURES), jnp.float32), jnp.zeros((TRUNK_FEATURES,), jnp.float32))
    learnable_derivatives, (looped_results, dencs) = lax.scan(step, init, (enc.reshape(blocks, rows, C), dyb.reshape(blocks, rows, TRUNK_FEATURES)))
    predicted_field = looped_results.reshape(PARALLEL_ROWS, MERIDIAN_COLUMNS, TRUNK_FEATURES)
    denc = dencs.reshape(PARALLEL_ROWS, MERIDIAN_COLUMNS, C)
    dspread = denc / (1.0 + density)
    ddensity = -dspread * enc32
    gk_rows = []
    for j, (a, b) in enumerate(offsets):
        gk_rows.append(lax.optimization_barrier(jnp.sum(dspread * shifted(psums, a, b) + ddensity * shifted(pcounts, a, b), axis=(0, 1))))
    filter_matrix_derivative = jnp.stack(gk_rows)
    pgrad = jnp.pad(dspread, ((1, 1), (1, 1), (0, 0)))
    dsums = jnp.zeros((PARALLEL_ROWS, MERIDIAN_COLUMNS, C), jnp.float32)
    for j, (a, b) in enumerate(offsets):
        dsums = dsums + kernel[j] * unshifted(pgrad, a, b)
    d_obs = dsums.reshape(-1, C)[flat]
    sensor_offset_derivative = jax.ops.segment_sum(d_obs, obs_instrument, INSTR)
    return (predicted_field, learnable_derivatives[0], learnable_derivatives[1], learnable_derivatives[2], learnable_derivatives[3], filter_matrix_derivative, sensor_offset_derivative)
```

```python
import jax
import jax.numpy as jnp
from jax import lax
from jax.sharding import PartitionSpec as P

offsets = [(a, b) for a in (-1, 0, 1) for b in (-1, 0, 1)]
f32, bf16 = jnp.float32, jnp.bfloat16


def padded_2(shard, sides, width):
    for axis, dim in sides:
        size, length = (lax.axis_size(axis), shard.shape[dim])
        up = [(i, (i + 1) % size) for i in range(size - 1)]
        down = [(j, i) for i, j in up]
        last = lax.slice_in_dim(shard, length - width, length, axis=dim)
        first = lax.slice_in_dim(shard, 0, width, axis=dim)
        before = lax.ppermute(last, axis, up)
        after = lax.ppermute(first, axis, down)
        shard = jnp.concatenate([before, shard, after], axis=dim)
    return shard


def inner(left, right, precision=None):
    return lax.dot_general(
        left,
        right,
        (((0,), (0,)), ((), ())),
        precision=precision,
        preferred_element_type=f32,
    )


def along(left, right):
    return lax.dot_general(left, right, (((1,), (1,)), ((), ())), preferred_element_type=f32)


def pack(obs_values, obs_instrument, obs_target, obs_cell, inst_bias, devices, capacity, lon_cols):
    obs_rows, channels = obs_values.shape
    instruments = inst_bias.shape[0]
    pick = (obs_instrument[:, None] == jnp.arange(instruments)[None, :]).astype(f32)
    feat = (
        obs_values.astype(f32) + jnp.dot(pick, inst_bias, precision=lax.Precision.HIGHEST)
    ).astype(bf16)
    target = obs_target[:, 0]
    hits = (target[:, None] == jnp.arange(devices)[None, :]).astype(bf16)
    block = 256
    hits3 = hits.reshape(obs_rows // block, block, devices)
    below = (jnp.arange(block)[:, None] > jnp.arange(block)[None, :]).astype(bf16)
    within = lax.dot_general(
        jnp.broadcast_to(below, (obs_rows // block, block, block)),
        hits3,
        (((2,), (1,)), ((0,), (0,))),
        preferred_element_type=f32,
    )
    totals = jnp.sum(hits3.astype(f32), axis=1)
    ahead = jnp.cumsum(totals, axis=0) - totals
    before = within + ahead[:, None, :]
    slot = jnp.sum(before * hits3.astype(f32), axis=2).reshape(obs_rows).astype(jnp.int32)
    place = target * capacity + slot
    lat, lon = obs_cell // lon_cols, obs_cell % lon_cols
    notes = jnp.stack([lat, lon, obs_instrument, jnp.ones_like(lat)], axis=1).astype(bf16)
    notes = jnp.pad(notes, ((0, 0), (0, channels - 4)))
    choose = (jnp.arange(devices * capacity)[:, None] == place[None, :]).astype(bf16)
    packed = jnp.dot(choose, jnp.concatenate([feat, notes], axis=1), preferred_element_type=f32)
    rows = packed[:, :channels].astype(bf16)
    tags = packed[:, channels : channels + 4].astype(jnp.int32)
    code = ((tags[:, 2] * 32 + tags[:, 0]) * lon_cols + tags[:, 1] + 1) * tags[:, 3]
    return rows, code


def shards(
    obs_values,
    obs_instrument,
    obs_target,
    obs_cell,
    inst_bias,
    kernel,
    w_in,
    norm_gain,
    w_up,
    w_down,
    cotangent,
):
    n_inst = lax.axis_size("inst")
    n_tile = lax.axis_size("tile")
    devices = n_inst * n_tile
    obs_rows, channels = obs_values.shape
    capacity = 2 * obs_rows // devices
    lat_rows, lon_cols, width = cotangent.shape
    cells = lat_rows * lon_cols
    instruments = inst_bias.shape[0]
    rows, code = pack(
        obs_values, obs_instrument, obs_target, obs_cell, inst_bias, devices, capacity, lon_cols
    )
    got_rows = lax.all_to_all(
        rows.reshape(devices, capacity, channels), ("inst", "tile"), 0, 0, tiled=True
    ).reshape(-1, channels)
    got_code = lax.all_to_all(
        code.reshape(devices, capacity), ("inst", "tile"), 0, 0, tiled=True
    ).reshape(-1)
    used = got_code > 0
    cell = jnp.where(used, (got_code - 1) % cells, -1)
    instr = jnp.where(used, (got_code - 1) // cells, -1)
    lands = (jnp.arange(cells)[:, None] == cell[None, :]).astype(bf16)
    kinds = (instr[:, None] == jnp.arange(channels)[None, :]).astype(bf16)
    both = jnp.dot(
        lands, jnp.concatenate([got_rows, kinds], axis=1), preferred_element_type=f32
    ).reshape(lat_rows, lon_cols, 2 * channels)[:, :, : channels + instruments]
    padded = padded_2(both, (("tile", 0), ("inst", 1)), 1)
    psums, pkinds = padded[:, :, :channels], padded[:, :, channels:]
    pcounts = jnp.sum(pkinds, axis=2, keepdims=True)

    def shifted(padded, a, b):
        return padded[1 + a : 1 + a + lat_rows, 1 + b : 1 + b + lon_cols]

    spread = jnp.zeros((lat_rows, lon_cols, channels), f32)
    density = jnp.zeros((lat_rows, lon_cols, channels), f32)
    for j, (a, b) in enumerate(offsets):
        spread = spread + kernel[j] * shifted(psums, a, b)
        density = density + kernel[j] * shifted(pcounts, a, b)
    enc32 = spread / (1.0 + density)
    enc = enc32.astype(bf16).reshape(cells, channels)
    h0 = jnp.dot(enc, w_in, preferred_element_type=f32)
    rinv = lax.rsqrt(jnp.mean(h0 * h0, axis=-1, keepdims=True) + 1e-06)
    normed = (h0 * rinv * norm_gain).astype(bf16)
    act = jnp.dot(normed, w_up, preferred_element_type=f32)
    gelu_out, gelu_back = jax.vjp(jax.nn.gelu, act)
    hidden = gelu_out.astype(bf16)
    predicted_field = (
        (h0 + jnp.dot(hidden, w_down, preferred_element_type=f32))
        .astype(bf16)
        .reshape(lat_rows, lon_cols, width)
    )
    scale = 1.0 / (lat_rows * n_tile * lon_cols * n_inst) ** 0.5
    dyb = (cotangent.astype(f32) * scale).astype(bf16).reshape(cells, width)
    gw_down = inner(hidden, dyb)
    dact = gelu_back(along(dyb, w_down))[0].astype(bf16)
    gw_up = inner(normed, dact)
    dnormed = along(dact, w_up)
    g_gain = jnp.sum(dnormed * h0 * rinv, axis=0)
    scaled = dnormed * norm_gain
    dh = (
        rinv * scaled
        - h0 * rinv**3 * jnp.mean(scaled * h0, axis=-1, keepdims=True)
        + dyb.astype(f32)
    ).astype(bf16)
    gw_in = inner(enc, dh)
    denc = along(dh, w_in).reshape(lat_rows, lon_cols, channels)
    dspread = denc / (1.0 + density)
    ddensity = -dspread * enc32
    kernel_rows = []
    bias = jnp.zeros((instruments, channels), f32)
    flat = dspread.reshape(cells, channels)
    for j, (a, b) in enumerate(offsets):
        near = shifted(pkinds, a, b)
        kernel_rows.append(
            jnp.sum(dspread * shifted(psums, a, b) + ddensity * shifted(pcounts, a, b), axis=(0, 1))
        )
        bias = bias + kernel[j] * inner(
            near.reshape(cells, instruments), flat, lax.Precision.HIGHEST
        )
    g_kernel = jnp.stack(kernel_rows)
    totals = lax.psum((gw_in, gw_up, gw_down, g_gain, g_kernel, bias), ("inst", "tile"))
    return (predicted_field, *totals)


def solution(mesh):
    return jax.shard_map(
        shards,
        mesh=mesh,
        in_specs=(
            P(("inst", "tile"), None),
            P(("inst", "tile")),
            P(("inst", "tile"), None),
            P(("inst", "tile")),
            P(),
            P(),
            P(),
            P(),
            P(),
            P(),
            P("tile", "inst", None),
        ),
        out_specs=(P("tile", "inst", None), P(), P(), P(), P(), P(), P()),
        check_vma=False,
    )
```

```python
import jax
import jax.numpy as jnp
from jax import lax
from jax.experimental import pallas as pl
from jax.experimental.pallas import tpu as pltpu
from jax.sharding import PartitionSpec as P

offsets = [(a, b) for a in (-1, 0, 1) for b in (-1, 0, 1)]
f32, bf16 = jnp.float32, jnp.bfloat16


def padded_2(shard, sides, width):
    for axis, dim in sides:
        size, length = (lax.axis_size(axis), shard.shape[dim])
        up = [(i, (i + 1) % size) for i in range(size - 1)]
        down = [(j, i) for i, j in up]
        last = lax.slice_in_dim(shard, length - width, length, axis=dim)
        first = lax.slice_in_dim(shard, 0, width, axis=dim)
        before = lax.ppermute(last, axis, up)
        after = lax.ppermute(first, axis, down)
        shard = jnp.concatenate([before, shard, after], axis=dim)
    return shard


def inner(left, right, precision=None):
    return lax.dot_general(
        left,
        right,
        (((0,), (0,)), ((), ())),
        precision=precision,
        preferred_element_type=f32,
    )


def along(left, right):
    return lax.dot_general(left, right, (((1,), (1,)), ((), ())), preferred_element_type=f32)


MESH = pl.DeviceIdType.MESH
HALF = 1152
ROWS = 1024
STREAMS = (
    (0, 256, ("x", "y", "z")),
    (256, 128, ("y", "z", "x")),
    (384, 128, ("z", "x", "y")),
    (512, 128, ("x", "y", "z")),
    (640, 256, ("y", "z", "x")),
    (896, 128, ("z", "x", "y")),
    (1024, 128, ("z", "x", "y")),
)


def place():
    inst, tile = lax.axis_index("inst"), lax.axis_index("tile")
    return {"z": inst // 4, "x": inst % 4, "y": tile // 2, "core": tile % 2}


def device_at(at):
    return (at["z"] * 4 + at["x"], at["y"] * 2 + at["core"])


def moved(at, axis, step):
    size = 2 if axis == "core" else 4
    return {**at, axis: lax.rem(at[axis] + step, size)}


def send(source, target, send_sem, recv_sem, at):
    copy = pltpu.make_async_remote_copy(
        src_ref=source,
        dst_ref=target,
        send_sem=send_sem,
        recv_sem=recv_sem,
        device_id=device_at(at),
        device_id_type=MESH,
    )
    copy.start()
    return copy


def aligned(index, size):
    return pl.ds(pl.multiple_of(index * size, size), size)


class Stream:
    def __init__(self, number, at, t, o, bufs, send_sem, recv_sem):
        first, wide, self.order = STREAMS[number]
        self.cols = pl.ds(first, wide)
        self.wide = wide
        self.at, self.t, self.o = at, t, o
        self.core_in, self.core_sum, self.ins, self.outs = bufs
        self.sends, self.recvs = send_sem.at[number], recv_sem.at[number]
        self.started = []
        self.core = at["core"]

    def go(self, source, target, slot, at):
        copy = send(source, target, self.sends.at[slot], self.recvs.at[slot], at)
        self.started.append(copy)
        return copy

    def core_scatter(self):
        other = moved(self.at, "core", 1)
        self.pending = [
            self.go(
                self.t.at[1 - self.core, :, self.cols], self.core_in.at[:, self.cols], 0, other
            )
        ]

    def core_add(self):
        for copy in self.pending:
            copy.wait_recv()
        step = 128

        def body(i, carry):
            rows = aligned(i, step)
            total = self.t[self.core, rows, self.cols].astype(f32) + self.core_in[
                rows, self.cols
            ].astype(f32)
            self.core_sum[rows, self.cols] = total.astype(bf16)
            return carry

        lax.fori_loop(0, ROWS // step, body, 0)

    def axis_scatter(self, level):
        axis, size = self.order[level], (256, 64, 16)[level]
        source = self.core_sum if level == 0 else self.outs[level - 1]
        self.pending = []
        for step in (1, 2, 3):
            peer = moved(self.at, axis, step)
            self.pending.append(
                self.go(
                    source.at[aligned(peer[axis], size), self.cols],
                    self.ins[level].at[step - 1, :, self.cols],
                    1 + 3 * level + step - 1,
                    peer,
                )
            )

    def axis_add(self, level):
        axis, size = self.order[level], (256, 64, 16)[level]
        source = self.core_sum if level == 0 else self.outs[level - 1]
        for copy in self.pending:
            copy.wait_recv()
        step = min(size, 64)

        def body(i, carry):
            rows = aligned(i, step)
            mine = pl.ds(pl.multiple_of(self.at[axis] * size + i * step, step), step)
            total = source[mine, self.cols].astype(f32)
            for j in range(3):
                total = total + self.ins[level][j, rows, self.cols].astype(f32)
            if level < 2:
                self.outs[level][rows, self.cols] = total.astype(bf16)
            else:
                self.o[self.core, self.owned(2), self.cols] = total.astype(bf16)
            return carry

        lax.fori_loop(0, size // step, body, 0)

    def owned(self, level):
        start = 0
        for axis, size in list(zip(self.order, (256, 64, 16)))[: level + 1]:
            start = start + self.at[axis] * size
        size = (256, 64, 16)[level]
        return pl.ds(pl.multiple_of(start, size), size)

    def axis_gather(self, level):
        axis = self.order[level]
        rows = self.owned(level)
        self.pending = []
        for step in (1, 2, 3):
            peer = moved(self.at, axis, step)
            part = self.o.at[self.core, rows, self.cols]
            self.pending.append(self.go(part, part, 10 + 3 * (2 - level) + step - 1, peer))

    def gather_wait(self):
        for copy in self.pending:
            copy.wait_recv()

    def core_gather(self):
        part = self.o.at[self.core, :, self.cols]
        self.pending = [self.go(part, part, 19, moved(self.at, "core", 1))]

    def finish(self):
        self.gather_wait()
        for copy in self.started:
            copy.wait_send()


def greet(at):
    barrier = pltpu.get_barrier_semaphore()
    peers = [moved(at, axis, step) for axis in ("x", "y", "z") for step in (1, 2, 3)]
    peers.append(moved(at, "core", 1))
    for peer in peers:
        pl.semaphore_signal(barrier, inc=1, device_id=device_at(peer), device_id_type=MESH)
    pl.semaphore_wait(barrier, len(peers))


def reduce_scratch():
    return [
        pltpu.VMEM((ROWS, HALF), bf16),
        pltpu.VMEM((ROWS, HALF), bf16),
        pltpu.VMEM((3, 256, HALF), bf16),
        pltpu.VMEM((3, 64, HALF), bf16),
        pltpu.VMEM((3, 16, HALF), bf16),
        pltpu.VMEM((256, HALF), bf16),
        pltpu.VMEM((64, HALF), bf16),
        pltpu.SemaphoreType.DMA((len(STREAMS), 20)),
        pltpu.SemaphoreType.DMA((len(STREAMS), 20)),
    ]


def reduce_kernel(t, o, core_in, core_sum, in0, in1, in2, out0, out1, send_sem, recv_sem):
    at = place()
    greet(at)
    bufs = (core_in, core_sum, (in0, in1, in2), (out0, out1))
    streams = [Stream(k, at, t, o, bufs, send_sem, recv_sem) for k in range(len(STREAMS))]
    for s in streams:
        s.core_scatter()
    for s in streams:
        s.core_add()
        s.axis_scatter(0)
    for level in (0, 1):
        for s in streams:
            s.axis_add(level)
            s.axis_scatter(level + 1)
    for s in streams:
        s.axis_add(2)
        s.axis_gather(2)
    for level in (1, 0):
        for s in streams:
            s.gather_wait()
            s.axis_gather(level)
    for s in streams:
        s.gather_wait()
        s.core_gather()
    for s in streams:
        s.finish()


def all_reduce(t):
    return pl.pallas_call(
        reduce_kernel,
        out_shape=jax.ShapeDtypeStruct((2, ROWS, HALF), bf16),
        in_specs=[pl.BlockSpec(memory_space=pltpu.VMEM)],
        out_specs=pl.BlockSpec(memory_space=pltpu.VMEM),
        scratch_shapes=reduce_scratch(),
        compiler_params=pltpu.CompilerParams(
            collective_id=0, has_side_effects=True, vmem_limit_bytes=56 << 20
        ),
    )(t)


def pack_grads(gw_down, gw_up, gw_in_t, g_gain, g_kernel, bias):
    small = jnp.concatenate([g_gain.reshape(8, 128), g_kernel, bias], axis=0)
    small = jnp.pad(small, ((0, ROWS - small.shape[0]), (0, 0)))
    halves = [
        jnp.concatenate([gw_down[:, :512], gw_up[:, :512], gw_in_t], axis=1),
        jnp.concatenate([gw_down[:, 512:], gw_up[:, 512:], small], axis=1),
    ]
    return jnp.stack(halves).astype(bf16)


def unpack_grads(o):
    gw_down = jnp.concatenate([o[0, :, :512], o[1, :, :512]], axis=1).astype(f32)
    gw_up = jnp.concatenate([o[0, :, 512:1024], o[1, :, 512:1024]], axis=1).astype(f32)
    gw_in = o[0, :, 1024:].T.astype(f32)
    small = o[1, :33, 1024:].astype(f32)
    return gw_in, gw_up, gw_down, small[:8].reshape(1024), small[8:17], small[17:33]


def pack(obs_values, obs_instrument, obs_target, obs_cell, inst_bias, devices, capacity, lon_cols):
    obs_rows, channels = obs_values.shape
    instruments = inst_bias.shape[0]
    pick = (obs_instrument[:, None] == jnp.arange(instruments)[None, :]).astype(f32)
    feat = (
        obs_values.astype(f32) + jnp.dot(pick, inst_bias, precision=lax.Precision.HIGHEST)
    ).astype(bf16)
    target = obs_target[:, 0]
    hits = (target[:, None] == jnp.arange(devices)[None, :]).astype(bf16)
    block = 256
    hits3 = hits.reshape(obs_rows // block, block, devices)
    below = (jnp.arange(block)[:, None] > jnp.arange(block)[None, :]).astype(bf16)
    within = lax.dot_general(
        jnp.broadcast_to(below, (obs_rows // block, block, block)),
        hits3,
        (((2,), (1,)), ((0,), (0,))),
        preferred_element_type=f32,
    )
    totals = jnp.sum(hits3.astype(f32), axis=1)
    ahead = jnp.cumsum(totals, axis=0) - totals
    before = within + ahead[:, None, :]
    slot = jnp.sum(before * hits3.astype(f32), axis=2).reshape(obs_rows).astype(jnp.int32)
    place = target * capacity + slot
    lat, lon = obs_cell // lon_cols, obs_cell % lon_cols
    notes = jnp.stack([lat, lon, obs_instrument, jnp.ones_like(lat)], axis=1).astype(bf16)
    notes = jnp.pad(notes, ((0, 0), (0, channels - 4)))
    choose = (jnp.arange(devices * capacity)[:, None] == place[None, :]).astype(bf16)
    packed = jnp.dot(choose, jnp.concatenate([feat, notes], axis=1), preferred_element_type=f32)
    rows = packed[:, :channels].astype(bf16)
    tags = packed[:, channels : channels + 4].astype(jnp.int32)
    code = ((tags[:, 2] * 32 + tags[:, 0]) * lon_cols + tags[:, 1] + 1) * tags[:, 3]
    return rows, code


def shards(
    obs_values,
    obs_instrument,
    obs_target,
    obs_cell,
    inst_bias,
    kernel,
    w_in,
    norm_gain,
    w_up,
    w_down,
    cotangent,
):
    n_inst = lax.axis_size("inst")
    n_tile = lax.axis_size("tile")
    devices = n_inst * n_tile
    obs_rows, channels = obs_values.shape
    capacity = 2 * obs_rows // devices
    lat_rows, lon_cols, width = cotangent.shape
    cells = lat_rows * lon_cols
    instruments = inst_bias.shape[0]
    rows, code = pack(
        obs_values, obs_instrument, obs_target, obs_cell, inst_bias, devices, capacity, lon_cols
    )
    got_rows = lax.all_to_all(
        rows.reshape(devices, capacity, channels), ("inst", "tile"), 0, 0, tiled=True
    ).reshape(-1, channels)
    got_code = lax.all_to_all(
        code.reshape(devices, capacity), ("inst", "tile"), 0, 0, tiled=True
    ).reshape(-1)
    used = got_code > 0
    cell = jnp.where(used, (got_code - 1) % cells, -1)
    instr = jnp.where(used, (got_code - 1) // cells, -1)
    lands = (jnp.arange(cells)[:, None] == cell[None, :]).astype(bf16)
    kinds = (instr[:, None] == jnp.arange(channels)[None, :]).astype(bf16)
    both = jnp.dot(
        lands, jnp.concatenate([got_rows, kinds], axis=1), preferred_element_type=f32
    ).reshape(lat_rows, lon_cols, 2 * channels)[:, :, : channels + instruments]
    padded = padded_2(both, (("tile", 0), ("inst", 1)), 1)
    psums, pkinds = padded[:, :, :channels], padded[:, :, channels:]
    pcounts = jnp.sum(pkinds, axis=2, keepdims=True)

    def shifted(padded, a, b):
        return padded[1 + a : 1 + a + lat_rows, 1 + b : 1 + b + lon_cols]

    spread = jnp.zeros((lat_rows, lon_cols, channels), f32)
    density = jnp.zeros((lat_rows, lon_cols, channels), f32)
    for j, (a, b) in enumerate(offsets):
        spread = spread + kernel[j] * shifted(psums, a, b)
        density = density + kernel[j] * shifted(pcounts, a, b)
    enc32 = spread / (1.0 + density)
    enc = enc32.astype(bf16).reshape(cells, channels)
    h0 = jnp.dot(enc, w_in, preferred_element_type=f32)
    rinv = lax.rsqrt(jnp.mean(h0 * h0, axis=-1, keepdims=True) + 1e-06)
    normed = (h0 * rinv * norm_gain).astype(bf16)
    act = jnp.dot(normed, w_up, preferred_element_type=f32)
    gelu_out, gelu_back = jax.vjp(jax.nn.gelu, act)
    hidden = gelu_out.astype(bf16)
    predicted_field = (
        (h0 + jnp.dot(hidden, w_down, preferred_element_type=f32))
        .astype(bf16)
        .reshape(lat_rows, lon_cols, width)
    )
    scale = 1.0 / (lat_rows * n_tile * lon_cols * n_inst) ** 0.5
    dyb = (cotangent.astype(f32) * scale).astype(bf16).reshape(cells, width)
    gw_down = inner(hidden, dyb)
    dact = gelu_back(along(dyb, w_down))[0].astype(bf16)
    gw_up = inner(normed, dact)
    dnormed = along(dact, w_up)
    g_gain = jnp.sum(dnormed * h0 * rinv, axis=0)
    scaled = dnormed * norm_gain
    dh = (
        rinv * scaled
        - h0 * rinv**3 * jnp.mean(scaled * h0, axis=-1, keepdims=True)
        + dyb.astype(f32)
    ).astype(bf16)
    gw_in_t = inner(dh, enc)
    denc = along(dh, w_in).reshape(lat_rows, lon_cols, channels)
    dspread = denc / (1.0 + density)
    ddensity = -dspread * enc32
    kernel_rows = []
    bias = jnp.zeros((instruments, channels), f32)
    flat = dspread.reshape(cells, channels)
    for j, (a, b) in enumerate(offsets):
        near = shifted(pkinds, a, b)
        kernel_rows.append(
            jnp.sum(dspread * shifted(psums, a, b) + ddensity * shifted(pcounts, a, b), axis=(0, 1))
        )
        bias = bias + kernel[j] * inner(
            near.reshape(cells, instruments), flat, lax.Precision.HIGHEST
        )
    g_kernel = jnp.stack(kernel_rows)
    totals = unpack_grads(
        all_reduce(pack_grads(gw_down, gw_up, gw_in_t, g_gain, g_kernel, bias))
    )
    return (predicted_field, *totals)


def solution(mesh):
    return jax.shard_map(
        shards,
        mesh=mesh,
        in_specs=(
            P(("inst", "tile"), None),
            P(("inst", "tile")),
            P(("inst", "tile"), None),
            P(("inst", "tile")),
            P(),
            P(),
            P(),
            P(),
            P(),
            P(),
            P("tile", "inst", None),
        ),
        out_specs=(P("tile", "inst", None), P(), P(), P(), P(), P(), P()),
        check_vma=False,
    )
```

```python
import jax
import jax.numpy as jnp
from jax import lax
from jax.experimental import pallas as pl
from jax.experimental.pallas import tpu as pltpu
from jax.sharding import PartitionSpec as P

offsets = [(a, b) for a in (-1, 0, 1) for b in (-1, 0, 1)]
f32, bf16 = jnp.float32, jnp.bfloat16


def inner(left, right, precision=None):
    return lax.dot_general(
        left,
        right,
        (((0,), (0,)), ((), ())),
        precision=precision,
        preferred_element_type=f32,
    )


def along(left, right):
    return lax.dot_general(left, right, (((1,), (1,)), ((), ())), preferred_element_type=f32)


MESH = pl.DeviceIdType.MESH
HALF = 1152
ROWS = 1024
STREAMS = (
    (0, 256, ("x", "y", "z")),
    (256, 128, ("y", "z", "x")),
    (384, 128, ("z", "x", "y")),
    (512, 128, ("x", "y", "z")),
    (640, 256, ("y", "z", "x")),
    (896, 128, ("z", "x", "y")),
    (1024, 128, ("z", "x", "y")),
)


def place():
    inst, tile = lax.axis_index("inst"), lax.axis_index("tile")
    return {"z": inst // 4, "x": inst % 4, "y": tile // 2, "core": tile % 2}


def device_at(at):
    return (at["z"] * 4 + at["x"], at["y"] * 2 + at["core"])


def moved(at, axis, step):
    size = 2 if axis == "core" else 4
    return {**at, axis: lax.rem(at[axis] + step, size)}


def send_to(source, landing, send_sem, recv_sem, to):
    copy = pltpu.make_async_remote_copy(
        src_ref=source,
        dst_ref=landing,
        send_sem=send_sem,
        recv_sem=recv_sem,
        device_id=to,
        device_id_type=MESH,
    )
    copy.start()
    return copy


def aligned(index, size):
    return pl.ds(pl.multiple_of(index * size, size), size)


class Stream:
    def __init__(self, number, at, t, o, bufs, send_sem, recv_sem):
        first, wide, self.order = STREAMS[number]
        self.cols = pl.ds(first, wide)
        self.wide = wide
        self.at, self.t, self.o = at, t, o
        self.core_in, self.core_sum, self.ins, self.outs = bufs
        self.sends, self.recvs = send_sem.at[number], recv_sem.at[number]
        self.started = []
        self.core = at["core"]

    def go(self, source, target, slot, at):
        copy = send_to(
            source, target, self.sends.at[slot], self.recvs.at[slot], device_at(at)
        )
        self.started.append(copy)
        return copy

    def core_scatter(self):
        other = moved(self.at, "core", 1)
        self.pending = [
            self.go(
                self.t.at[1 - self.core, :, self.cols], self.core_in.at[:, self.cols], 0, other
            )
        ]

    def core_add(self):
        for copy in self.pending:
            copy.wait_recv()
        step = 128

        def body(i, carry):
            rows = aligned(i, step)
            total = self.t[self.core, rows, self.cols].astype(f32) + self.core_in[
                rows, self.cols
            ].astype(f32)
            self.core_sum[rows, self.cols] = total.astype(bf16)
            return carry

        lax.fori_loop(0, ROWS // step, body, 0)

    def axis_scatter(self, level):
        axis, size = self.order[level], (256, 64, 16)[level]
        source = self.core_sum if level == 0 else self.outs[level - 1]
        self.pending = []
        for step in (1, 2, 3):
            peer = moved(self.at, axis, step)
            self.pending.append(
                self.go(
                    source.at[aligned(peer[axis], size), self.cols],
                    self.ins[level].at[step - 1, :, self.cols],
                    1 + 3 * level + step - 1,
                    peer,
                )
            )

    def axis_add(self, level):
        axis, size = self.order[level], (256, 64, 16)[level]
        source = self.core_sum if level == 0 else self.outs[level - 1]
        for copy in self.pending:
            copy.wait_recv()
        step = min(size, 64)

        def body(i, carry):
            rows = aligned(i, step)
            mine = pl.ds(pl.multiple_of(self.at[axis] * size + i * step, step), step)
            total = source[mine, self.cols].astype(f32)
            for j in range(3):
                total = total + self.ins[level][j, rows, self.cols].astype(f32)
            if level < 2:
                self.outs[level][rows, self.cols] = total.astype(bf16)
            else:
                self.o[self.core, self.owned(2), self.cols] = total.astype(bf16)
            return carry

        lax.fori_loop(0, size // step, body, 0)

    def owned(self, level):
        start = 0
        for axis, size in list(zip(self.order, (256, 64, 16)))[: level + 1]:
            start = start + self.at[axis] * size
        size = (256, 64, 16)[level]
        return pl.ds(pl.multiple_of(start, size), size)

    def axis_gather(self, level):
        axis = self.order[level]
        rows = self.owned(level)
        self.pending = []
        for step in (1, 2, 3):
            peer = moved(self.at, axis, step)
            part = self.o.at[self.core, rows, self.cols]
            self.pending.append(self.go(part, part, 10 + 3 * (2 - level) + step - 1, peer))

    def gather_wait(self):
        for copy in self.pending:
            copy.wait_recv()

    def core_gather(self):
        part = self.o.at[self.core, :, self.cols]
        self.pending = [self.go(part, part, 19, moved(self.at, "core", 1))]

    def finish(self):
        self.gather_wait()
        for copy in self.started:
            copy.wait_send()


def greet(at):
    barrier = pltpu.get_barrier_semaphore()
    peers = [moved(at, axis, step) for axis in ("x", "y", "z") for step in (1, 2, 3)]
    peers.append(moved(at, "core", 1))
    for peer in peers:
        pl.semaphore_signal(barrier, inc=1, device_id=device_at(peer), device_id_type=MESH)
    pl.semaphore_wait(barrier, len(peers))


def reduce_scratch():
    return [
        pltpu.VMEM((ROWS, HALF), bf16),
        pltpu.VMEM((ROWS, HALF), bf16),
        pltpu.VMEM((3, 256, HALF), bf16),
        pltpu.VMEM((3, 64, HALF), bf16),
        pltpu.VMEM((3, 16, HALF), bf16),
        pltpu.VMEM((256, HALF), bf16),
        pltpu.VMEM((64, HALF), bf16),
        pltpu.SemaphoreType.DMA((len(STREAMS), 20)),
        pltpu.SemaphoreType.DMA((len(STREAMS), 20)),
    ]


def reduce_kernel(t, o, core_in, core_sum, in0, in1, in2, out0, out1, send_sem, recv_sem):
    at = place()
    greet(at)
    bufs = (core_in, core_sum, (in0, in1, in2), (out0, out1))
    streams = [Stream(k, at, t, o, bufs, send_sem, recv_sem) for k in range(len(STREAMS))]
    for s in streams:
        s.core_scatter()
    for s in streams:
        s.core_add()
        s.axis_scatter(0)
    for level in (0, 1):
        for s in streams:
            s.axis_add(level)
            s.axis_scatter(level + 1)
    for s in streams:
        s.axis_add(2)
        s.axis_gather(2)
    for level in (1, 0):
        for s in streams:
            s.gather_wait()
            s.axis_gather(level)
    for s in streams:
        s.gather_wait()
        s.core_gather()
    for s in streams:
        s.finish()


def all_reduce(t):
    return pl.pallas_call(
        reduce_kernel,
        out_shape=jax.ShapeDtypeStruct((2, ROWS, HALF), bf16),
        in_specs=[pl.BlockSpec(memory_space=pltpu.VMEM)],
        out_specs=pl.BlockSpec(memory_space=pltpu.VMEM),
        scratch_shapes=reduce_scratch(),
        compiler_params=pltpu.CompilerParams(
            collective_id=0, has_side_effects=True, vmem_limit_bytes=56 << 20
        ),
    )(t)


def pack_grads(gw_down, gw_up, gw_in_t, g_gain, g_kernel, bias):
    small = jnp.concatenate([g_gain.reshape(8, 128), g_kernel, bias], axis=0)
    small = jnp.pad(small, ((0, ROWS - small.shape[0]), (0, 0)))
    halves = [
        jnp.concatenate([gw_down[:, :512], gw_up[:, :512], gw_in_t], axis=1),
        jnp.concatenate([gw_down[:, 512:], gw_up[:, 512:], small], axis=1),
    ]
    return jnp.stack(halves).astype(bf16)


def unpack_grads(o):
    gw_down = jnp.concatenate([o[0, :, :512], o[1, :, :512]], axis=1).astype(f32)
    gw_up = jnp.concatenate([o[0, :, 512:1024], o[1, :, 512:1024]], axis=1).astype(f32)
    gw_in = o[0, :, 1024:].T.astype(f32)
    small = o[1, :33, 1024:].astype(f32)
    return gw_in, gw_up, gw_down, small[:8].reshape(1024), small[8:17], small[17:33]


DEVICES, SLOTS, CH = 128, 32, 128
SIDE = 32
OBS_HERE = 2048


def iota(shape, axis):
    return lax.broadcasted_iota(jnp.int32, shape, axis)


def nt_dot(left, right):
    return lax.dot_general(left, right, (((1,), (1,)), ((), ())), preferred_element_type=f32)


def tn_dot(left, right):
    return lax.dot_general(left, right, (((0,), (0,)), ((), ())), preferred_element_type=f32)


def exchange_kernel(
    values,
    instr,
    target,
    cell,
    bias3,
    kern,
    enc,
    enc32,
    inv,
    pad_out,
    feat,
    places,
    packed,
    tags_out,
    got,
    tags_in,
    lands,
    right,
    spots,
    pad,
    cpad,
    side_out,
    side_in,
    corner_out,
    corner_in,
    sems,
    halo_send,
    halo_recv,
):
    inst, tile = lax.axis_index("inst"), lax.axis_index("tile")
    me = inst * 8 + tile
    barrier = pltpu.get_barrier_semaphore()

    def greet_one(i, carry):
        peer = lax.rem(me + i, DEVICES)
        pl.semaphore_signal(
            barrier, inc=1, device_id=(peer // 8, lax.rem(peer, 8)), device_id_type=MESH
        )
        return carry

    lax.fori_loop(1, DEVICES, greet_one, 0)

    block = 256
    upper = (iota((block, block), 0) < iota((block, block), 1)).astype(bf16)
    ahead = jnp.zeros((DEVICES, 1), f32)
    tags = jnp.zeros((DEVICES, CH), f32)
    for b in range(OBS_HERE // block):
        cols = slice(b * block, (b + 1) * block)
        to = target[:, cols]
        hit = (to == iota((DEVICES, block), 0)).astype(f32)
        hit16 = hit.astype(bf16)
        before = jnp.dot(hit16, upper, preferred_element_type=f32) + ahead
        slot = jnp.sum(hit * before, axis=0, keepdims=True)
        ahead = ahead + jnp.sum(hit, axis=1, keepdims=True)
        slot = slot.astype(jnp.int32)
        places[:, cols] = to * SLOTS + slot
        mine = (slot == iota((SLOTS, block), 0)).astype(f32)
        where = cell[:, cols]
        kind = instr[:, cols]
        notes = jnp.concatenate(
            [
                mine * (where // SIDE + 1).astype(f32),
                mine * (where % SIDE + 1).astype(f32),
                mine * (kind + 1).astype(f32),
                jnp.zeros((SLOTS, block), f32),
            ],
            axis=0,
        ).astype(bf16)
        tags = tags + nt_dot(hit16, notes)
        pick = (kind == iota((16, block), 0)).astype(f32)
        pick3 = jnp.concatenate([pick, pick, pick], axis=0).T.astype(bf16)
        offset = jnp.dot(pick3, bias3[...], preferred_element_type=f32)
        feat[cols, :] = (values[cols, :].astype(f32) + offset).astype(bf16)
    for t in range(DEVICES):
        tags_out[t] = tags[t : t + 1, :]

    pl.semaphore_wait(barrier, DEVICES - 1)

    group = 8 * SLOTS

    def pack_and_send(i, carry):
        tb = lax.rem(inst + i, 16)
        choose = (places[...] - tb * group == iota((group, OBS_HERE), 0)).astype(f32).astype(bf16)
        rows = jnp.dot(choose, feat[...], preferred_element_type=f32).astype(bf16)
        packed[pl.ds(pl.multiple_of(tb * 8, 8), 8)] = rows.reshape(8, SLOTS, CH)

        def send_one(j, inner_carry):
            to_tile = lax.rem(tile + j, 8)
            t = tb * 8 + to_tile

            @pl.when(t != me)
            def _():
                for source, landing, k in ((packed, got, 0), (tags_out, tags_in, 1)):
                    pltpu.make_async_remote_copy(
                        src_ref=source.at[t],
                        dst_ref=landing.at[me],
                        send_sem=sems.at[k],
                        recv_sem=sems.at[2 + k],
                        device_id=(tb, to_tile),
                        device_id_type=MESH,
                    ).start()

            return inner_carry

        lax.fori_loop(0, 8, send_one, 0)
        return carry

    lax.fori_loop(0, 16, pack_and_send, 0)
    got[me] = packed[me]
    tags_in[me] = tags_out[me]
    others = pl.ds(0, DEVICES - 1)
    pltpu.make_async_copy(tags_in.at[others], tags_in.at[others], sems.at[3]).wait()
    every = tags_in[...].reshape(DEVICES, CH)
    for k in range(3):
        spots[k] = jnp.concatenate(
            [every[SIDE * m : SIDE * (m + 1), 32 * k : 32 * (k + 1)] for m in range(4)], axis=1
        )

    def place_group(g, carry):
        row = pl.ds(g, 1)
        lat, lon, kind = (spots[k, row, :] for k in range(3))
        number = iota((SIDE, CH), 0).astype(f32) + 1.0
        at_lon = (lon == number).astype(f32)
        cols = aligned(g, CH)
        for p in range(SIDE):
            lands[p * SIDE : (p + 1) * SIDE, cols] = jnp.where(
                lat == float(p + 1), at_lon, 0.0
            ).astype(bf16)
        kinds = (kind == iota((CH, CH), 0).astype(f32) + 1.0).astype(f32).T.astype(bf16)
        right[aligned(g, CH), CH:] = kinds
        return carry

    lax.fori_loop(0, SIDE, place_group, 0)
    pltpu.make_async_copy(got.at[others], got.at[others], sems.at[2]).wait()

    def collect_rows(g, carry):
        for m in range(4):
            rows = pl.ds(pl.multiple_of(g * CH + m * SLOTS, SLOTS), SLOTS)
            right[rows, :CH] = got[g + SIDE * m]
        return carry

    lax.fori_loop(0, SIDE, collect_rows, 0)

    def sum_block(i, carry):
        total = jnp.dot(lands[aligned(i, 256), :], right[...], preferred_element_type=f32)
        pad[pl.ds(1 + 8 * i, 8), 8:40, :] = total.reshape(8, SIDE, 2 * CH)
        return carry

    lax.fori_loop(0, 4, sum_block, 0)

    for p in range(SIDE):
        side_out[0, p : p + 1, :] = pad[1 + p, 8:9, :]
        side_out[1, p : p + 1, :] = pad[1 + p, 39:40, :]
    for k, (p, q) in enumerate(((1, 8), (1, 39), (32, 8), (32, 39))):
        corner_out[k] = pad[p, q : q + 1, :]
    north, south = lax.rem(tile + 7, 8), lax.rem(tile + 1, 8)
    west, east = lax.rem(inst + 15, 16), lax.rem(inst + 1, 16)
    halo = (
        (pad.at[1, 8:40], pad.at[33, 8:40], (inst, north)),
        (pad.at[32, 8:40], pad.at[0, 8:40], (inst, south)),
        (side_out.at[0], side_in.at[1], (west, tile)),
        (side_out.at[1], side_in.at[0], (east, tile)),
        (corner_out.at[0], corner_in.at[3], (west, north)),
        (corner_out.at[1], corner_in.at[2], (east, north)),
        (corner_out.at[2], corner_in.at[1], (west, south)),
        (corner_out.at[3], corner_in.at[0], (east, south)),
    )
    copies = [
        send_to(source, landing, halo_send.at[k], halo_recv.at[k], to)
        for k, (source, landing, to) in enumerate(halo)
    ]
    for copy in copies:
        copy.wait_recv()
    keep_north = (tile > 0).astype(f32)
    keep_south = (tile < 7).astype(f32)
    keep_west = (inst > 0).astype(f32)
    keep_east = (inst < 15).astype(f32)
    pad[0, 8:40, :] = pad[0, 8:40, :] * keep_north
    pad[33, 8:40, :] = pad[33, 8:40, :] * keep_south
    for p in range(SIDE):
        pad[1 + p, 7:8, :] = side_in[0, p : p + 1, :] * keep_west
        pad[1 + p, 40:41, :] = side_in[1, p : p + 1, :] * keep_east
    pad[0, 7:8, :] = corner_in[0] * (keep_north * keep_west)
    pad[0, 40:41, :] = corner_in[1] * (keep_north * keep_east)
    pad[33, 7:8, :] = corner_in[2] * (keep_south * keep_west)
    pad[33, 40:41, :] = corner_in[3] * (keep_south * keep_east)

    def count(p, carry):
        total = jnp.sum(pad[p, :, CH:], axis=-1, keepdims=True)
        cpad[p] = jnp.broadcast_to(total, (48, CH))
        pad_out[p] = pad[p]
        return carry

    lax.fori_loop(0, 34, count, 0)

    def encode(p, carry):
        spread = jnp.zeros((SIDE, CH), f32)
        density = jnp.zeros((SIDE, CH), f32)
        for j, (a, b) in enumerate(offsets):
            weight = kern[j : j + 1, :]
            spread = spread + weight * pad[p + 1 + a, 8 + b : 40 + b, :CH]
            density = density + weight * cpad[p + 1 + a, 8 + b : 40 + b, :]
        share = 1.0 / (1.0 + density)
        value = spread * share
        inv[p] = share
        enc32[p] = value
        enc[aligned(p, SIDE), :] = value.astype(bf16)
        return carry

    lax.fori_loop(0, SIDE, encode, 0)
    for copy in copies:
        copy.wait_send()
    for source, k in ((packed, 0), (tags_out, 1)):
        pltpu.make_async_copy(source.at[others], source.at[others], sems.at[k]).wait()


def exchange(values, instr, target, cell, bias, kernel):
    hi = bias.astype(bf16)
    rest = bias - hi.astype(f32)
    mid = rest.astype(bf16)
    low = (rest - mid.astype(f32)).astype(bf16)
    bias3 = jnp.concatenate([hi, mid, low], axis=0)
    cells = SIDE * SIDE
    return pl.pallas_call(
        exchange_kernel,
        out_shape=(
            jax.ShapeDtypeStruct((cells, CH), bf16),
            jax.ShapeDtypeStruct((SIDE, SIDE, CH), f32),
            jax.ShapeDtypeStruct((SIDE, SIDE, CH), f32),
            jax.ShapeDtypeStruct((34, 48, 2 * CH), f32),
        ),
        in_specs=[pl.BlockSpec(memory_space=pltpu.VMEM)] * 6,
        out_specs=[pl.BlockSpec(memory_space=pltpu.VMEM)] * 4,
        scratch_shapes=[
            pltpu.VMEM((OBS_HERE, CH), bf16),
            pltpu.VMEM((1, OBS_HERE), jnp.int32),
            pltpu.VMEM((DEVICES, SLOTS, CH), bf16),
            pltpu.VMEM((DEVICES, 1, CH), f32),
            pltpu.VMEM((DEVICES, SLOTS, CH), bf16),
            pltpu.VMEM((DEVICES, 1, CH), f32),
            pltpu.VMEM((cells, DEVICES * SLOTS), bf16),
            pltpu.VMEM((DEVICES * SLOTS, 2 * CH), bf16),
            pltpu.VMEM((3, SIDE, CH), f32),
            pltpu.VMEM((34, 48, 2 * CH), f32),
            pltpu.VMEM((34, 48, CH), f32),
            pltpu.VMEM((2, SIDE, 2 * CH), f32),
            pltpu.VMEM((2, SIDE, 2 * CH), f32),
            pltpu.VMEM((4, 1, 2 * CH), f32),
            pltpu.VMEM((4, 1, 2 * CH), f32),
            pltpu.SemaphoreType.DMA((4,)),
            pltpu.SemaphoreType.DMA((8,)),
            pltpu.SemaphoreType.DMA((8,)),
        ],
        compiler_params=pltpu.CompilerParams(
            collective_id=1, has_side_effects=True, vmem_limit_bytes=56 << 20
        ),
    )(
        values,
        instr.reshape(1, OBS_HERE),
        target.reshape(1, OBS_HERE),
        cell.reshape(1, OBS_HERE),
        bias3,
        kernel,
    )


def shards(
    obs_values,
    obs_instrument,
    obs_target,
    obs_cell,
    inst_bias,
    kernel,
    w_in,
    norm_gain,
    w_up,
    w_down,
    cotangent,
):
    n_inst = lax.axis_size("inst")
    n_tile = lax.axis_size("tile")
    channels = obs_values.shape[1]
    lat_rows, lon_cols, width = cotangent.shape
    cells = lat_rows * lon_cols
    instruments = inst_bias.shape[0]
    enc, enc32, inv, padded = exchange(
        obs_values, obs_instrument, obs_target, obs_cell, inst_bias, kernel
    )
    psums, pkinds = padded[:, 7:41, :channels], padded[:, 7:41, channels : channels + instruments]
    pcounts = jnp.sum(pkinds, axis=2, keepdims=True)

    def shifted(padded, a, b):
        return padded[1 + a : 1 + a + lat_rows, 1 + b : 1 + b + lon_cols]

    h0 = jnp.dot(enc, w_in, preferred_element_type=f32)
    rinv = lax.rsqrt(jnp.mean(h0 * h0, axis=-1, keepdims=True) + 1e-06)
    normed = (h0 * rinv * norm_gain).astype(bf16)
    act = jnp.dot(normed, w_up, preferred_element_type=f32)
    gelu_out, gelu_back = jax.vjp(jax.nn.gelu, act)
    hidden = gelu_out.astype(bf16)
    predicted_field = (
        (h0 + jnp.dot(hidden, w_down, preferred_element_type=f32))
        .astype(bf16)
        .reshape(lat_rows, lon_cols, width)
    )
    scale = 1.0 / (lat_rows * n_tile * lon_cols * n_inst) ** 0.5
    dyb = (cotangent.astype(f32) * scale).astype(bf16).reshape(cells, width)
    gw_down = inner(hidden, dyb)
    dact = gelu_back(along(dyb, w_down))[0].astype(bf16)
    gw_up = inner(normed, dact)
    dnormed = along(dact, w_up)
    g_gain = jnp.sum(dnormed * h0 * rinv, axis=0)
    scaled = dnormed * norm_gain
    dh = (
        rinv * scaled
        - h0 * rinv**3 * jnp.mean(scaled * h0, axis=-1, keepdims=True)
        + dyb.astype(f32)
    ).astype(bf16)
    gw_in_t = inner(dh, enc)
    denc = along(dh, w_in).reshape(lat_rows, lon_cols, channels)
    dspread = denc * inv
    ddensity = -dspread * enc32
    kernel_rows = []
    bias = jnp.zeros((instruments, channels), f32)
    flat = dspread.reshape(cells, channels)
    for j, (a, b) in enumerate(offsets):
        near = shifted(pkinds, a, b)
        kernel_rows.append(
            jnp.sum(dspread * shifted(psums, a, b) + ddensity * shifted(pcounts, a, b), axis=(0, 1))
        )
        bias = bias + kernel[j] * inner(
            near.reshape(cells, instruments), flat, lax.Precision.HIGHEST
        )
    g_kernel = jnp.stack(kernel_rows)
    totals = unpack_grads(
        all_reduce(pack_grads(gw_down, gw_up, gw_in_t, g_gain, g_kernel, bias))
    )
    return (predicted_field, *totals)


def solution(mesh):
    return jax.shard_map(
        shards,
        mesh=mesh,
        in_specs=(
            P(("inst", "tile"), None),
            P(("inst", "tile")),
            P(("inst", "tile"), None),
            P(("inst", "tile")),
            P(),
            P(),
            P(),
            P(),
            P(),
            P(),
            P("tile", "inst", None),
        ),
        out_specs=(P("tile", "inst", None), P(), P(), P(), P(), P(), P()),
        check_vma=False,
    )
```

```python
import functools

import jax
import jax.numpy as jnp
from jax import lax
from jax.experimental import pallas as pl
from jax.experimental.pallas import tpu as pltpu
from jax.sharding import PartitionSpec as P

offsets = [(a, b) for a in (-1, 0, 1) for b in (-1, 0, 1)]
f32, bf16 = jnp.float32, jnp.bfloat16


MESH = pl.DeviceIdType.MESH
HALF = 1152
ROWS = 1024
STREAMS = (
    (0, 256, ("x", "y", "z"), 0, 0),
    (256, 128, ("y", "z", "x"), 0, 256),
    (384, 128, ("z", "x", "y"), 0, 384),
    (512, 128, ("x", "y", "z"), 1, 0),
    (640, 256, ("y", "z", "x"), 1, 128),
    (896, 128, ("z", "x", "y"), 1, 384),
    (1024, 128, ("z", "x", "y"), 2, 0),
)


def place():
    inst, tile = lax.axis_index("inst"), lax.axis_index("tile")
    return {"z": inst // 4, "x": inst % 4, "y": tile // 2, "core": tile % 2}


def device_at(at):
    return (at["z"] * 4 + at["x"], at["y"] * 2 + at["core"])


def moved(at, axis, step):
    size = 2 if axis == "core" else 4
    return {**at, axis: lax.rem(at[axis] + step, size)}


def send_to(source, landing, send_sem, recv_sem, to):
    copy = pltpu.make_async_remote_copy(
        src_ref=source,
        dst_ref=landing,
        send_sem=send_sem,
        recv_sem=recv_sem,
        device_id=to,
        device_id_type=MESH,
    )
    copy.start()
    return copy


def aligned(index, size):
    return pl.ds(pl.multiple_of(index * size, size), size)


class Stream:
    def __init__(self, number, at, t, outs, bufs, send_sem, recv_sem):
        first, wide, self.order, output, first_out = STREAMS[number]
        self.cols = pl.ds(first, wide)
        self.at, self.t, self.o = at, t, outs[output]
        half = self.o.shape[1] // 2
        self.out_cols = pl.ds(pl.multiple_of(at["core"] * half + first_out, 128), wide)
        self.core_in, self.core_sum, self.ins, self.outs = bufs
        self.sends, self.recvs = send_sem.at[number], recv_sem.at[number]
        self.started = []
        self.core = at["core"]

    def go(self, source, target, slot, at):
        copy = send_to(
            source, target, self.sends.at[slot], self.recvs.at[slot], device_at(at)
        )
        self.started.append(copy)
        return copy

    def core_scatter(self):
        other = moved(self.at, "core", 1)
        self.pending = [
            self.go(
                self.t.at[1 - self.core, :, self.cols], self.core_in.at[:, self.cols], 0, other
            )
        ]

    def core_add(self):
        for copy in self.pending:
            copy.wait_recv()
        step = 128

        def body(i, carry):
            rows = aligned(i, step)
            total = self.t[self.core, rows, self.cols].astype(f32) + self.core_in[
                rows, self.cols
            ].astype(f32)
            self.core_sum[rows, self.cols] = total.astype(bf16)
            return carry

        lax.fori_loop(0, ROWS // step, body, 0)

    def axis_scatter(self, level):
        axis, size = self.order[level], (256, 64, 16)[level]
        source = self.core_sum if level == 0 else self.outs[level - 1]
        self.pending = []
        for step in (1, 2, 3):
            peer = moved(self.at, axis, step)
            self.pending.append(
                self.go(
                    source.at[aligned(peer[axis], size), self.cols],
                    self.ins[level].at[step - 1, :, self.cols],
                    1 + 3 * level + step - 1,
                    peer,
                )
            )

    def axis_add(self, level):
        axis, size = self.order[level], (256, 64, 16)[level]
        source = self.core_sum if level == 0 else self.outs[level - 1]
        for copy in self.pending:
            copy.wait_recv()
        step = min(size, 64)

        def body(i, carry):
            rows = aligned(i, step)
            mine = pl.ds(pl.multiple_of(self.at[axis] * size + i * step, step), step)
            total = source[mine, self.cols].astype(f32)
            for j in range(3):
                total = total + self.ins[level][j, rows, self.cols].astype(f32)
            if level < 2:
                self.outs[level][rows, self.cols] = total.astype(bf16)
            else:
                self.o[self.owned(2), self.out_cols] = total.astype(bf16)
            return carry

        lax.fori_loop(0, size // step, body, 0)

    def owned(self, level):
        start = 0
        for axis, size in list(zip(self.order, (256, 64, 16)))[: level + 1]:
            start = start + self.at[axis] * size
        size = (256, 64, 16)[level]
        return pl.ds(pl.multiple_of(start, size), size)

    def axis_gather(self, level):
        axis = self.order[level]
        rows = self.owned(level)
        self.pending = []
        for step in (1, 2, 3):
            peer = moved(self.at, axis, step)
            part = self.o.at[rows, self.out_cols]
            self.pending.append(self.go(part, part, 10 + 3 * (2 - level) + step - 1, peer))

    def gather_wait(self):
        for copy in self.pending:
            copy.wait_recv()

    def core_gather(self):
        part = self.o.at[:, self.out_cols]
        self.pending = [self.go(part, part, 19, moved(self.at, "core", 1))]

    def finish(self):
        self.gather_wait()
        for copy in self.started:
            copy.wait_send()


def greet(at):
    barrier = pltpu.get_barrier_semaphore()
    peers = [moved(at, axis, step) for axis in ("x", "y", "z") for step in (1, 2, 3)]
    peers.append(moved(at, "core", 1))
    for peer in peers:
        pl.semaphore_signal(barrier, inc=1, device_id=device_at(peer), device_id_type=MESH)
    pl.semaphore_wait(barrier, len(peers))


def reduce_scratch():
    return [
        pltpu.VMEM((ROWS, HALF), bf16),
        pltpu.VMEM((ROWS, HALF), bf16),
        pltpu.VMEM((3, 256, HALF), bf16),
        pltpu.VMEM((3, 64, HALF), bf16),
        pltpu.VMEM((3, 16, HALF), bf16),
        pltpu.VMEM((256, HALF), bf16),
        pltpu.VMEM((64, HALF), bf16),
        pltpu.SemaphoreType.DMA((len(STREAMS), 20)),
        pltpu.SemaphoreType.DMA((len(STREAMS), 20)),
    ]


DEVICES, SLOTS, CH = 128, 32, 128
SIDE = 32
OBS_HERE = 2048


def iota(shape, axis):
    return lax.broadcasted_iota(jnp.int32, shape, axis)


def nt_dot(left, right):
    return lax.dot_general(left, right, (((1,), (1,)), ((), ())), preferred_element_type=f32)


def tn_dot(left, right):
    return lax.dot_general(left, right, (((0,), (0,)), ((), ())), preferred_element_type=f32)


def exchange_kernel(
    values,
    instr,
    target,
    cell,
    bias3,
    kern,
    enc,
    enc32,
    inv,
    pad_out,
    feat,
    places,
    packed,
    tags_out,
    got,
    tags_in,
    lands,
    right,
    spots,
    pad,
    side_out,
    side_in,
    corner_out,
    corner_in,
    sems,
    halo_send,
    halo_recv,
):
    inst, tile = lax.axis_index("inst"), lax.axis_index("tile")
    me = inst * 8 + tile
    barrier = pltpu.get_barrier_semaphore()

    def greet_one(i, carry):
        peer = lax.rem(me + i, DEVICES)
        pl.semaphore_signal(
            barrier, inc=1, device_id=(peer // 8, lax.rem(peer, 8)), device_id_type=MESH
        )
        return carry

    def clear(p, carry):
        pad[p] = jnp.zeros((48, 2 * CH), f32)
        return carry

    lax.fori_loop(0, 34, clear, 0)
    lax.fori_loop(1, DEVICES, greet_one, 0)

    block = 256
    upper = (iota((block, block), 0) < iota((block, block), 1)).astype(bf16)
    ahead = jnp.zeros((DEVICES, 1), f32)
    tags = jnp.zeros((DEVICES, CH), f32)
    for b in range(OBS_HERE // block):
        cols = slice(b * block, (b + 1) * block)
        to = target[:, cols]
        hit = (to == iota((DEVICES, block), 0)).astype(f32)
        hit16 = hit.astype(bf16)
        before = jnp.dot(hit16, upper, preferred_element_type=f32) + ahead
        slot = jnp.sum(hit * before, axis=0, keepdims=True)
        ahead = ahead + jnp.sum(hit, axis=1, keepdims=True)
        slot = slot.astype(jnp.int32)
        places[:, cols] = to * SLOTS + slot
        mine = (slot == iota((SLOTS, block), 0)).astype(f32)
        where = cell[:, cols]
        kind = instr[:, cols]
        notes = jnp.concatenate(
            [
                mine * (where // SIDE + 1).astype(f32),
                mine * (where % SIDE + 1).astype(f32),
                mine * (kind + 1).astype(f32),
                jnp.zeros((SLOTS, block), f32),
            ],
            axis=0,
        ).astype(bf16)
        tags = tags + nt_dot(hit16, notes)
        pick = (kind == iota((16, block), 0)).astype(f32)
        pick3 = jnp.concatenate([pick, pick, pick], axis=0).T.astype(bf16)
        offset = jnp.dot(pick3, bias3[...], preferred_element_type=f32)
        feat[cols, :] = (values[cols, :].astype(f32) + offset).astype(bf16)
    for t in range(DEVICES):
        tags_out[t] = tags[t : t + 1, :]

    pl.semaphore_wait(barrier, DEVICES - 1)

    group = 8 * SLOTS

    def pack_and_send(i, carry):
        tb = lax.rem(inst + i, 16)
        choose = (places[...] - tb * group == iota((group, OBS_HERE), 0)).astype(f32).astype(bf16)
        rows = jnp.dot(choose, feat[...], preferred_element_type=f32).astype(bf16)
        packed[pl.ds(pl.multiple_of(tb * 8, 8), 8)] = rows.reshape(8, SLOTS, CH)

        def send_one(j, inner_carry):
            to_tile = lax.rem(tile + j, 8)
            t = tb * 8 + to_tile

            @pl.when(t != me)
            def _():
                for source, landing, k in ((packed, got, 0), (tags_out, tags_in, 1)):
                    pltpu.make_async_remote_copy(
                        src_ref=source.at[t],
                        dst_ref=landing.at[me],
                        send_sem=sems.at[k],
                        recv_sem=sems.at[2 + k],
                        device_id=(tb, to_tile),
                        device_id_type=MESH,
                    ).start()

            return inner_carry

        lax.fori_loop(0, 8, send_one, 0)
        return carry

    lax.fori_loop(0, 16, pack_and_send, 0)
    got[me] = packed[me]
    tags_in[me] = tags_out[me]
    others = pl.ds(0, DEVICES - 1)
    pltpu.make_async_copy(tags_in.at[others], tags_in.at[others], sems.at[3]).wait()
    every = tags_in[...].reshape(DEVICES, CH)
    for k in range(3):
        spots[k] = jnp.concatenate(
            [every[SIDE * m : SIDE * (m + 1), 32 * k : 32 * (k + 1)] for m in range(4)], axis=1
        )

    def place_group(g, carry):
        row = pl.ds(g, 1)
        lat, lon, kind = (spots[k, row, :] for k in range(3))
        number = iota((SIDE, CH), 0).astype(f32) + 1.0
        at_lon = (lon == number).astype(f32)
        cols = aligned(g, CH)
        for p in range(SIDE):
            lands[p * SIDE : (p + 1) * SIDE, cols] = jnp.where(
                lat == float(p + 1), at_lon, 0.0
            ).astype(bf16)
        kinds = (kind == iota((CH, CH), 0).astype(f32) + 1.0).astype(f32).T.astype(bf16)
        right[aligned(g, CH), CH:] = kinds
        return carry

    lax.fori_loop(0, SIDE, place_group, 0)
    pltpu.make_async_copy(got.at[others], got.at[others], sems.at[2]).wait()

    def collect_rows(g, carry):
        for m in range(4):
            rows = pl.ds(pl.multiple_of(g * CH + m * SLOTS, SLOTS), SLOTS)
            right[rows, :CH] = got[g + SIDE * m]
        return carry

    lax.fori_loop(0, SIDE, collect_rows, 0)

    def sum_block(i, carry):
        total = jnp.dot(lands[aligned(i, 256), :], right[...], preferred_element_type=f32)
        pad[pl.ds(1 + 8 * i, 8), 8:40, :] = total.reshape(8, SIDE, 2 * CH)
        return carry

    lax.fori_loop(0, 4, sum_block, 0)

    for p in range(SIDE):
        side_out[0, p : p + 1, :] = pad[1 + p, 8:9, :]
        side_out[1, p : p + 1, :] = pad[1 + p, 39:40, :]
    for k, (p, q) in enumerate(((1, 8), (1, 39), (32, 8), (32, 39))):
        corner_out[k] = pad[p, q : q + 1, :]
    north, south = lax.rem(tile + 7, 8), lax.rem(tile + 1, 8)
    west, east = lax.rem(inst + 15, 16), lax.rem(inst + 1, 16)
    halo = (
        (pad.at[1, 8:40], pad.at[33, 8:40], (inst, north)),
        (pad.at[32, 8:40], pad.at[0, 8:40], (inst, south)),
        (side_out.at[0], side_in.at[1], (west, tile)),
        (side_out.at[1], side_in.at[0], (east, tile)),
        (corner_out.at[0], corner_in.at[3], (west, north)),
        (corner_out.at[1], corner_in.at[2], (east, north)),
        (corner_out.at[2], corner_in.at[1], (west, south)),
        (corner_out.at[3], corner_in.at[0], (east, south)),
    )
    copies = [
        send_to(source, landing, halo_send.at[k], halo_recv.at[k], to)
        for k, (source, landing, to) in enumerate(halo)
    ]
    for copy in copies:
        copy.wait_recv()
    keep_north = (tile > 0).astype(f32)
    keep_south = (tile < 7).astype(f32)
    keep_west = (inst > 0).astype(f32)
    keep_east = (inst < 15).astype(f32)
    pad[0, 8:40, :] = pad[0, 8:40, :] * keep_north
    pad[33, 8:40, :] = pad[33, 8:40, :] * keep_south
    for p in range(SIDE):
        pad[1 + p, 7:8, :] = side_in[0, p : p + 1, :] * keep_west
        pad[1 + p, 40:41, :] = side_in[1, p : p + 1, :] * keep_east
    pad[0, 7:8, :] = corner_in[0] * (keep_north * keep_west)
    pad[0, 40:41, :] = corner_in[1] * (keep_north * keep_east)
    pad[33, 7:8, :] = corner_in[2] * (keep_south * keep_west)
    pad[33, 40:41, :] = corner_in[3] * (keep_south * keep_east)

    def count(p, carry):
        total = jnp.sum(pad[p, :, CH:], axis=-1, keepdims=True)
        pad_out[p, :, : 2 * CH] = pad[p]
        pad_out[p, :, 2 * CH :] = jnp.broadcast_to(total, (48, CH))
        return carry

    lax.fori_loop(0, 34, count, 0)

    def encode(p, carry):
        spread = jnp.zeros((SIDE, CH), f32)
        density = jnp.zeros((SIDE, CH), f32)
        for j, (a, b) in enumerate(offsets):
            weight = kern[j : j + 1, :]
            spread = spread + weight * pad[p + 1 + a, 8 + b : 40 + b, :CH]
            density = density + weight * pad_out[p + 1 + a, 8 + b : 40 + b, 2 * CH :]
        share = 1.0 / (1.0 + density)
        value = spread * share
        inv[p] = share
        enc32[p] = value
        enc[aligned(p, SIDE), :] = value.astype(bf16)
        return carry

    lax.fori_loop(0, SIDE, encode, 0)
    for copy in copies:
        copy.wait_send()
    for source, k in ((packed, 0), (tags_out, 1)):
        pltpu.make_async_copy(source.at[others], source.at[others], sems.at[k]).wait()


def exchange(values, instr, target, cell, bias, kernel):
    hi = bias.astype(bf16)
    rest = bias - hi.astype(f32)
    mid = rest.astype(bf16)
    low = (rest - mid.astype(f32)).astype(bf16)
    bias3 = jnp.concatenate([hi, mid, low], axis=0)
    cells = SIDE * SIDE
    return pl.pallas_call(
        exchange_kernel,
        out_shape=(
            jax.ShapeDtypeStruct((cells, CH), bf16),
            jax.ShapeDtypeStruct((SIDE, SIDE, CH), f32),
            jax.ShapeDtypeStruct((SIDE, SIDE, CH), f32),
            jax.ShapeDtypeStruct((34, 48, 3 * CH), f32),
        ),
        in_specs=[pl.BlockSpec(memory_space=pltpu.VMEM)] * 6,
        out_specs=[pl.BlockSpec(memory_space=pltpu.VMEM)] * 4,
        scratch_shapes=[
            pltpu.VMEM((OBS_HERE, CH), bf16),
            pltpu.VMEM((1, OBS_HERE), jnp.int32),
            pltpu.VMEM((DEVICES, SLOTS, CH), bf16),
            pltpu.VMEM((DEVICES, 1, CH), f32),
            pltpu.VMEM((DEVICES, SLOTS, CH), bf16),
            pltpu.VMEM((DEVICES, 1, CH), f32),
            pltpu.VMEM((cells, DEVICES * SLOTS), bf16),
            pltpu.VMEM((DEVICES * SLOTS, 2 * CH), bf16),
            pltpu.VMEM((3, SIDE, CH), f32),
            pltpu.VMEM((34, 48, 2 * CH), f32),
            pltpu.VMEM((2, SIDE, 2 * CH), f32),
            pltpu.VMEM((2, SIDE, 2 * CH), f32),
            pltpu.VMEM((4, 1, 2 * CH), f32),
            pltpu.VMEM((4, 1, 2 * CH), f32),
            pltpu.SemaphoreType.DMA((4,)),
            pltpu.SemaphoreType.DMA((8,)),
            pltpu.SemaphoreType.DMA((8,)),
        ],
        compiler_params=pltpu.CompilerParams(
            collective_id=1, has_side_effects=True, vmem_limit_bytes=56 << 20
        ),
    )(
        values,
        instr.reshape(1, OBS_HERE),
        target.reshape(1, OBS_HERE),
        cell.reshape(1, OBS_HERE),
        bias3,
        kernel,
    )


WIDTH = 1024
CELLS = SIDE * SIDE
TANH_SCALE = 0.7978845608028654
CUBIC = 0.044715


def small_reduce(at, axis, level, mine, boxes, send_sem, recv_sem):
    size = 2 if axis == "core" else 4
    boxes[level, at[axis]] = mine
    copies = []
    for step in range(1, size):
        box = boxes.at[level, at[axis]]
        k = 3 * level + step - 1
        copies.append(
            send_to(box, box, send_sem.at[k], recv_sem.at[k], device_at(moved(at, axis, step)))
        )
    return copies


def small_total(axis, level, boxes, copies):
    for copy in copies:
        copy.wait_recv()
    total = boxes[level, 0]
    for k in range(1, 2 if axis == "core" else 4):
        total = total + boxes[level, k]
    return total


def train_kernel(
    scale,
    enc,
    enc32,
    inv,
    pad,
    kern,
    gain,
    w_in_hbm,
    w_up_hbm,
    w_down_hbm,
    cot_hbm,
    y_hbm,
    o_down,
    o_up,
    o_in,
    o_small,
    w_in,
    w_up,
    w_down,
    dyb,
    h0,
    rinv,
    u,
    g,
    dact,
    ds,
    dz,
    gain_sum,
    boxes,
    t,
    load_sem,
    small_send,
    small_recv,
    core_in,
    core_sum,
    in0,
    in1,
    in2,
    out0,
    out1,
    send_sem,
    recv_sem,
):
    at = place()
    loads = [
        pltpu.make_async_copy(source, target, load_sem.at[k])
        for k, (source, target) in enumerate(
            ((w_in_hbm, w_in), (w_up_hbm, w_up), (cot_hbm, dyb), (w_down_hbm, w_down))
        )
    ]
    for load in loads:
        load.start()
    greet(at)
    bufs = (core_in, core_sum, (in0, in1, in2), (out0, out1))
    outs = (o_down, o_up, o_in)
    streams = [Stream(k, at, t, outs, bufs, send_sem, recv_sem) for k in range(len(STREAMS))]
    down, up, rest = streams[:3], streams[3:6], streams[6:]
    block = 256
    for load in loads:
        load.wait()

    def forward(i, carry):
        rows = aligned(i, block)
        h = jnp.dot(enc[rows, :], w_in[...], preferred_element_type=f32)
        h0[rows, :] = h
        r = lax.rsqrt(jnp.mean(h * h, axis=-1, keepdims=True) + 1e-06)
        rinv[rows, :] = jnp.broadcast_to(r, (block, CH))
        u_here = (h * r * gain[...]).astype(bf16)
        u[rows, :] = u_here
        dy_here = (dyb[rows, :].astype(f32) * scale).astype(bf16)
        dyb[rows, :] = dy_here
        for n in range(WIDTH // block):
            cols = slice(n * block, (n + 1) * block)
            act = jnp.dot(u_here, w_up[:, cols], preferred_element_type=f32)
            back = nt_dot(dy_here, w_down[cols, :])
            square = act * act
            tanh = jnp.tanh(TANH_SCALE * act * (1.0 + CUBIC * square))
            cdf = 0.5 + 0.5 * tanh
            slope = cdf + act * (0.5 - 0.5 * tanh * tanh) * (
                TANH_SCALE + (3.0 * CUBIC * TANH_SCALE) * square
            )
            g[rows, cols] = (act * cdf).astype(bf16)
            dact[rows, cols] = (slope * back).astype(bf16)
        return carry

    lax.fori_loop(0, CELLS // block, forward, 0)

    def weight_grad(left, right, first):
        def body(i, carry):
            cols = aligned(i, block)
            part = tn_dot(left[:, cols], right[...]).astype(bf16)
            t[0, cols, first : first + 512] = part[:, :512]
            t[1, cols, first : first + 512] = part[:, 512:]
            return carry

        lax.fori_loop(0, WIDTH // block, body, 0)

    weight_grad(g, dyb, 0)
    for s in down:
        s.core_scatter()
    weight_grad(u, dact, 512)
    for s in up:
        s.core_scatter()
    for s in down:
        s.core_add()
        s.axis_scatter(0)

    gain_sum[...] = jnp.zeros_like(gain_sum)

    def backward(i, carry):
        rows = aligned(i, block)
        du = nt_dot(dact[rows, :], w_up[...])
        h = h0[rows, :]
        r = rinv[rows, :1]
        gain_sum[...] += jnp.sum(du * h * r, axis=0, keepdims=True)
        scaled = du * gain[...]
        mean = jnp.mean(scaled * h, axis=-1, keepdims=True)
        dh = (r * scaled - h * (r * r * r * mean) + dyb[rows, :].astype(f32)).astype(bf16)
        u[rows, :] = dh
        denc = nt_dot(dh, w_in[...])
        eight = pl.ds(pl.multiple_of(i * 8, 8), 8)
        ds[eight] = denc.reshape(8, SIDE, CH) * inv[eight]
        return carry

    lax.fori_loop(0, CELLS // block, backward, 0)
    for s in up:
        s.core_add()
        s.axis_scatter(0)

    def in_grad(i, carry):
        cols = aligned(i, block)
        t[0, cols, 1024:] = tn_dot(u[:, cols], enc[...]).astype(bf16)
        t[1, cols, 1024:] = jnp.zeros((block, CH), bf16)
        return carry

    lax.fori_loop(0, WIDTH // block, in_grad, 0)
    for s in rest:
        s.core_scatter()
    for s in down:
        s.axis_add(0)
        s.axis_scatter(1)

    for k in (0, 1, 34, 35):
        dz[k] = jnp.zeros((64, CH), f32)

    def filter_grad(p, sums):
        here = ds[p]
        dz[p + 2, :16] = jnp.zeros((16, CH), f32)
        dz[p + 2, 16:48] = here
        dz[p + 2, 48:] = jnp.zeros((16, CH), f32)
        value = enc32[p]
        new = []
        for j, (a, b) in enumerate(offsets):
            near = pad[p + 1 + a, 8 + b : 40 + b, :CH]
            near_count = pad[p + 1 + a, 8 + b : 40 + b, 2 * CH :]
            part = here * (near - value * near_count)
            new.append(sums[j] + jnp.sum(part.reshape(4, 8, CH), axis=0))
        return tuple(new)

    zeros = jnp.zeros((8, CH), f32)
    filter_sums = lax.fori_loop(0, SIDE, filter_grad, (zeros,) * 9)

    def bias_grad(p, total):
        spread = jnp.zeros((48, CH), f32)
        for j, (a, b) in enumerate(offsets):
            spread = spread + kern[j : j + 1, :] * dz[p + 1 - a, 8 - b : 56 - b, :]
        return total + lax.dot_general(
            pad[p, :, CH : 2 * CH],
            spread,
            (((0,), (0,)), ((), ())),
            precision=lax.Precision.HIGHEST,
            preferred_element_type=f32,
        )

    bias_sum = lax.fori_loop(0, 34, bias_grad, jnp.zeros((CH, CH), f32))
    small = jnp.concatenate(
        [gain_sum[:, k * CH : (k + 1) * CH] for k in range(8)]
        + [jnp.sum(part, axis=0, keepdims=True) for part in filter_sums]
        + [jnp.zeros((7, CH), f32), bias_sum[:16]],
        axis=0,
    )
    small_copies = small_reduce(at, "x", 0, small, boxes, small_send, small_recv)
    all_small = list(small_copies)
    for s in rest:
        s.core_add()
        s.axis_scatter(0)
    for s in up:
        s.axis_add(0)
        s.axis_scatter(1)
    for s in down:
        s.axis_add(1)
        s.axis_scatter(2)

    def forecast(i, carry):
        rows = aligned(i, block)
        y = h0[rows, :] + jnp.dot(g[rows, :], w_down[...], preferred_element_type=f32)
        dact[rows, :] = y.astype(bf16)
        return carry

    lax.fori_loop(0, CELLS // block, forecast, 0)
    store = pltpu.make_async_copy(dact, y_hbm, load_sem.at[4])
    store.start()
    for s in down:
        s.axis_add(2)
        s.axis_gather(2)
    for s in rest:
        s.axis_add(0)
        s.axis_scatter(1)
    for s in up:
        s.axis_add(1)
        s.axis_scatter(2)
    small = small_total("x", 0, boxes, small_copies)
    small_copies = small_reduce(at, "y", 1, small, boxes, small_send, small_recv)
    all_small += small_copies
    for s in down:
        s.gather_wait()
        s.axis_gather(1)
    for s in rest:
        s.axis_add(1)
        s.axis_scatter(2)
    for s in up:
        s.axis_add(2)
        s.axis_gather(2)
    small = small_total("y", 1, boxes, small_copies)
    small_copies = small_reduce(at, "z", 2, small, boxes, small_send, small_recv)
    all_small += small_copies
    for s in down:
        s.gather_wait()
        s.axis_gather(0)
    for s in rest:
        s.axis_add(2)
        s.axis_gather(2)
    for s in up:
        s.gather_wait()
        s.axis_gather(1)
    small = small_total("z", 2, boxes, small_copies)
    small_copies = small_reduce(at, "core", 3, small, boxes, small_send, small_recv)
    all_small += small_copies
    for s in rest:
        s.gather_wait()
        s.axis_gather(1)
    for s in up:
        s.gather_wait()
        s.axis_gather(0)
    for s in down:
        s.gather_wait()
        s.core_gather()
    for s in rest:
        s.gather_wait()
        s.axis_gather(0)
    o_small[...] = small_total("core", 3, boxes, small_copies)
    for s in up + rest:
        s.gather_wait()
        s.core_gather()
    for s in streams:
        s.finish()
    for copy in all_small:
        copy.wait_send()
    store.wait()


def train(scale, enc, enc32, inv, pad, kern, gain, w_in, w_up, w_down, cot):
    vmem, hbm = pl.BlockSpec(memory_space=pltpu.VMEM), pl.BlockSpec(memory_space=pl.ANY)
    return pl.pallas_call(
        functools.partial(train_kernel, scale),
        out_shape=(
            jax.ShapeDtypeStruct((CELLS, WIDTH), bf16),
            jax.ShapeDtypeStruct((WIDTH, WIDTH), bf16),
            jax.ShapeDtypeStruct((WIDTH, WIDTH), bf16),
            jax.ShapeDtypeStruct((WIDTH, 2 * CH), bf16),
            jax.ShapeDtypeStruct((40, CH), f32),
        ),
        in_specs=[vmem] * 6 + [hbm] * 4,
        out_specs=[hbm] + [vmem] * 4,
        scratch_shapes=[
            pltpu.VMEM((CH, WIDTH), bf16),
            pltpu.VMEM((WIDTH, WIDTH), bf16),
            pltpu.VMEM((WIDTH, WIDTH), bf16),
            pltpu.VMEM((CELLS, WIDTH), bf16),
            pltpu.VMEM((CELLS, WIDTH), f32),
            pltpu.VMEM((CELLS, CH), f32),
            pltpu.VMEM((CELLS, WIDTH), bf16),
            pltpu.VMEM((CELLS, WIDTH), bf16),
            pltpu.VMEM((CELLS, WIDTH), bf16),
            pltpu.VMEM((SIDE, SIDE, CH), f32),
            pltpu.VMEM((36, 64, CH), f32),
            pltpu.VMEM((1, WIDTH), f32),
            pltpu.VMEM((4, 4, 40, CH), f32),
            pltpu.VMEM((2, ROWS, HALF), bf16),
            pltpu.SemaphoreType.DMA((5,)),
            pltpu.SemaphoreType.DMA((12,)),
            pltpu.SemaphoreType.DMA((12,)),
        ]
        + reduce_scratch(),
        compiler_params=pltpu.CompilerParams(
            collective_id=0, has_side_effects=True, vmem_limit_bytes=60 << 20
        ),
    )(enc, enc32, inv, pad, kern, gain, w_in, w_up, w_down, cot)


def widen_kernel(y, down, up, into, y_out, down_out, up_out, in_out):
    y_out[...] = y[...]
    down_out[...] = down[...].astype(f32)
    up_out[...] = up[...].astype(f32)
    in_out[...] = into[:, :CH].astype(f32).T


def widen(y, down, up, into):
    block = 128
    wide = pl.BlockSpec((block, WIDTH), lambda i: (i, 0))
    return pl.pallas_call(
        widen_kernel,
        grid=(WIDTH // block,),
        out_shape=(
            jax.ShapeDtypeStruct((CELLS, WIDTH), bf16),
            jax.ShapeDtypeStruct((WIDTH, WIDTH), f32),
            jax.ShapeDtypeStruct((WIDTH, WIDTH), f32),
            jax.ShapeDtypeStruct((CH, WIDTH), f32),
        ),
        in_specs=[wide, wide, wide, pl.BlockSpec((block, 2 * CH), lambda i: (i, 0))],
        out_specs=[wide, wide, wide, pl.BlockSpec((CH, block), lambda i: (0, i))],
        compiler_params=pltpu.CompilerParams(vmem_limit_bytes=32 << 20),
    )(y, down, up, into)


def shards(
    obs_values,
    obs_instrument,
    obs_target,
    obs_cell,
    inst_bias,
    kernel,
    w_in,
    norm_gain,
    w_up,
    w_down,
    cotangent,
):
    enc, enc32, inv, pad = exchange(
        obs_values, obs_instrument, obs_target, obs_cell, inst_bias, kernel
    )
    scale = 1.0 / (CELLS * DEVICES) ** 0.5
    y, down, up, into, small = train(
        scale,
        enc,
        enc32,
        inv,
        pad,
        kernel,
        norm_gain.reshape(1, WIDTH),
        w_in,
        w_up,
        w_down,
        cotangent.reshape(CELLS, WIDTH),
    )
    y, down, up, into = widen(y, down, up, into)
    return (
        y.reshape(cotangent.shape),
        into,
        up,
        down,
        small[:8].reshape(WIDTH),
        small[8:17],
        small[24:40],
    )


def solution(mesh):
    return jax.shard_map(
        shards,
        mesh=mesh,
        in_specs=(
            P(("inst", "tile"), None),
            P(("inst", "tile")),
            P(("inst", "tile"), None),
            P(("inst", "tile")),
            P(),
            P(),
            P(),
            P(),
            P(),
            P(),
            P("tile", "inst", None),
        ),
        out_specs=(P("tile", "inst", None), P(), P(), P(), P(), P(), P()),
        check_vma=False,
    )
```

```python
import functools

import jax
import jax.numpy as jnp
from jax import lax
from jax.experimental import pallas as pl
from jax.experimental.pallas import tpu as pltpu
from jax.sharding import PartitionSpec as P

offsets = [(a, b) for a in (-1, 0, 1) for b in (-1, 0, 1)]
f32, bf16 = jnp.float32, jnp.bfloat16


MESH = pl.DeviceIdType.MESH
HALF = 1152
ROWS = 1024
STREAMS = (
    (0, 256, ("x", "y", "z"), 0, 0),
    (256, 128, ("y", "z", "x"), 0, 256),
    (384, 128, ("z", "x", "y"), 0, 384),
    (512, 128, ("x", "y", "z"), 1, 0),
    (640, 256, ("y", "z", "x"), 1, 128),
    (896, 128, ("z", "x", "y"), 1, 384),
    (1024, 128, ("z", "x", "y"), 2, 0),
)


def place():
    inst, tile = lax.axis_index("inst"), lax.axis_index("tile")
    return {"z": inst // 4, "x": inst % 4, "y": tile // 2, "core": tile % 2}


def device_at(at):
    return (at["z"] * 4 + at["x"], at["y"] * 2 + at["core"])


def moved(at, axis, step):
    size = 2 if axis == "core" else 4
    return {**at, axis: lax.rem(at[axis] + step, size)}


def send_to(source, landing, send_sem, recv_sem, to):
    copy = pltpu.make_async_remote_copy(
        src_ref=source,
        dst_ref=landing,
        send_sem=send_sem,
        recv_sem=recv_sem,
        device_id=to,
        device_id_type=MESH,
    )
    copy.start()
    return copy


def aligned(index, size):
    return pl.ds(pl.multiple_of(index * size, size), size)


class Stream:
    def __init__(self, number, at, give, keep, outs, bufs, send_sem, recv_sem):
        first, wide, self.order, output, first_out = STREAMS[number]
        self.cols = pl.ds(first, wide)
        self.at, self.give, self.keep, self.o = at, give, keep, outs[output]
        half = self.o.shape[1] // 2
        self.out_cols = pl.ds(pl.multiple_of(at["core"] * half + first_out, 128), wide)
        self.core_in, self.core_sum, self.ins, self.outs = bufs
        self.sends, self.recvs = send_sem.at[number], recv_sem.at[number]
        self.started = []

    def go(self, source, target, slot, at):
        copy = send_to(
            source, target, self.sends.at[slot], self.recvs.at[slot], device_at(at)
        )
        self.started.append(copy)
        return copy

    def core_scatter(self):
        other = moved(self.at, "core", 1)
        self.pending = [
            self.go(self.give.at[:, self.cols], self.core_in.at[:, self.cols], 0, other)
        ]

    def core_add(self):
        for copy in self.pending:
            copy.wait_recv()
        step = 128

        def body(i, carry):
            rows = aligned(i, step)
            total = self.keep[rows, self.cols].astype(f32) + self.core_in[rows, self.cols].astype(f32)
            self.core_sum[rows, self.cols] = total.astype(bf16)
            return carry

        lax.fori_loop(0, ROWS // step, body, 0)

    def axis_scatter(self, level):
        axis, size = self.order[level], (256, 64, 16)[level]
        source = self.core_sum if level == 0 else self.outs[level - 1]
        self.pending = []
        for step in (1, 2, 3):
            peer = moved(self.at, axis, step)
            self.pending.append(
                self.go(
                    source.at[aligned(peer[axis], size), self.cols],
                    self.ins[level].at[step - 1, :, self.cols],
                    1 + 3 * level + step - 1,
                    peer,
                )
            )

    def axis_add(self, level):
        axis, size = self.order[level], (256, 64, 16)[level]
        source = self.core_sum if level == 0 else self.outs[level - 1]
        for copy in self.pending:
            copy.wait_recv()
        step = min(size, 64)

        def body(i, carry):
            rows = aligned(i, step)
            mine = pl.ds(pl.multiple_of(self.at[axis] * size + i * step, step), step)
            total = source[mine, self.cols].astype(f32)
            for j in range(3):
                total = total + self.ins[level][j, rows, self.cols].astype(f32)
            if level < 2:
                self.outs[level][rows, self.cols] = total.astype(bf16)
            else:
                self.o[self.owned(2), self.out_cols] = total.astype(bf16)
            return carry

        lax.fori_loop(0, size // step, body, 0)

    def owned(self, level):
        start = 0
        for axis, size in list(zip(self.order, (256, 64, 16)))[: level + 1]:
            start = start + self.at[axis] * size
        size = (256, 64, 16)[level]
        return pl.ds(pl.multiple_of(start, size), size)

    def axis_gather(self, level):
        axis = self.order[level]
        rows = self.owned(level)
        self.pending = []
        for step in (1, 2, 3):
            peer = moved(self.at, axis, step)
            part = self.o.at[rows, self.out_cols]
            self.pending.append(self.go(part, part, 10 + 3 * (2 - level) + step - 1, peer))

    def gather_wait(self):
        for copy in self.pending:
            copy.wait_recv()

    def core_gather(self):
        part = self.o.at[:, self.out_cols]
        self.pending = [self.go(part, part, 19, moved(self.at, "core", 1))]

    def finish(self):
        self.gather_wait()
        for copy in self.started:
            copy.wait_send()


def reduce_scratch():
    return [
        pltpu.VMEM((ROWS, HALF), bf16),
        pltpu.VMEM((ROWS, HALF), bf16),
        pltpu.VMEM((3, 256, HALF), bf16),
        pltpu.VMEM((3, 64, HALF), bf16),
        pltpu.VMEM((3, 16, HALF), bf16),
        pltpu.VMEM((256, HALF), bf16),
        pltpu.VMEM((64, HALF), bf16),
        pltpu.SemaphoreType.DMA((len(STREAMS), 20)),
        pltpu.SemaphoreType.DMA((len(STREAMS), 20)),
    ]


DEVICES, SLOTS, CH = 128, 32, 128
SIDE = 32
OBS_HERE = 2048


def iota(shape, axis):
    return lax.broadcasted_iota(jnp.int32, shape, axis)


def nt_dot(left, right):
    return lax.dot_general(left, right, (((1,), (1,)), ((), ())), preferred_element_type=f32)


def tn_dot(left, right):
    return lax.dot_general(left, right, (((0,), (0,)), ((), ())), preferred_element_type=f32)


WIDTH = 1024
CELLS = SIDE * SIDE
TANH_SCALE = 0.7978845608028654
CUBIC = 0.044715
SCALE = 1.0 / (CELLS * DEVICES) ** 0.5


def small_reduce(at, axis, level, mine, boxes, send_sem, recv_sem):
    size = 2 if axis == "core" else 4
    boxes[level, at[axis]] = mine
    copies = []
    for step in range(1, size):
        box = boxes.at[level, at[axis]]
        k = 3 * level + step - 1
        copies.append(
            send_to(box, box, send_sem.at[k], recv_sem.at[k], device_at(moved(at, axis, step)))
        )
    return copies


def small_total(axis, level, boxes, copies):
    for copy in copies:
        copy.wait_recv()
    total = boxes[level, 0]
    for k in range(1, 2 if axis == "core" else 4):
        total = total + boxes[level, k]
    return total


def counts_of(kinds):
    shape = kinds.shape
    flat = kinds.reshape(-1, CH)
    lane = iota(flat.shape, 1)
    return jnp.where(lane < 16, pltpu.roll(flat, CH // 2, 1), flat).reshape(shape)


def step_kernel(
    values,
    instr,
    target,
    cell,
    bias,
    kern,
    gain,
    w_in_hbm,
    w_up_hbm,
    w_down_hbm,
    cot_hbm,
    y_hbm,
    down_hbm,
    up_hbm,
    in_hbm,
    o_small,
    feat,
    places,
    packed,
    tags_out,
    got,
    tags_in,
    lands,
    right,
    spots,
    pad,
    side_out,
    side_in,
    corner_out,
    corner_in,
    sems,
    halo_send,
    halo_recv,
    o_down,
    o_up,
    o_in,
    enc,
    enc32,
    inv,
    w_in,
    w_up,
    w_down,
    dyb,
    back,
    h0,
    rinv,
    u,
    dact,
    ds,
    dz,
    two,
    gain_sum,
    boxes,
    load_sem,
    small_send,
    small_recv,
    core_in,
    core_sum,
    in0,
    in1,
    in2,
    out0,
    out1,
    send_sem,
    recv_sem,
):
    at = place()
    inst, tile = lax.axis_index("inst"), lax.axis_index("tile")
    me = inst * 8 + tile
    barrier = pltpu.get_barrier_semaphore()
    loads = [
        pltpu.make_async_copy(source, landing, load_sem.at[k])
        for k, (source, landing) in enumerate(
            ((cot_hbm, dyb), (w_down_hbm, w_down), (w_in_hbm, w_in), (w_up_hbm, w_up))
        )
    ]
    for load in loads:
        load.start()

    def greet_one(i, carry):
        peer = lax.rem(me + i, DEVICES)
        pl.semaphore_signal(
            barrier, inc=1, device_id=(peer // 8, lax.rem(peer, 8)), device_id_type=MESH
        )
        return carry

    lax.fori_loop(1, DEVICES, greet_one, 0)

    def clear(p, carry):
        pad[p] = jnp.zeros((48, 2 * CH), f32)
        dz[p] = jnp.zeros((64, CH), f32)
        return carry

    lax.fori_loop(0, 34, clear, 0)
    for k in (34, 35):
        dz[k] = jnp.zeros((64, CH), f32)

    block = 256
    upper = (iota((block, block), 0) < iota((block, block), 1)).astype(bf16)
    ahead = jnp.zeros((DEVICES, 1), f32)
    tags = jnp.zeros((DEVICES, CH), f32)
    for b in range(OBS_HERE // block):
        cols = slice(b * block, (b + 1) * block)
        to = target[:, cols]
        hit = (to == iota((DEVICES, block), 0)).astype(f32)
        hit16 = hit.astype(bf16)
        before = jnp.dot(hit16, upper, preferred_element_type=f32) + ahead
        slot = jnp.sum(hit * before, axis=0, keepdims=True)
        ahead = ahead + jnp.sum(hit, axis=1, keepdims=True)
        slot = slot.astype(jnp.int32)
        places[:, cols] = to * SLOTS + slot
        mine = (slot == iota((SLOTS, block), 0)).astype(f32)
        where = cell[:, cols]
        notes = jnp.concatenate(
            [
                mine * (where // SIDE + 1).astype(f32),
                mine * (where % SIDE + 1).astype(f32),
                mine * (instr[:, cols] + 1).astype(f32),
                jnp.zeros((SLOTS, block), f32),
            ],
            axis=0,
        ).astype(bf16)
        tags = tags + nt_dot(hit16, notes)
    for t in range(DEVICES):
        tags_out[t] = tags[t : t + 1, :]

    pl.semaphore_wait(barrier, DEVICES - 1)

    def send_slot(source, landing, k, to_inst, to_tile):
        t = to_inst * 8 + to_tile
        pltpu.make_async_remote_copy(
            src_ref=source.at[t],
            dst_ref=landing.at[me],
            send_sem=sems.at[k],
            recv_sem=sems.at[2 + k],
            device_id=(to_inst, to_tile),
            device_id_type=MESH,
        ).start()

    def send_tags(i, carry):
        peer = lax.rem(me + i * 37, DEVICES)
        send_slot(tags_out, tags_in, 1, peer // 8, lax.rem(peer, 8))
        return carry

    lax.fori_loop(1, DEVICES, send_tags, 0)

    hi = bias[...].astype(bf16)
    rest_part = bias[...] - hi.astype(f32)
    mid = rest_part.astype(bf16)
    low = (rest_part - mid.astype(f32)).astype(bf16)
    bias3 = jnp.concatenate([hi, mid, low], axis=0)
    for b in range(OBS_HERE // block):
        cols = slice(b * block, (b + 1) * block)
        pick = (instr[:, cols] == iota((16, block), 0)).astype(f32)
        pick3 = jnp.concatenate([pick, pick, pick], axis=0).T.astype(bf16)
        offset = jnp.dot(pick3, bias3, preferred_element_type=f32)
        feat[cols, :] = (values[cols, :].astype(f32) + offset).astype(bf16)

    group = 8 * SLOTS

    def pack_and_send(i, carry):
        turn = lax.rem(i * 7, 16)
        to_inst = lax.rem(at["z"] + turn // 4, 4) * 4 + lax.rem(at["x"] + lax.rem(turn, 4), 4)
        spot = jnp.clip(places[...] - to_inst * group, -1, group).astype(f32).astype(bf16)
        number = iota((group, OBS_HERE), 0).astype(f32).astype(bf16)
        choose = jnp.where(spot == number, jnp.bfloat16(1), jnp.bfloat16(0))
        rows = jnp.dot(choose, feat[...], preferred_element_type=f32).astype(bf16)
        packed[pl.ds(pl.multiple_of(to_inst * 8, 8), 8)] = rows.reshape(8, SLOTS, CH)

        def send_one(j, inner_carry):
            to_tile = lax.rem(tile + j * 3, 8)

            @pl.when(to_inst * 8 + to_tile != me)
            def _():
                send_slot(packed, got, 0, to_inst, to_tile)

            return inner_carry

        lax.fori_loop(0, 8, send_one, 0)
        return carry

    lax.fori_loop(1, 17, pack_and_send, 0)
    got[me] = packed[me]
    tags_in[me] = tags_out[me]
    others = pl.ds(0, DEVICES - 1)
    pltpu.make_async_copy(tags_in.at[others], tags_in.at[others], sems.at[3]).wait()
    every = tags_in[...].reshape(DEVICES, CH)
    for k in range(3):
        spots[k] = jnp.concatenate(
            [every[SIDE * m : SIDE * (m + 1), 32 * k : 32 * (k + 1)] for m in range(4)], axis=1
        )

    def place_group(g, carry):
        row = pl.ds(g, 1)
        lat, lon, kind = (spots[k, row, :] for k in range(3))
        number = iota((SIDE, CH), 0).astype(f32) + 1.0
        at_lon = (lon == number).astype(f32)
        cols = aligned(g, CH)
        for p in range(SIDE):
            lands[p * SIDE : (p + 1) * SIDE, cols] = jnp.where(
                lat == float(p + 1), at_lon, 0.0
            ).astype(bf16)
        which = iota((CH, CH), 0)
        kinds = jnp.where(
            which < 16, (kind == which.astype(f32) + 1.0).astype(f32), (kind > 0.0).astype(f32)
        )
        right[cols, CH:] = kinds.T.astype(bf16)
        return carry

    lax.fori_loop(0, SIDE, place_group, 0)

    half = CELLS // 2

    def go_back(i):
        rows = pl.ds(i * half, half)
        dy_here = (dyb[rows, :].astype(f32) * SCALE).astype(bf16)
        dyb[rows, :] = dy_here
        back[rows, :] = nt_dot(dy_here, w_down[...])

    loads[0].wait()
    loads[1].wait()
    go_back(0)
    pltpu.make_async_copy(got.at[others], got.at[others], sems.at[2]).wait()

    def collect_rows(g, carry):
        for m in range(4):
            rows = pl.ds(pl.multiple_of(g * CH + m * SLOTS, SLOTS), SLOTS)
            right[rows, :CH] = got[g + SIDE * m]
        return carry

    lax.fori_loop(0, SIDE, collect_rows, 0)

    def sum_block(i, carry):
        total = jnp.dot(lands[aligned(i, half), :], right[...], preferred_element_type=f32)
        pad[pl.ds(1 + 16 * i, 16), 8:40, :] = total.reshape(16, SIDE, 2 * CH)
        return carry

    lax.fori_loop(0, 2, sum_block, 0)

    for p in range(SIDE):
        side_out[0, p : p + 1, :] = pad[1 + p, 8:9, :]
        side_out[1, p : p + 1, :] = pad[1 + p, 39:40, :]
    for k, (p, q) in enumerate(((1, 8), (1, 39), (32, 8), (32, 39))):
        corner_out[k] = pad[p, q : q + 1, :]
    north, south = lax.rem(tile + 7, 8), lax.rem(tile + 1, 8)
    west, east = lax.rem(inst + 15, 16), lax.rem(inst + 1, 16)
    halo = (
        (pad.at[1, 8:40], pad.at[33, 8:40], (inst, north)),
        (pad.at[32, 8:40], pad.at[0, 8:40], (inst, south)),
        (side_out.at[0], side_in.at[1], (west, tile)),
        (side_out.at[1], side_in.at[0], (east, tile)),
        (corner_out.at[0], corner_in.at[3], (west, north)),
        (corner_out.at[1], corner_in.at[2], (east, north)),
        (corner_out.at[2], corner_in.at[1], (west, south)),
        (corner_out.at[3], corner_in.at[0], (east, south)),
    )
    halo_copies = [
        send_to(source, landing, halo_send.at[k], halo_recv.at[k], to)
        for k, (source, landing, to) in enumerate(halo)
    ]
    go_back(1)
    for load in loads[2:]:
        load.wait()
    for copy in halo_copies:
        copy.wait_recv()
    keep_north = (tile > 0).astype(f32)
    keep_south = (tile < 7).astype(f32)
    keep_west = (inst > 0).astype(f32)
    keep_east = (inst < 15).astype(f32)
    pad[0, 8:40, :] = pad[0, 8:40, :] * keep_north
    pad[33, 8:40, :] = pad[33, 8:40, :] * keep_south
    for p in range(SIDE):
        pad[1 + p, 7:8, :] = side_in[0, p : p + 1, :] * keep_west
        pad[1 + p, 40:41, :] = side_in[1, p : p + 1, :] * keep_east
    pad[0, 7:8, :] = corner_in[0] * (keep_north * keep_west)
    pad[0, 40:41, :] = corner_in[1] * (keep_north * keep_east)
    pad[33, 7:8, :] = corner_in[2] * (keep_south * keep_west)
    pad[33, 40:41, :] = corner_in[3] * (keep_south * keep_east)

    lats = 4

    def encode(i, carry):
        spread = jnp.zeros((lats, SIDE, CH), f32)
        density = jnp.zeros((lats, SIDE, CH), f32)
        near = pl.ds(lats * i, lats + 2)
        for b in (-1, 0, 1):
            sums = pad[near, 8 + b : 40 + b, :CH]
            counts = counts_of(pad[near, 8 + b : 40 + b, CH:])
            for a in (-1, 0, 1):
                j = 3 * (a + 1) + (b + 1)
                weight = kern[j : j + 1, :].reshape(1, 1, CH)
                spread = spread + weight * sums[1 + a : 1 + a + lats]
                density = density + weight * counts[1 + a : 1 + a + lats]
        share = 1.0 / (1.0 + density)
        value = spread * share
        here = pl.ds(lats * i, lats)
        inv[here] = share
        enc32[here] = value
        enc[aligned(i, lats * SIDE), :] = value.reshape(lats * SIDE, CH).astype(bf16)
        return carry

    lax.fori_loop(0, SIDE // lats, encode, 0)
    for copy in halo_copies:
        copy.wait_send()
    for source, k in ((packed, 0), (tags_out, 1)):
        pltpu.make_async_copy(source.at[others], source.at[others], sems.at[k]).wait()

    give, keep = lands.at[:, :HALF], lands.at[:, HALF : 2 * HALF]
    g = lands.at[:, 2 * HALF : 2 * HALF + WIDTH]
    bufs = (core_in, core_sum, (in0, in1, in2), (out0, out1))
    outs = (o_down, o_up, o_in)
    streams = [
        Stream(k, at, give, keep, outs, bufs, send_sem, recv_sem) for k in range(len(STREAMS))
    ]
    down, up, rest = [streams[k] for k in (1, 2, 0)], [streams[k] for k in (3, 5, 4)], streams[6:]
    core = at["core"]

    def forward(i, carry):
        rows = aligned(i, block)
        h = jnp.dot(enc[rows, :], w_in[...], preferred_element_type=f32)
        h0[rows, :] = h
        r = lax.rsqrt(jnp.mean(h * h, axis=-1, keepdims=True) + 1e-06)
        rinv[rows, :] = jnp.broadcast_to(r, (block, CH))
        u_here = (h * r * gain[...]).astype(bf16)
        u[rows, :] = u_here
        for n in range(WIDTH // block):
            cols = slice(n * block, (n + 1) * block)
            act = jnp.dot(u_here, w_up[:, cols], preferred_element_type=f32)
            square = act * act
            tanh = jnp.tanh(TANH_SCALE * act * (1.0 + CUBIC * square))
            cdf = 0.5 + 0.5 * tanh
            slope = cdf + act * (0.5 - 0.5 * tanh * tanh) * (
                TANH_SCALE + (3.0 * CUBIC * TANH_SCALE) * square
            )
            g[rows, cols] = (act * cdf).astype(bf16)
            dact[rows, cols] = (slope * back[rows, cols]).astype(bf16)
        return carry

    lax.fori_loop(0, CELLS // block, forward, 0)

    def weight_grad(left, right_side, into, part, first):
        cols_in = aligned(part, 512)

        def body(i, carry):
            cols = aligned(i, 512)
            into[cols, first : first + 512] = tn_dot(left[:, cols], right_side[:, cols_in]).astype(
                bf16
            )
            return carry

        lax.fori_loop(0, WIDTH // 512, body, 0)

    weight_grad(g, dyb, give, 1 - core, 0)
    for s in down:
        s.core_scatter()
    weight_grad(g, dyb, keep, core, 0)
    for s in down:
        s.core_add()
        s.axis_scatter(0)
    weight_grad(u, dact, give, 1 - core, 512)
    for s in up:
        s.core_scatter()
    weight_grad(u, dact, keep, core, 512)
    for s in up:
        s.core_add()
        s.axis_scatter(0)

    gain_sum[...] = jnp.zeros_like(gain_sum)

    def backward(i, carry):
        rows = aligned(i, block)
        du = nt_dot(dact[rows, :], w_up[...])
        h = h0[rows, :]
        r = rinv[rows, :1]
        gain_sum[...] += jnp.sum(du * h * r, axis=0, keepdims=True)
        scaled = du * gain[...]
        mean = jnp.mean(scaled * h, axis=-1, keepdims=True)
        dh = (r * scaled - h * (r * r * r * mean) + dyb[rows, :].astype(f32)).astype(bf16)
        u[rows, :] = dh
        denc = nt_dot(dh, w_in[...])
        eight = pl.ds(pl.multiple_of(i * 8, 8), 8)
        ds[eight] = denc.reshape(8, SIDE, CH) * inv[eight]
        return carry

    lax.fori_loop(0, 2, backward, 0)
    for s in down:
        s.axis_add(0)
        s.axis_scatter(1)
    lax.fori_loop(2, 4, backward, 0)
    for s in down:
        s.axis_add(1)
        s.axis_scatter(2)

    def in_grad(i, carry):
        cols = aligned(i, block)
        part = tn_dot(enc[...], u[:, cols]).T
        give[cols, 1024:] = jnp.where(core == 1, part, 0.0).astype(bf16)
        keep[cols, 1024:] = jnp.where(core == 0, part, 0.0).astype(bf16)
        return carry

    lax.fori_loop(0, WIDTH // block, in_grad, 0)
    for s in rest:
        s.core_scatter()
    for s in up:
        s.axis_add(0)
        s.axis_scatter(1)

    def filter_grad(i, totals):
        near, here = pl.ds(lats * i, lats + 2), pl.ds(lats * i, lats)
        slope = ds[here]
        dz[pl.ds(lats * i + 2, lats), 16:48] = slope
        both = slope * enc32[here]
        new = list(totals)
        for b in (-1, 0, 1):
            sums = pad[near, 8 + b : 40 + b, :CH]
            counts = counts_of(pad[near, 8 + b : 40 + b, CH:])
            for a in (-1, 0, 1):
                j = 3 * (a + 1) + (b + 1)
                part = slope * sums[1 + a : 1 + a + lats] - both * counts[1 + a : 1 + a + lats]
                new[j] = new[j] + jnp.sum(part.reshape(lats * 4, 8, CH), axis=0)
        return tuple(new)

    zeros = jnp.zeros((8, CH), f32)
    filter_sums = lax.fori_loop(0, SIDE // lats, filter_grad, (zeros,) * 9)
    for s in down:
        s.axis_add(2)
        s.axis_gather(2)
    for s in rest:
        s.core_add()
        s.axis_scatter(0)

    def spread_back(i, carry):
        value = jnp.zeros((2, 48, CH), f32)
        for b in (-1, 0, 1):
            slab = dz[pl.ds(2 * i, 4), 8 - b : 56 - b, :]
            for a in (-1, 0, 1):
                j = 3 * (a + 1) + (b + 1)
                value = value + kern[j : j + 1, :].reshape(1, 1, CH) * slab[1 - a : 3 - a]
        kinds = pad[pl.ds(2 * i, 2), :, CH:]
        rows = aligned(i, 96)
        for part, k in ((value, 0), (kinds, 1)):
            part = part.reshape(96, CH)
            top = part.astype(bf16)
            two[k, rows, :CH] = top
            two[k, rows, CH:] = (part - top.astype(f32)).astype(bf16)
        return carry

    lax.fori_loop(0, 17, spread_back, 0)
    quarters = tn_dot(two[1], two[0])
    bias_sum = (quarters[:16, :CH] + quarters[:16, CH:]) + (
        quarters[CH : CH + 16, :CH] + quarters[CH : CH + 16, CH:]
    )
    small = jnp.concatenate(
        [gain_sum[:, k * CH : (k + 1) * CH] for k in range(8)]
        + [jnp.sum(part, axis=0, keepdims=True) for part in filter_sums]
        + [jnp.zeros((7, CH), f32), bias_sum],
        axis=0,
    )
    small_copies = small_reduce(at, "x", 0, small, boxes, small_send, small_recv)
    all_small = list(small_copies)
    for s in up:
        s.axis_add(1)
        s.axis_scatter(2)
    for s in down:
        s.gather_wait()
        s.axis_gather(1)

    def forecast(i):
        rows = pl.ds(i * half, half)
        y = h0[rows, :] + jnp.dot(g[rows, :], w_down[...], preferred_element_type=f32)
        dact[rows, :] = y.astype(bf16)

    forecast(0)
    for s in rest:
        s.axis_add(0)
        s.axis_scatter(1)
    small = small_total("x", 0, boxes, small_copies)
    small_copies = small_reduce(at, "y", 1, small, boxes, small_send, small_recv)
    all_small += small_copies
    for s in up:
        s.axis_add(2)
        s.axis_gather(2)
    for s in down:
        s.gather_wait()
        s.axis_gather(0)
    forecast(1)
    stores = [pltpu.make_async_copy(dact, y_hbm, load_sem.at[4])]
    stores[0].start()
    for s in rest:
        s.axis_add(1)
        s.axis_scatter(2)
    small = small_total("y", 1, boxes, small_copies)
    small_copies = small_reduce(at, "z", 2, small, boxes, small_send, small_recv)
    all_small += small_copies
    for s in up:
        s.gather_wait()
        s.axis_gather(1)
    for s in rest:
        s.axis_add(2)
        s.axis_gather(2)
    small = small_total("z", 2, boxes, small_copies)
    small_copies = small_reduce(at, "core", 3, small, boxes, small_send, small_recv)
    all_small += small_copies
    for s in up:
        s.gather_wait()
        s.axis_gather(0)
    for s in rest:
        s.gather_wait()
        s.axis_gather(1)
    for s in down:
        s.gather_wait()
        s.core_gather()
    o_small[...] = small_total("core", 3, boxes, small_copies)
    for s in rest:
        s.gather_wait()
        s.axis_gather(0)
    for s in down:
        s.finish()
    stores.append(pltpu.make_async_copy(o_down, down_hbm, load_sem.at[5]))
    stores[1].start()
    for s in up + rest:
        s.gather_wait()
        s.core_gather()
    for s in up + rest:
        s.finish()
    for k, (source, landing) in enumerate(((o_up, up_hbm), (o_in, in_hbm))):
        stores.append(pltpu.make_async_copy(source, landing, load_sem.at[6 + k]))
        stores[2 + k].start()
    for copy in all_small:
        copy.wait_send()
    for store in stores:
        store.wait()


def step(values, instr, target, cell, bias, kern, gain, w_in, w_up, w_down, cot):
    vmem, hbm = pl.BlockSpec(memory_space=pltpu.VMEM), pl.BlockSpec(memory_space=pl.ANY)
    return pl.pallas_call(
        step_kernel,
        out_shape=(
            jax.ShapeDtypeStruct((CELLS, WIDTH), bf16),
            jax.ShapeDtypeStruct((WIDTH, WIDTH), bf16),
            jax.ShapeDtypeStruct((WIDTH, WIDTH), bf16),
            jax.ShapeDtypeStruct((WIDTH, 2 * CH), bf16),
            jax.ShapeDtypeStruct((40, CH), f32),
        ),
        in_specs=[vmem] * 7 + [hbm] * 4,
        out_specs=[hbm] * 4 + [vmem],
        scratch_shapes=[
            pltpu.VMEM((OBS_HERE, CH), bf16),
            pltpu.VMEM((1, OBS_HERE), jnp.int32),
            pltpu.VMEM((DEVICES, SLOTS, CH), bf16),
            pltpu.VMEM((DEVICES, 1, CH), f32),
            pltpu.VMEM((DEVICES, SLOTS, CH), bf16),
            pltpu.VMEM((DEVICES, 1, CH), f32),
            pltpu.VMEM((CELLS, DEVICES * SLOTS), bf16),
            pltpu.VMEM((DEVICES * SLOTS, 2 * CH), bf16),
            pltpu.VMEM((3, SIDE, CH), f32),
            pltpu.VMEM((34, 48, 2 * CH), f32),
            pltpu.VMEM((2, SIDE, 2 * CH), f32),
            pltpu.VMEM((2, SIDE, 2 * CH), f32),
            pltpu.VMEM((4, 1, 2 * CH), f32),
            pltpu.VMEM((4, 1, 2 * CH), f32),
            pltpu.SemaphoreType.DMA((4,)),
            pltpu.SemaphoreType.DMA((8,)),
            pltpu.SemaphoreType.DMA((8,)),
            pltpu.VMEM((WIDTH, WIDTH), bf16),
            pltpu.VMEM((WIDTH, WIDTH), bf16),
            pltpu.VMEM((WIDTH, 2 * CH), bf16),
            pltpu.VMEM((CELLS, CH), bf16),
            pltpu.VMEM((SIDE, SIDE, CH), f32),
            pltpu.VMEM((SIDE, SIDE, CH), f32),
            pltpu.VMEM((CH, WIDTH), bf16),
            pltpu.VMEM((WIDTH, WIDTH), bf16),
            pltpu.VMEM((WIDTH, WIDTH), bf16),
            pltpu.VMEM((CELLS, WIDTH), bf16),
            pltpu.VMEM((CELLS, WIDTH), f32),
            pltpu.VMEM((CELLS, WIDTH), f32),
            pltpu.VMEM((CELLS, CH), f32),
            pltpu.VMEM((CELLS, WIDTH), bf16),
            pltpu.VMEM((CELLS, WIDTH), bf16),
            pltpu.VMEM((SIDE, SIDE, CH), f32),
            pltpu.VMEM((36, 64, CH), f32),
            pltpu.VMEM((2, 34 * 48, 2 * CH), bf16),
            pltpu.VMEM((1, WIDTH), f32),
            pltpu.VMEM((4, 4, 40, CH), f32),
            pltpu.SemaphoreType.DMA((8,)),
            pltpu.SemaphoreType.DMA((12,)),
            pltpu.SemaphoreType.DMA((12,)),
        ]
        + reduce_scratch(),
        compiler_params=pltpu.CompilerParams(
            collective_id=0, has_side_effects=True, vmem_limit_bytes=62 << 20
        ),
    )(values, instr, target, cell, bias, kern, gain, w_in, w_up, w_down, cot)


def widen_kernel(y, down, up, into, small, y_out, down_out, up_out, in_out, gain, kern, bias):
    y_out[...] = y[...]
    down_out[...] = down[...].astype(f32)
    up_out[...] = up[...].astype(f32)
    in_out[...] = into[:, :CH].astype(f32).T
    gain[...] = small[:8]
    kern[...] = small[8:17]
    bias[...] = small[24:40]


def widen(y, down, up, into, small):
    block = 128
    wide = pl.BlockSpec((block, WIDTH), lambda i: (i, 0))

    def whole(rows):
        return pl.BlockSpec((rows, CH), lambda i: (0, 0))

    return pl.pallas_call(
        widen_kernel,
        grid=(WIDTH // block,),
        out_shape=(
            jax.ShapeDtypeStruct((CELLS, WIDTH), bf16),
            jax.ShapeDtypeStruct((WIDTH, WIDTH), f32),
            jax.ShapeDtypeStruct((WIDTH, WIDTH), f32),
            jax.ShapeDtypeStruct((CH, WIDTH), f32),
            jax.ShapeDtypeStruct((8, CH), f32),
            jax.ShapeDtypeStruct((9, CH), f32),
            jax.ShapeDtypeStruct((16, CH), f32),
        ),
        in_specs=[wide, wide, wide, pl.BlockSpec((block, 2 * CH), lambda i: (i, 0)), whole(40)],
        out_specs=[
            wide,
            wide,
            wide,
            pl.BlockSpec((CH, block), lambda i: (0, i)),
            whole(8),
            whole(9),
            whole(16),
        ],
        compiler_params=pltpu.CompilerParams(vmem_limit_bytes=60 << 20),
    )(y, down, up, into, small)


def shards(
    obs_values,
    obs_instrument,
    obs_target,
    obs_cell,
    inst_bias,
    kernel,
    w_in,
    norm_gain,
    w_up,
    w_down,
    cotangent,
):
    y, down, up, into, small = step(
        obs_values,
        obs_instrument.reshape(1, OBS_HERE),
        obs_target.reshape(1, OBS_HERE),
        obs_cell.reshape(1, OBS_HERE),
        inst_bias,
        kernel,
        norm_gain.reshape(1, WIDTH),
        w_in,
        w_up,
        w_down,
        cotangent.reshape(CELLS, WIDTH),
    )
    y, down, up, into, gain, filters, bias = widen(y, down, up, into, small)
    return (y.reshape(cotangent.shape), into, up, down, gain.reshape(WIDTH), filters, bias)


def solution(mesh):
    return jax.shard_map(
        shards,
        mesh=mesh,
        in_specs=(
            P(("inst", "tile"), None),
            P(("inst", "tile")),
            P(("inst", "tile"), None),
            P(("inst", "tile")),
            P(),
            P(),
            P(),
            P(),
            P(),
            P(),
            P("tile", "inst", None),
        ),
        out_specs=(P("tile", "inst", None), P(), P(), P(), P(), P(), P()),
        check_vma=False,
    )
```

```python
import functools

import jax
import jax.numpy as jnp
from jax import lax
from jax.experimental import pallas as pl
from jax.experimental.pallas import tpu as pltpu
from jax.sharding import PartitionSpec as P

offsets = [(a, b) for a in (-1, 0, 1) for b in (-1, 0, 1)]
f32, bf16 = jnp.float32, jnp.bfloat16


MESH = pl.DeviceIdType.MESH
HALF = 1152
ROWS = 1024
STREAMS = (
    (0, 256, "x", "yz", 0, 0),
    (256, 256, "y", "zx", 0, 256),
    (512, 256, "z", "xy", 1, 0),
    (768, 128, "x", "yz", 1, 256),
    (896, 128, "y", "zx", 1, 384),
    (1024, 128, "z", "xy", 2, 0),
)


PLAN = (
    "gd0", 1, 0, "gd1", "gu0", 2, 4, "gu1", "b0", 0, 3, 2, 4, "b1", 1, "b2", "b3", "i", 5, 4, 0,
    3, 5, 2, 1, 4, "f", 3, 5, 0, 2, 1, 4, 5, 0, 3, 2, "t", "s", 1, "y0", 5, 3, 4, "s", "y1", 0,
    "s", 2, 3, 1, "s", 5, 4, 0, "s", 1, 3, 2, 5,
)


def place():
    inst, tile = lax.axis_index("inst"), lax.axis_index("tile")
    return {"z": inst // 4, "x": inst % 4, "y": tile // 2, "core": tile % 2}


def device_at(at):
    return (at["z"] * 4 + at["x"], at["y"] * 2 + at["core"])


def moved(at, axis, step):
    size = 2 if axis == "core" else 4
    return {**at, axis: lax.rem(at[axis] + step, size)}


def send_to(source, landing, send_sem, recv_sem, to):
    copy = pltpu.make_async_remote_copy(
        src_ref=source,
        dst_ref=landing,
        send_sem=send_sem,
        recv_sem=recv_sem,
        device_id=to,
        device_id_type=MESH,
    )
    copy.start()
    return copy


def aligned(index, size):
    return pl.ds(pl.multiple_of(index * size, size), size)


class Stream:
    def __init__(self, number, at, give, keep, outs, bufs, send_sem, recv_sem):
        first, wide, self.axis, self.plane, output, first_out = STREAMS[number]
        self.cols = pl.ds(first, wide)
        self.at, self.give, self.keep, self.o = at, give, keep, outs[output]
        half = self.o.shape[1] // 2
        self.out_cols = pl.ds(pl.multiple_of(at["core"] * half + first_out, 128), wide)
        self.core_in, self.core_sum, self.axis_in, self.plane_in, self.axis_sum = bufs
        self.sends, self.recvs = send_sem.at[number], recv_sem.at[number]
        self.mine = at[self.plane[0]] * 4 + at[self.plane[1]]
        self.done = 0

    def go(self, source, target, slot, at):
        send_to(source, target, self.sends.at[slot], self.recvs.at[slot], device_at(at))

    def to_axis(self, slot, refs):
        for step in (1, 2, 3):
            peer = moved(self.at, self.axis, step)
            self.go(*refs(step, peer), slot, peer)

    def to_plane(self, slot, refs):
        def body(step, carry):
            peer = moved(self.at, self.plane[0], step // 4)
            peer = moved(peer, self.plane[1], lax.rem(step, 4))
            self.go(*refs(step, peer), slot, peer)
            return carry

        lax.fori_loop(1, 16, body, 0)

    def arrived(self, slot, ref):
        pltpu.make_async_copy(ref, ref, self.recvs.at[slot]).wait()

    def rows_of(self, count):
        return self.o.at[pl.ds(0, count), self.out_cols]

    def my_rows(self, size):
        start = self.at[self.axis] * 256
        if size == 16:
            start = start + self.mine * 16
        return pl.ds(pl.multiple_of(start, size), size)

    def step0(self):
        other = moved(self.at, "core", 1)
        self.go(self.give.at[:, self.cols], self.core_in.at[:, self.cols], 0, other)

    def step1(self):
        self.arrived(0, self.core_in.at[:, self.cols])
        size = 256

        def body(i, carry):
            rows = aligned(i, size)
            total = self.keep[rows, self.cols].astype(f32) + self.core_in[rows, self.cols].astype(f32)
            self.core_sum[rows, self.cols] = total.astype(bf16)
            return carry

        lax.fori_loop(0, ROWS // size, body, 0)
        self.to_axis(
            1,
            lambda step, peer: (
                self.core_sum.at[aligned(peer[self.axis], 256), self.cols],
                self.axis_in.at[step - 1, :, self.cols],
            ),
        )

    def step2(self):
        self.arrived(1, self.axis_in.at[:, :, self.cols])
        size = 64

        def body(i, carry):
            rows = aligned(i, size)
            own = pl.ds(pl.multiple_of(self.at[self.axis] * 256 + i * size, size), size)
            total = self.core_sum[own, self.cols].astype(f32)
            for j in range(3):
                total = total + self.axis_in[j, rows, self.cols].astype(f32)
            self.axis_sum[rows, self.cols] = total.astype(bf16)
            return carry

        lax.fori_loop(0, 256 // size, body, 0)
        self.to_plane(
            2,
            lambda step, peer: (
                self.axis_sum.at[
                    aligned(peer[self.plane[0]] * 4 + peer[self.plane[1]], 16), self.cols
                ],
                self.plane_in.at[step - 1, :, self.cols],
            ),
        )

    def step3(self):
        self.arrived(2, self.plane_in.at[:, :, self.cols])
        total = self.axis_sum[aligned(self.mine, 16), self.cols].astype(f32)
        for j in range(15):
            total = total + self.plane_in[j, :, self.cols].astype(f32)
        self.o[self.my_rows(16), self.out_cols] = total.astype(bf16)
        part = self.o.at[self.my_rows(16), self.out_cols]
        self.to_plane(3, lambda step, peer: (part, part))

    def step4(self):
        self.arrived(3, self.rows_of(240))
        part = self.o.at[self.my_rows(256), self.out_cols]
        self.to_axis(4, lambda step, peer: (part, part))

    def step5(self):
        self.arrived(4, self.rows_of(768))
        part = self.o.at[:, self.out_cols]
        self.go(part, part, 5, moved(self.at, "core", 1))

    def step6(self):
        self.arrived(5, self.rows_of(ROWS))

    def advance(self):
        getattr(self, "step" + str(self.done))()
        self.done += 1

    def finish(self):
        for slot, rows in enumerate((ROWS, 768, 240, 240, 768, ROWS)):
            ref = self.rows_of(rows)
            pltpu.make_async_copy(ref, ref, self.sends.at[slot]).wait()


def reduce_scratch():
    return [
        pltpu.VMEM((ROWS, HALF), bf16),
        pltpu.VMEM((ROWS, HALF), bf16),
        pltpu.VMEM((3, 256, HALF), bf16),
        pltpu.VMEM((15, 16, HALF), bf16),
        pltpu.VMEM((256, HALF), bf16),
        pltpu.SemaphoreType.DMA((len(STREAMS), 6)),
        pltpu.SemaphoreType.DMA((len(STREAMS), 6)),
    ]


DEVICES, SLOTS, CH = 128, 32, 128
SIDE = 32
OBS_HERE = 2048


def iota(shape, axis):
    return lax.broadcasted_iota(jnp.int32, shape, axis)


def nt_dot(left, right):
    return lax.dot_general(left, right, (((1,), (1,)), ((), ())), preferred_element_type=f32)


def tn_dot(left, right):
    return lax.dot_general(left, right, (((0,), (0,)), ((), ())), preferred_element_type=f32)


WIDTH = 1024
CELLS = SIDE * SIDE
TANH_SCALE = 0.7978845608028654
CUBIC = 0.044715
SCALE = 1.0 / (CELLS * DEVICES) ** 0.5


def small_reduce(at, axis, level, mine, boxes, send_sem, recv_sem):
    size = 2 if axis == "core" else 4
    boxes[level, at[axis]] = mine
    copies = []
    for step in range(1, size):
        box = boxes.at[level, at[axis]]
        k = 3 * level + step - 1
        copies.append(
            send_to(box, box, send_sem.at[k], recv_sem.at[k], device_at(moved(at, axis, step)))
        )
    return copies


def small_total(axis, level, boxes, copies):
    for copy in copies:
        copy.wait_recv()
    total = boxes[level, 0]
    for k in range(1, 2 if axis == "core" else 4):
        total = total + boxes[level, k]
    return total


def counts_of(kinds):
    shape = kinds.shape
    flat = kinds.reshape(-1, CH)
    lane = iota(flat.shape, 1)
    return jnp.where(lane < 16, pltpu.roll(flat, CH // 2, 1), flat).reshape(shape)


def step_kernel(
    values,
    instr,
    target,
    cell,
    bias,
    kern,
    gain,
    w_in_hbm,
    w_up_hbm,
    w_down_hbm,
    cot_hbm,
    y_hbm,
    down_hbm,
    up_hbm,
    in_hbm,
    o_small,
    feat,
    places,
    packed,
    tags_out,
    got,
    tags_in,
    lands,
    right,
    spots,
    pad,
    side_out,
    side_in,
    corner_out,
    corner_in,
    sems,
    halo_send,
    halo_recv,
    rows_in,
    o_down,
    o_up,
    o_in,
    enc,
    enc32,
    inv,
    w_in,
    w_up,
    w_down,
    dyb,
    back,
    h0,
    rinv,
    u,
    dact,
    ds,
    dz,
    two,
    gain_sum,
    boxes,
    load_sem,
    small_send,
    small_recv,
    core_in,
    core_sum,
    in0,
    in1,
    out0,
    send_sem,
    recv_sem,
):
    at = place()
    inst, tile = lax.axis_index("inst"), lax.axis_index("tile")
    me = inst * 8 + tile
    barrier = pltpu.get_barrier_semaphore()
    loads = [
        pltpu.make_async_copy(source, landing, load_sem.at[k])
        for k, (source, landing) in enumerate(
            ((cot_hbm, dyb), (w_down_hbm, w_down), (w_in_hbm, w_in), (w_up_hbm, w_up))
        )
    ]
    for load in loads:
        load.start()

    def greet_row(i, carry):
        peer = (inst, lax.rem(tile + i, 8))
        pl.semaphore_signal(barrier, inc=1, device_id=peer, device_id_type=MESH)
        return carry

    def greet_column(i, carry):
        peer = (lax.rem(inst + i, 16), tile)
        pl.semaphore_signal(barrier, inc=1, device_id=peer, device_id_type=MESH)
        return carry

    def tell_column(i, carry):
        peer = (lax.rem(inst + i, 16), tile)
        pl.semaphore_signal(rows_in, inc=1, device_id=peer, device_id_type=MESH)
        return carry

    lax.fori_loop(1, 8, greet_row, 0)
    lax.fori_loop(1, 16, greet_column, 0)

    def clear(p, carry):
        pad[p] = jnp.zeros((48, 2 * CH), f32)
        dz[p] = jnp.zeros((64, CH), f32)
        return carry

    lax.fori_loop(0, 34, clear, 0)
    for k in (34, 35):
        dz[k] = jnp.zeros((64, CH), f32)

    block = 256
    upper = (iota((block, block), 0) < iota((block, block), 1)).astype(bf16)
    ahead = jnp.zeros((DEVICES, 1), f32)
    tags = jnp.zeros((DEVICES, CH), f32)
    for b in range(OBS_HERE // block):
        cols = slice(b * block, (b + 1) * block)
        to = target[:, cols]
        hit = (to == iota((DEVICES, block), 0)).astype(f32)
        hit16 = hit.astype(bf16)
        before = jnp.dot(hit16, upper, preferred_element_type=f32) + ahead
        slot = jnp.sum(hit * before, axis=0, keepdims=True)
        ahead = ahead + jnp.sum(hit, axis=1, keepdims=True)
        slot = slot.astype(jnp.int32)
        places[:, cols] = to * SLOTS + slot
        mine = (slot == iota((SLOTS, block), 0)).astype(f32)
        where = cell[:, cols]
        notes = jnp.concatenate(
            [
                mine * (where // SIDE + 1).astype(f32),
                mine * (where % SIDE + 1).astype(f32),
                mine * (instr[:, cols] + 1).astype(f32),
                jnp.zeros((SLOTS, block), f32),
            ],
            axis=0,
        ).astype(bf16)
        tags = tags + nt_dot(hit16, notes)
    for t in range(DEVICES):
        tags_out[t] = tags[t : t + 1, :]

    pl.semaphore_wait(barrier, 22)
    lax.fori_loop(1, 16, tell_column, 0)

    hi = bias[...].astype(bf16)
    rest_part = bias[...] - hi.astype(f32)
    mid = rest_part.astype(bf16)
    low = (rest_part - mid.astype(f32)).astype(bf16)
    bias3 = jnp.concatenate([hi, mid, low], axis=0)
    for b in range(OBS_HERE // block):
        cols = slice(b * block, (b + 1) * block)
        pick = (instr[:, cols] == iota((16, block), 0)).astype(f32)
        pick3 = jnp.concatenate([pick, pick, pick], axis=0).T.astype(bf16)
        offset = jnp.dot(pick3, bias3, preferred_element_type=f32)
        feat[cols, :] = (values[cols, :].astype(f32) + offset).astype(bf16)

    pl.semaphore_wait(rows_in, 15)

    def send_slot(source, landing, k, to_inst, to_tile):
        t = to_inst * 8 + to_tile
        pltpu.make_async_remote_copy(
            src_ref=source.at[t],
            dst_ref=landing.at[me],
            send_sem=sems.at[k],
            recv_sem=sems.at[2 + k],
            device_id=(to_inst, to_tile),
            device_id_type=MESH,
        ).start()

    def send_tags(i, carry):
        peer = lax.rem(me + i * 37, DEVICES)
        send_slot(tags_out, tags_in, 1, peer // 8, lax.rem(peer, 8))
        return carry

    group = 8 * SLOTS

    def pack_and_send(i, carry):
        turn = lax.rem(i * 7, 16)
        to_inst = lax.rem(at["z"] + turn // 4, 4) * 4 + lax.rem(at["x"] + lax.rem(turn, 4), 4)
        spot = jnp.clip(places[...] - to_inst * group, -1, group).astype(f32).astype(bf16)
        number = iota((group, OBS_HERE), 0).astype(f32).astype(bf16)
        choose = jnp.where(spot == number, jnp.bfloat16(1), jnp.bfloat16(0))
        rows = jnp.dot(choose, feat[...], preferred_element_type=f32).astype(bf16)
        packed[pl.ds(pl.multiple_of(to_inst * 8, 8), 8)] = rows.reshape(8, SLOTS, CH)

        def send_one(j, inner_carry):
            to_tile = lax.rem(tile + j * 3, 8)

            @pl.when(to_inst * 8 + to_tile != me)
            def _():
                send_slot(packed, got, 0, to_inst, to_tile)

            return inner_carry

        lax.fori_loop(0, 8, send_one, 0)
        lax.fori_loop(
            jnp.minimum((i - 1) * 16 + 1, DEVICES), jnp.minimum(i * 16 + 1, DEVICES), send_tags, 0
        )
        return carry

    lax.fori_loop(1, 17, pack_and_send, 0)
    got[me] = packed[me]
    tags_in[me] = tags_out[me]
    others = pl.ds(0, DEVICES - 1)
    pltpu.make_async_copy(tags_in.at[others], tags_in.at[others], sems.at[3]).wait()
    every = tags_in[...].reshape(DEVICES, CH)
    for k in range(3):
        spots[k] = jnp.concatenate(
            [every[SIDE * m : SIDE * (m + 1), 32 * k : 32 * (k + 1)] for m in range(4)], axis=1
        )

    def place_group(g, carry):
        row = pl.ds(g, 1)
        lat, lon, kind = (spots[k, row, :] for k in range(3))
        number = iota((SIDE, CH), 0).astype(f32) + 1.0
        at_lon = (lon == number).astype(f32)
        cols = aligned(g, CH)
        for p in range(SIDE):
            lands[p * SIDE : (p + 1) * SIDE, cols] = jnp.where(
                lat == float(p + 1), at_lon, 0.0
            ).astype(bf16)
        which = iota((CH, CH), 0)
        kinds = jnp.where(
            which < 16, (kind == which.astype(f32) + 1.0).astype(f32), (kind > 0.0).astype(f32)
        )
        right[cols, CH:] = kinds.T.astype(bf16)
        return carry

    lax.fori_loop(0, SIDE, place_group, 0)

    half = CELLS // 2

    def go_back(i):
        rows = pl.ds(i * half, half)
        dy_here = (dyb[rows, :].astype(f32) * SCALE).astype(bf16)
        dyb[rows, :] = dy_here
        back[rows, :] = nt_dot(dy_here, w_down[...])

    loads[0].wait()
    loads[1].wait()
    go_back(0)
    pltpu.make_async_copy(got.at[others], got.at[others], sems.at[2]).wait()

    def collect_rows(g, carry):
        for m in range(4):
            rows = pl.ds(pl.multiple_of(g * CH + m * SLOTS, SLOTS), SLOTS)
            right[rows, :CH] = got[g + SIDE * m]
        return carry

    lax.fori_loop(0, SIDE, collect_rows, 0)

    def sum_block(i, carry):
        total = jnp.dot(lands[aligned(i, half), :], right[...], preferred_element_type=f32)
        pad[pl.ds(1 + 16 * i, 16), 8:40, :] = total.reshape(16, SIDE, 2 * CH)
        return carry

    lax.fori_loop(0, 2, sum_block, 0)

    for p in range(SIDE):
        side_out[0, p : p + 1, :] = pad[1 + p, 8:9, :]
        side_out[1, p : p + 1, :] = pad[1 + p, 39:40, :]
    for k, (p, q) in enumerate(((1, 8), (1, 39), (32, 8), (32, 39))):
        corner_out[k] = pad[p, q : q + 1, :]
    north, south = lax.rem(tile + 7, 8), lax.rem(tile + 1, 8)
    west, east = lax.rem(inst + 15, 16), lax.rem(inst + 1, 16)
    halo = (
        (pad.at[1, 8:40], pad.at[33, 8:40], (inst, north)),
        (pad.at[32, 8:40], pad.at[0, 8:40], (inst, south)),
        (side_out.at[0], side_in.at[1], (west, tile)),
        (side_out.at[1], side_in.at[0], (east, tile)),
        (corner_out.at[0], corner_in.at[3], (west, north)),
        (corner_out.at[1], corner_in.at[2], (east, north)),
        (corner_out.at[2], corner_in.at[1], (west, south)),
        (corner_out.at[3], corner_in.at[0], (east, south)),
    )
    halo_copies = [
        send_to(source, landing, halo_send.at[k], halo_recv.at[k], to)
        for k, (source, landing, to) in enumerate(halo)
    ]
    go_back(1)
    for load in loads[2:]:
        load.wait()
    for copy in halo_copies:
        copy.wait_recv()
    keep_north = (tile > 0).astype(f32)
    keep_south = (tile < 7).astype(f32)
    keep_west = (inst > 0).astype(f32)
    keep_east = (inst < 15).astype(f32)
    pad[0, 8:40, :] = pad[0, 8:40, :] * keep_north
    pad[33, 8:40, :] = pad[33, 8:40, :] * keep_south
    for p in range(SIDE):
        pad[1 + p, 7:8, :] = side_in[0, p : p + 1, :] * keep_west
        pad[1 + p, 40:41, :] = side_in[1, p : p + 1, :] * keep_east
    pad[0, 7:8, :] = corner_in[0] * (keep_north * keep_west)
    pad[0, 40:41, :] = corner_in[1] * (keep_north * keep_east)
    pad[33, 7:8, :] = corner_in[2] * (keep_south * keep_west)
    pad[33, 40:41, :] = corner_in[3] * (keep_south * keep_east)

    lats = 4

    def encode(i, carry):
        spread = jnp.zeros((lats, SIDE, CH), f32)
        density = jnp.zeros((lats, SIDE, CH), f32)
        near = pl.ds(lats * i, lats + 2)
        for b in (-1, 0, 1):
            sums = pad[near, 8 + b : 40 + b, :CH]
            counts = counts_of(pad[near, 8 + b : 40 + b, CH:])
            for a in (-1, 0, 1):
                j = 3 * (a + 1) + (b + 1)
                weight = kern[j : j + 1, :].reshape(1, 1, CH)
                spread = spread + weight * sums[1 + a : 1 + a + lats]
                density = density + weight * counts[1 + a : 1 + a + lats]
        share = 1.0 / (1.0 + density)
        value = spread * share
        here = pl.ds(lats * i, lats)
        inv[here] = share
        enc32[here] = value
        enc[aligned(i, lats * SIDE), :] = value.reshape(lats * SIDE, CH).astype(bf16)
        return carry

    lax.fori_loop(0, SIDE // lats, encode, 0)
    for copy in halo_copies:
        copy.wait_send()
    for source, k in ((packed, 0), (tags_out, 1)):
        pltpu.make_async_copy(source.at[others], source.at[others], sems.at[k]).wait()

    give, keep = lands.at[:, :HALF], lands.at[:, HALF : 2 * HALF]
    g = lands.at[:, 2 * HALF : 2 * HALF + WIDTH]
    bufs = (core_in, core_sum, in0, in1, out0)
    outs = (o_down, o_up, o_in)
    streams = [
        Stream(k, at, give, keep, outs, bufs, send_sem, recv_sem) for k in range(len(STREAMS))
    ]
    core = at["core"]

    def forward(i, carry):
        rows = aligned(i, block)
        h = jnp.dot(enc[rows, :], w_in[...], preferred_element_type=f32)
        h0[rows, :] = h
        r = lax.rsqrt(jnp.mean(h * h, axis=-1, keepdims=True) + 1e-06)
        rinv[rows, :] = jnp.broadcast_to(r, (block, CH))
        u_here = (h * r * gain[...]).astype(bf16)
        u[rows, :] = u_here
        for n in range(WIDTH // block):
            cols = slice(n * block, (n + 1) * block)
            act = jnp.dot(u_here, w_up[:, cols], preferred_element_type=f32)
            square = act * act
            tanh = jnp.tanh(TANH_SCALE * act * (1.0 + CUBIC * square))
            cdf = 0.5 + 0.5 * tanh
            slope = cdf + act * (0.5 - 0.5 * tanh * tanh) * (
                TANH_SCALE + (3.0 * CUBIC * TANH_SCALE) * square
            )
            g[rows, cols] = (act * cdf).astype(bf16)
            dact[rows, cols] = (slope * back[rows, cols]).astype(bf16)
        return carry

    lax.fori_loop(0, CELLS // block, forward, 0)

    def weight_grad(left, right_side, into, part, first):
        cols_in = aligned(part, 512)

        def body(i, carry):
            cols = aligned(i, 512)
            into[cols, first : first + 512] = tn_dot(left[:, cols], right_side[:, cols_in]).astype(
                bf16
            )
            return carry

        lax.fori_loop(0, WIDTH // 512, body, 0)

    gain_sum[...] = jnp.zeros_like(gain_sum)

    def backward(i, carry):
        rows = pl.ds(i * block, block)
        du = nt_dot(dact[rows, :], w_up[...])
        h = h0[rows, :]
        r = rinv[rows, :1]
        gain_sum[...] += jnp.sum(du * h * r, axis=0, keepdims=True)
        scaled = du * gain[...]
        mean = jnp.mean(scaled * h, axis=-1, keepdims=True)
        dh = (r * scaled - h * (r * r * r * mean) + dyb[rows, :].astype(f32)).astype(bf16)
        u[rows, :] = dh
        denc = nt_dot(dh, w_in[...])
        eight = pl.ds(i * 8, 8)
        ds[eight] = denc.reshape(8, SIDE, CH) * inv[eight]
        return carry

    def in_grad(i, carry):
        cols = aligned(i, block)
        part = tn_dot(enc[...], u[:, cols]).T
        give[cols, 1024:] = jnp.where(core == 1, part, 0.0).astype(bf16)
        keep[cols, 1024:] = jnp.where(core == 0, part, 0.0).astype(bf16)
        return carry

    def filter_grad(i, totals):
        near, here = pl.ds(lats * i, lats + 2), pl.ds(lats * i, lats)
        slope = ds[here]
        dz[pl.ds(lats * i + 2, lats), 16:48] = slope
        both = slope * enc32[here]
        new = list(totals)
        for b in (-1, 0, 1):
            sums = pad[near, 8 + b : 40 + b, :CH]
            counts = counts_of(pad[near, 8 + b : 40 + b, CH:])
            for a in (-1, 0, 1):
                j = 3 * (a + 1) + (b + 1)
                part = slope * sums[1 + a : 1 + a + lats] - both * counts[1 + a : 1 + a + lats]
                new[j] = new[j] + jnp.sum(part.reshape(lats * 4, 8, CH), axis=0)
        return tuple(new)

    def spread_back(i, carry):
        value = jnp.zeros((2, 48, CH), f32)
        for b in (-1, 0, 1):
            slab = dz[pl.ds(2 * i, 4), 8 - b : 56 - b, :]
            for a in (-1, 0, 1):
                j = 3 * (a + 1) + (b + 1)
                value = value + kern[j : j + 1, :].reshape(1, 1, CH) * slab[1 - a : 3 - a]
        kinds = pad[pl.ds(2 * i, 2), :, CH:]
        rows = aligned(i, 96)
        for part, k in ((value, 0), (kinds, 1)):
            part = part.reshape(96, CH)
            top = part.astype(bf16)
            two[k, rows, :CH] = top
            two[k, rows, CH:] = (part - top.astype(f32)).astype(bf16)
        return carry

    def forecast(i):
        rows = pl.ds(i * half, half)
        y = h0[rows, :] + jnp.dot(g[rows, :], w_down[...], preferred_element_type=f32)
        dact[rows, :] = y.astype(bf16)

    totals = {}

    def take_filter():
        zeros = jnp.zeros((8, CH), f32)
        totals["filter"] = lax.fori_loop(0, SIDE // lats, filter_grad, (zeros,) * 9)

    def take_small():
        lax.fori_loop(0, 17, spread_back, 0)
        quarters = tn_dot(two[1], two[0])
        bias_sum = (quarters[:16, :CH] + quarters[:16, CH:]) + (
            quarters[CH : CH + 16, :CH] + quarters[CH : CH + 16, CH:]
        )
        totals["small"] = jnp.concatenate(
            [gain_sum[:, k * CH : (k + 1) * CH] for k in range(8)]
            + [jnp.sum(part, axis=0, keepdims=True) for part in totals["filter"]]
            + [jnp.zeros((7, CH), f32), bias_sum],
            axis=0,
        )

    all_small, small_levels = [], ("x", "y", "z", "core")

    def pass_small():
        level = totals.get("level", 0)
        if level:
            total = small_total(small_levels[level - 1], level - 1, boxes, totals["copies"])
        else:
            total = totals["small"]
        if level == 4:
            o_small[...] = total
            return
        totals["copies"] = small_reduce(
            at, small_levels[level], level, total, boxes, small_send, small_recv
        )
        all_small.extend(totals["copies"])
        totals["level"] = level + 1

    stores = []

    def store(source, landing):
        stores.append(pltpu.make_async_copy(source, landing, load_sem.at[4 + len(stores)]))
        stores[-1].start()

    def last_forecast():
        forecast(1)
        store(dact, y_hbm)

    tasks = {
        "gd0": lambda: weight_grad(g, dyb, give, 1 - core, 0),
        "gd1": lambda: weight_grad(g, dyb, keep, core, 0),
        "gu0": lambda: weight_grad(u, dact, give, 1 - core, 512),
        "gu1": lambda: weight_grad(u, dact, keep, core, 512),
        "b0": lambda: backward(0, 0),
        "b1": lambda: backward(1, 0),
        "b2": lambda: backward(2, 0),
        "b3": lambda: backward(3, 0),
        "i": lambda: lax.fori_loop(0, WIDTH // block, in_grad, 0),
        "f": take_filter,
        "t": take_small,
        "s": pass_small,
        "y0": lambda: forecast(0),
        "y1": last_forecast,
    }
    for task in PLAN:
        if task in tasks:
            tasks[task]()
            continue
        streams[task].advance()
        if streams[0].done == 7 and streams[1].done == 7 and task in (0, 1):
            store(o_down, down_hbm)
        if all(streams[k].done == 7 for k in (2, 3, 4)) and task in (2, 3, 4):
            store(o_up, up_hbm)
    store(o_in, in_hbm)
    for s in streams:
        s.finish()
    for copy in all_small:
        copy.wait_send()
    for copy in stores:
        copy.wait()


def step(values, instr, target, cell, bias, kern, gain, w_in, w_up, w_down, cot):
    vmem, hbm = pl.BlockSpec(memory_space=pltpu.VMEM), pl.BlockSpec(memory_space=pl.ANY)
    return pl.pallas_call(
        step_kernel,
        out_shape=(
            jax.ShapeDtypeStruct((CELLS, WIDTH), bf16),
            jax.ShapeDtypeStruct((WIDTH, WIDTH), bf16),
            jax.ShapeDtypeStruct((WIDTH, WIDTH), bf16),
            jax.ShapeDtypeStruct((WIDTH, 2 * CH), bf16),
            jax.ShapeDtypeStruct((40, CH), f32),
        ),
        in_specs=[vmem] * 7 + [hbm] * 4,
        out_specs=[hbm] * 4 + [vmem],
        scratch_shapes=[
            pltpu.VMEM((OBS_HERE, CH), bf16),
            pltpu.VMEM((1, OBS_HERE), jnp.int32),
            pltpu.VMEM((DEVICES, SLOTS, CH), bf16),
            pltpu.VMEM((DEVICES, 1, CH), f32),
            pltpu.VMEM((DEVICES, SLOTS, CH), bf16),
            pltpu.VMEM((DEVICES, 1, CH), f32),
            pltpu.VMEM((CELLS, DEVICES * SLOTS), bf16),
            pltpu.VMEM((DEVICES * SLOTS, 2 * CH), bf16),
            pltpu.VMEM((3, SIDE, CH), f32),
            pltpu.VMEM((34, 48, 2 * CH), f32),
            pltpu.VMEM((2, SIDE, 2 * CH), f32),
            pltpu.VMEM((2, SIDE, 2 * CH), f32),
            pltpu.VMEM((4, 1, 2 * CH), f32),
            pltpu.VMEM((4, 1, 2 * CH), f32),
            pltpu.SemaphoreType.DMA((4,)),
            pltpu.SemaphoreType.DMA((8,)),
            pltpu.SemaphoreType.DMA((8,)),
            pltpu.SemaphoreType.REGULAR,
            pltpu.VMEM((WIDTH, WIDTH), bf16),
            pltpu.VMEM((WIDTH, WIDTH), bf16),
            pltpu.VMEM((WIDTH, 2 * CH), bf16),
            pltpu.VMEM((CELLS, CH), bf16),
            pltpu.VMEM((SIDE, SIDE, CH), f32),
            pltpu.VMEM((SIDE, SIDE, CH), f32),
            pltpu.VMEM((CH, WIDTH), bf16),
            pltpu.VMEM((WIDTH, WIDTH), bf16),
            pltpu.VMEM((WIDTH, WIDTH), bf16),
            pltpu.VMEM((CELLS, WIDTH), bf16),
            pltpu.VMEM((CELLS, WIDTH), f32),
            pltpu.VMEM((CELLS, WIDTH), f32),
            pltpu.VMEM((CELLS, CH), f32),
            pltpu.VMEM((CELLS, WIDTH), bf16),
            pltpu.VMEM((CELLS, WIDTH), bf16),
            pltpu.VMEM((SIDE, SIDE, CH), f32),
            pltpu.VMEM((36, 64, CH), f32),
            pltpu.VMEM((2, 34 * 48, 2 * CH), bf16),
            pltpu.VMEM((1, WIDTH), f32),
            pltpu.VMEM((4, 4, 40, CH), f32),
            pltpu.SemaphoreType.DMA((8,)),
            pltpu.SemaphoreType.DMA((12,)),
            pltpu.SemaphoreType.DMA((12,)),
        ]
        + reduce_scratch(),
        compiler_params=pltpu.CompilerParams(
            collective_id=0, has_side_effects=True, vmem_limit_bytes=62 << 20
        ),
    )(values, instr, target, cell, bias, kern, gain, w_in, w_up, w_down, cot)


def widen_kernel(
    y, down, up, into, small, y_out, down_out, up_out, in_out, gain, kern, bias, *scratch
):
    down_in, up_in, in_in, down_wide, up_wide, in_wide, sems, out_sems = scratch
    size, parts = 256, 4
    rows = [pl.ds(k * size, size) for k in range(parts)]
    loads = [pltpu.make_async_copy(into, in_in, sems.at[0])]
    for k in range(parts):
        for which, (source, landing) in enumerate(((down, down_in), (up, up_in))):
            loads.append(
                pltpu.make_async_copy(
                    source.at[rows[k]], landing.at[rows[k]], sems.at[1 + 2 * k + which]
                )
            )
    for load in loads:
        load.start()
    stores = [pltpu.make_async_copy(y, y_out, out_sems.at[0])]
    stores[0].start()
    gain[...] = small[:8]
    kern[...] = small[8:17]
    bias[...] = small[24:40]
    loads[0].wait()
    for k in range(parts):
        in_wide[:, k * size : (k + 1) * size] = in_in[rows[k], :CH].astype(f32).T
    stores.append(pltpu.make_async_copy(in_wide, in_out, out_sems.at[1]))
    stores[1].start()
    for k in range(parts):
        for which, (narrow, wide, landing) in enumerate(
            ((down_in, down_wide, down_out), (up_in, up_wide, up_out))
        ):
            loads[1 + 2 * k + which].wait()
            wide[rows[k], :] = narrow[rows[k], :].astype(f32)
            stores.append(
                pltpu.make_async_copy(
                    wide.at[rows[k]], landing.at[rows[k]], out_sems.at[2 + 2 * k + which]
                )
            )
            stores[-1].start()
    for store in stores:
        store.wait()


def widen(y, down, up, into, small):
    vmem, hbm = pl.BlockSpec(memory_space=pltpu.VMEM), pl.BlockSpec(memory_space=pl.ANY)
    return pl.pallas_call(
        widen_kernel,
        out_shape=(
            jax.ShapeDtypeStruct((CELLS, WIDTH), bf16),
            jax.ShapeDtypeStruct((WIDTH, WIDTH), f32),
            jax.ShapeDtypeStruct((WIDTH, WIDTH), f32),
            jax.ShapeDtypeStruct((CH, WIDTH), f32),
            jax.ShapeDtypeStruct((8, CH), f32),
            jax.ShapeDtypeStruct((9, CH), f32),
            jax.ShapeDtypeStruct((16, CH), f32),
        ),
        in_specs=[hbm] * 4 + [vmem],
        out_specs=[hbm] * 4 + [vmem] * 3,
        scratch_shapes=[
            pltpu.VMEM((WIDTH, WIDTH), bf16),
            pltpu.VMEM((WIDTH, WIDTH), bf16),
            pltpu.VMEM((WIDTH, 2 * CH), bf16),
            pltpu.VMEM((WIDTH, WIDTH), f32),
            pltpu.VMEM((WIDTH, WIDTH), f32),
            pltpu.VMEM((CH, WIDTH), f32),
            pltpu.SemaphoreType.DMA((9,)),
            pltpu.SemaphoreType.DMA((10,)),
        ],
        compiler_params=pltpu.CompilerParams(vmem_limit_bytes=60 << 20),
    )(y, down, up, into, small)


def shards(
    obs_values,
    obs_instrument,
    obs_target,
    obs_cell,
    inst_bias,
    kernel,
    w_in,
    norm_gain,
    w_up,
    w_down,
    cotangent,
):
    y, down, up, into, small = step(
        obs_values,
        obs_instrument.reshape(1, OBS_HERE),
        obs_target.reshape(1, OBS_HERE),
        obs_cell.reshape(1, OBS_HERE),
        inst_bias,
        kernel,
        norm_gain.reshape(1, WIDTH),
        w_in,
        w_up,
        w_down,
        cotangent.reshape(CELLS, WIDTH),
    )
    y, down, up, into, gain, filters, bias = widen(y, down, up, into, small)
    return (y.reshape(cotangent.shape), into, up, down, gain.reshape(WIDTH), filters, bias)


def solution(mesh):
    return jax.shard_map(
        shards,
        mesh=mesh,
        in_specs=(
            P(("inst", "tile"), None),
            P(("inst", "tile")),
            P(("inst", "tile"), None),
            P(("inst", "tile")),
            P(),
            P(),
            P(),
            P(),
            P(),
            P(),
            P("tile", "inst", None),
        ),
        out_specs=(P("tile", "inst", None), P(), P(), P(), P(), P(), P()),
        check_vma=False,
    )
```

```python
import functools

import jax
import jax.numpy as jnp
from jax import lax
from jax.experimental import pallas as pl
from jax.experimental.pallas import tpu as pltpu
from jax.sharding import PartitionSpec as P

offsets = [(a, b) for a in (-1, 0, 1) for b in (-1, 0, 1)]
f32, bf16 = jnp.float32, jnp.bfloat16


MESH = pl.DeviceIdType.MESH
HALF = 1152
ROWS = 1024
STREAMS = (
    (0, 256, "x", "yz", 0, 0),
    (256, 256, "y", "zx", 0, 256),
    (512, 256, "z", "xy", 1, 0),
    (768, 128, "x", "yz", 1, 256),
    (896, 128, "y", "zx", 1, 384),
    (1024, 128, "z", "xy", 2, 0),
)


PLAN = (
    "gd0", 0, 1, "gd1", 0, 1, "gu0", 2, 3, 4, "gu1", 2, 3, 4, "b0", "b1", "b2", "b3", 0, 1, "i",
    5, 2, 3, 4, 5, "f", 0, 1, "t", "s", 2, 3, 4, 5, "s", 0, 1, "y0", 2, 3, 4, 5, "s", "y1", 0,
    1, 2, 3, 4, 5, "s", 0, 1, 2, 3, 4, 5, "s", 5,
)


def place():
    inst, tile = lax.axis_index("inst"), lax.axis_index("tile")
    return {"z": inst // 4, "x": inst % 4, "y": tile // 2, "core": tile % 2}


def device_at(at):
    return (at["z"] * 4 + at["x"], at["y"] * 2 + at["core"])


def moved(at, axis, step):
    size = 2 if axis == "core" else 4
    return {**at, axis: lax.rem(at[axis] + step, size)}


def send_to(source, landing, send_sem, recv_sem, to):
    copy = pltpu.make_async_remote_copy(
        src_ref=source,
        dst_ref=landing,
        send_sem=send_sem,
        recv_sem=recv_sem,
        device_id=to,
        device_id_type=MESH,
    )
    copy.start()
    return copy


def aligned(index, size):
    return pl.ds(pl.multiple_of(index * size, size), size)


class Stream:
    def __init__(self, number, at, give, keep, outs, bufs, send_sem, recv_sem):
        first, wide, self.axis, self.plane, output, first_out = STREAMS[number]
        self.cols = pl.ds(first, wide)
        self.at, self.give, self.keep, self.o = at, give, keep, outs[output]
        half = self.o.shape[1] // 2
        self.out_cols = pl.ds(pl.multiple_of(at["core"] * half + first_out, 128), wide)
        self.core_in, self.core_sum, self.axis_in, self.plane_in, self.axis_sum = bufs
        self.sends, self.recvs = send_sem.at[number], recv_sem.at[number]
        self.mine = at[self.plane[0]] * 4 + at[self.plane[1]]
        self.done = 0

    def go(self, source, target, slot, at):
        send_to(source, target, self.sends.at[slot], self.recvs.at[slot], device_at(at))

    def to_axis(self, slot, refs):
        for step in (1, 2, 3):
            peer = moved(self.at, self.axis, step)
            self.go(*refs(step, peer), slot, peer)

    def to_plane(self, slot, refs):
        def body(step, carry):
            peer = moved(self.at, self.plane[0], step // 4)
            peer = moved(peer, self.plane[1], lax.rem(step, 4))
            self.go(*refs(step, peer), slot, peer)
            return carry

        lax.fori_loop(1, 16, body, 0)

    def arrived(self, slot, ref):
        pltpu.make_async_copy(ref, ref, self.recvs.at[slot]).wait()

    def rows_of(self, count):
        return self.o.at[pl.ds(0, count), self.out_cols]

    def my_rows(self, size):
        start = self.at[self.axis] * 256
        if size == 16:
            start = start + self.mine * 16
        return pl.ds(pl.multiple_of(start, size), size)

    def step0(self):
        other = moved(self.at, "core", 1)
        self.go(self.give.at[:, self.cols], self.core_in.at[:, self.cols], 0, other)

    def step1(self):
        self.arrived(0, self.core_in.at[:, self.cols])
        size = 256

        def body(i, carry):
            rows = aligned(i, size)
            total = self.keep[rows, self.cols].astype(f32) + self.core_in[rows, self.cols].astype(f32)
            self.core_sum[rows, self.cols] = total.astype(bf16)
            return carry

        lax.fori_loop(0, ROWS // size, body, 0)
        self.to_axis(
            1,
            lambda step, peer: (
                self.core_sum.at[aligned(peer[self.axis], 256), self.cols],
                self.axis_in.at[step - 1, :, self.cols],
            ),
        )

    def step2(self):
        self.arrived(1, self.axis_in.at[:, :, self.cols])
        size = 64

        def body(i, carry):
            rows = aligned(i, size)
            own = pl.ds(pl.multiple_of(self.at[self.axis] * 256 + i * size, size), size)
            total = self.core_sum[own, self.cols].astype(f32)
            for j in range(3):
                total = total + self.axis_in[j, rows, self.cols].astype(f32)
            self.axis_sum[rows, self.cols] = total.astype(bf16)
            return carry

        lax.fori_loop(0, 256 // size, body, 0)
        self.to_plane(
            2,
            lambda step, peer: (
                self.axis_sum.at[
                    aligned(peer[self.plane[0]] * 4 + peer[self.plane[1]], 16), self.cols
                ],
                self.plane_in.at[step - 1, :, self.cols],
            ),
        )

    def step3(self):
        self.arrived(2, self.plane_in.at[:, :, self.cols])
        total = self.axis_sum[aligned(self.mine, 16), self.cols].astype(f32)
        for j in range(15):
            total = total + self.plane_in[j, :, self.cols].astype(f32)
        self.o[self.my_rows(16), self.out_cols] = total.astype(bf16)
        part = self.o.at[self.my_rows(16), self.out_cols]
        self.to_plane(3, lambda step, peer: (part, part))

    def step4(self):
        self.arrived(3, self.rows_of(240))
        part = self.o.at[self.my_rows(256), self.out_cols]
        self.to_axis(4, lambda step, peer: (part, part))

    def step5(self):
        self.arrived(4, self.rows_of(768))
        part = self.o.at[:, self.out_cols]
        self.go(part, part, 5, moved(self.at, "core", 1))

    def step6(self):
        self.arrived(5, self.rows_of(ROWS))

    def advance(self):
        getattr(self, "step" + str(self.done))()
        self.done += 1

    def finish(self):
        for slot, rows in enumerate((ROWS, 768, 240, 240, 768, ROWS)):
            ref = self.rows_of(rows)
            pltpu.make_async_copy(ref, ref, self.sends.at[slot]).wait()


def reduce_scratch():
    return [
        pltpu.VMEM((ROWS, HALF), bf16),
        pltpu.VMEM((ROWS, HALF), bf16),
        pltpu.VMEM((3, 256, HALF), bf16),
        pltpu.VMEM((15, 16, HALF), bf16),
        pltpu.VMEM((256, HALF), bf16),
        pltpu.SemaphoreType.DMA((len(STREAMS), 6)),
        pltpu.SemaphoreType.DMA((len(STREAMS), 6)),
    ]


DEVICES, SLOTS, CH = 128, 32, 128
SIDE = 32
OBS_HERE = 2048


def iota(shape, axis):
    return lax.broadcasted_iota(jnp.int32, shape, axis)


def nt_dot(left, right):
    return lax.dot_general(left, right, (((1,), (1,)), ((), ())), preferred_element_type=f32)


def tn_dot(left, right):
    return lax.dot_general(left, right, (((0,), (0,)), ((), ())), preferred_element_type=f32)


WIDTH = 1024
CELLS = SIDE * SIDE
TANH_SCALE = 0.7978845608028654
CUBIC = 0.044715
SCALE = 1.0 / (CELLS * DEVICES) ** 0.5


def small_reduce(at, axis, level, mine, boxes, send_sem, recv_sem):
    size = 2 if axis == "core" else 4
    boxes[level, at[axis]] = mine
    copies = []
    for step in range(1, size):
        box = boxes.at[level, at[axis]]
        k = 3 * level + step - 1
        copies.append(
            send_to(box, box, send_sem.at[k], recv_sem.at[k], device_at(moved(at, axis, step)))
        )
    return copies


def small_total(axis, level, boxes, copies):
    for copy in copies:
        copy.wait_recv()
    total = boxes[level, 0]
    for k in range(1, 2 if axis == "core" else 4):
        total = total + boxes[level, k]
    return total


def counts_of(kinds):
    shape = kinds.shape
    flat = kinds.reshape(-1, CH)
    lane = iota(flat.shape, 1)
    return jnp.where(lane < 16, pltpu.roll(flat, CH // 2, 1), flat).reshape(shape)


def step_kernel(
    values,
    instr,
    target,
    cell,
    bias,
    kern,
    gain,
    w_in_hbm,
    w_up_hbm,
    w_down_hbm,
    cot_hbm,
    y_hbm,
    down_hbm,
    up_hbm,
    in_hbm,
    o_small,
    feat,
    places,
    packed,
    tags_out,
    got,
    tags_in,
    lands,
    right,
    spots,
    pad,
    side_out,
    side_in,
    corner_out,
    corner_in,
    sems,
    halo_send,
    halo_recv,
    rows_in,
    o_down,
    o_up,
    o_in,
    enc,
    enc32,
    inv,
    w_in,
    w_up,
    w_down,
    dyb,
    back,
    h0,
    rinv,
    u,
    dact,
    ds,
    dz,
    two,
    gain_sum,
    boxes,
    load_sem,
    small_send,
    small_recv,
    core_in,
    core_sum,
    in0,
    in1,
    out0,
    send_sem,
    recv_sem,
):
    at = place()
    inst, tile = lax.axis_index("inst"), lax.axis_index("tile")
    me = inst * 8 + tile
    barrier = pltpu.get_barrier_semaphore()
    loads = [
        pltpu.make_async_copy(source, landing, load_sem.at[k])
        for k, (source, landing) in enumerate(
            ((cot_hbm, dyb), (w_down_hbm, w_down), (w_in_hbm, w_in), (w_up_hbm, w_up))
        )
    ]
    for load in loads:
        load.start()

    def greet_row(i, carry):
        peer = (inst, lax.rem(tile + i, 8))
        pl.semaphore_signal(barrier, inc=1, device_id=peer, device_id_type=MESH)
        return carry

    def greet_column(i, carry):
        peer = (lax.rem(inst + i, 16), tile)
        pl.semaphore_signal(barrier, inc=1, device_id=peer, device_id_type=MESH)
        return carry

    def tell_column(i, carry):
        peer = (lax.rem(inst + i, 16), tile)
        pl.semaphore_signal(rows_in, inc=1, device_id=peer, device_id_type=MESH)
        return carry

    lax.fori_loop(1, 8, greet_row, 0)
    lax.fori_loop(1, 16, greet_column, 0)

    def clear(p, carry):
        pad[p] = jnp.zeros((48, 2 * CH), f32)
        dz[p] = jnp.zeros((64, CH), f32)
        return carry

    lax.fori_loop(0, 34, clear, 0)
    for k in (34, 35):
        dz[k] = jnp.zeros((64, CH), f32)

    block = 256
    upper = (iota((block, block), 0) < iota((block, block), 1)).astype(bf16)
    ahead = jnp.zeros((DEVICES, 1), f32)
    tags = jnp.zeros((DEVICES, CH), f32)
    for b in range(OBS_HERE // block):
        cols = slice(b * block, (b + 1) * block)
        to = target[:, cols]
        hit = (to == iota((DEVICES, block), 0)).astype(f32)
        hit16 = hit.astype(bf16)
        before = jnp.dot(hit16, upper, preferred_element_type=f32) + ahead
        slot = jnp.sum(hit * before, axis=0, keepdims=True)
        ahead = ahead + jnp.sum(hit, axis=1, keepdims=True)
        slot = slot.astype(jnp.int32)
        places[:, cols] = to * SLOTS + slot
        mine = (slot == iota((SLOTS, block), 0)).astype(f32)
        where = cell[:, cols]
        notes = jnp.concatenate(
            [
                mine * (where // SIDE + 1).astype(f32),
                mine * (where % SIDE + 1).astype(f32),
                mine * (instr[:, cols] + 1).astype(f32),
                jnp.zeros((SLOTS, block), f32),
            ],
            axis=0,
        ).astype(bf16)
        tags = tags + nt_dot(hit16, notes)
    for t in range(DEVICES):
        tags_out[t] = tags[t : t + 1, :]

    pl.semaphore_wait(barrier, 22)
    lax.fori_loop(1, 16, tell_column, 0)

    hi = bias[...].astype(bf16)
    rest_part = bias[...] - hi.astype(f32)
    mid = rest_part.astype(bf16)
    low = (rest_part - mid.astype(f32)).astype(bf16)
    bias3 = jnp.concatenate([hi, mid, low], axis=0)
    for b in range(OBS_HERE // block):
        cols = slice(b * block, (b + 1) * block)
        pick = (instr[:, cols] == iota((16, block), 0)).astype(f32)
        pick3 = jnp.concatenate([pick, pick, pick], axis=0).T.astype(bf16)
        offset = jnp.dot(pick3, bias3, preferred_element_type=f32)
        feat[cols, :] = (values[cols, :].astype(f32) + offset).astype(bf16)

    pl.semaphore_wait(rows_in, 15)

    def send_slot(source, landing, k, to_inst, to_tile):
        t = to_inst * 8 + to_tile
        pltpu.make_async_remote_copy(
            src_ref=source.at[t],
            dst_ref=landing.at[me],
            send_sem=sems.at[k],
            recv_sem=sems.at[2 + k],
            device_id=(to_inst, to_tile),
            device_id_type=MESH,
        ).start()

    def send_tags(i, carry):
        peer = lax.rem(me + i * 37, DEVICES)
        send_slot(tags_out, tags_in, 1, peer // 8, lax.rem(peer, 8))
        return carry

    group = 8 * SLOTS

    def pack_and_send(i, carry):
        turn = lax.rem(i * 7, 16)
        to_inst = lax.rem(at["z"] + turn // 4, 4) * 4 + lax.rem(at["x"] + lax.rem(turn, 4), 4)
        spot = jnp.clip(places[...] - to_inst * group, -1, group).astype(f32).astype(bf16)
        number = iota((group, OBS_HERE), 0).astype(f32).astype(bf16)
        choose = jnp.where(spot == number, jnp.bfloat16(1), jnp.bfloat16(0))
        rows = jnp.dot(choose, feat[...], preferred_element_type=f32).astype(bf16)
        packed[pl.ds(pl.multiple_of(to_inst * 8, 8), 8)] = rows.reshape(8, SLOTS, CH)

        def send_one(j, inner_carry):
            to_tile = lax.rem(tile + j * 3, 8)

            @pl.when(to_inst * 8 + to_tile != me)
            def _():
                send_slot(packed, got, 0, to_inst, to_tile)

            return inner_carry

        lax.fori_loop(0, 8, send_one, 0)
        lax.fori_loop(
            jnp.minimum((i - 1) * 16 + 1, DEVICES), jnp.minimum(i * 16 + 1, DEVICES), send_tags, 0
        )
        return carry

    lax.fori_loop(1, 17, pack_and_send, 0)
    got[me] = packed[me]
    tags_in[me] = tags_out[me]
    others = pl.ds(0, DEVICES - 1)
    pltpu.make_async_copy(tags_in.at[others], tags_in.at[others], sems.at[3]).wait()
    every = tags_in[...].reshape(DEVICES, CH)
    for k in range(3):
        spots[k] = jnp.concatenate(
            [every[SIDE * m : SIDE * (m + 1), 32 * k : 32 * (k + 1)] for m in range(4)], axis=1
        )

    def place_group(g, carry):
        row = pl.ds(g, 1)
        lat, lon, kind = (spots[k, row, :] for k in range(3))
        number = iota((SIDE, CH), 0).astype(f32) + 1.0
        at_lon = (lon == number).astype(f32)
        cols = aligned(g, CH)
        for p in range(SIDE):
            lands[p * SIDE : (p + 1) * SIDE, cols] = jnp.where(
                lat == float(p + 1), at_lon, 0.0
            ).astype(bf16)
        which = iota((CH, CH), 0)
        kinds = jnp.where(
            which < 16, (kind == which.astype(f32) + 1.0).astype(f32), (kind > 0.0).astype(f32)
        )
        right[cols, CH:] = kinds.T.astype(bf16)
        return carry

    lax.fori_loop(0, SIDE, place_group, 0)

    half = CELLS // 2

    def go_back(i):
        rows = pl.ds(i * half, half)
        dy_here = (dyb[rows, :].astype(f32) * SCALE).astype(bf16)
        dyb[rows, :] = dy_here
        back[rows, :] = nt_dot(dy_here, w_down[...])

    loads[0].wait()
    loads[1].wait()
    go_back(0)
    pltpu.make_async_copy(got.at[others], got.at[others], sems.at[2]).wait()

    def collect_rows(g, carry):
        for m in range(4):
            rows = pl.ds(pl.multiple_of(g * CH + m * SLOTS, SLOTS), SLOTS)
            right[rows, :CH] = got[g + SIDE * m]
        return carry

    lax.fori_loop(0, SIDE, collect_rows, 0)

    def sum_block(i, carry):
        total = jnp.dot(lands[aligned(i, half), :], right[...], preferred_element_type=f32)
        pad[pl.ds(1 + 16 * i, 16), 8:40, :] = total.reshape(16, SIDE, 2 * CH)
        return carry

    lax.fori_loop(0, 2, sum_block, 0)

    for p in range(SIDE):
        side_out[0, p : p + 1, :] = pad[1 + p, 8:9, :]
        side_out[1, p : p + 1, :] = pad[1 + p, 39:40, :]
    for k, (p, q) in enumerate(((1, 8), (1, 39), (32, 8), (32, 39))):
        corner_out[k] = pad[p, q : q + 1, :]
    north, south = lax.rem(tile + 7, 8), lax.rem(tile + 1, 8)
    west, east = lax.rem(inst + 15, 16), lax.rem(inst + 1, 16)
    halo = (
        (pad.at[1, 8:40], pad.at[33, 8:40], (inst, north)),
        (pad.at[32, 8:40], pad.at[0, 8:40], (inst, south)),
        (side_out.at[0], side_in.at[1], (west, tile)),
        (side_out.at[1], side_in.at[0], (east, tile)),
        (corner_out.at[0], corner_in.at[3], (west, north)),
        (corner_out.at[1], corner_in.at[2], (east, north)),
        (corner_out.at[2], corner_in.at[1], (west, south)),
        (corner_out.at[3], corner_in.at[0], (east, south)),
    )
    halo_copies = [
        send_to(source, landing, halo_send.at[k], halo_recv.at[k], to)
        for k, (source, landing, to) in enumerate(halo)
    ]
    go_back(1)
    for load in loads[2:]:
        load.wait()
    for copy in halo_copies:
        copy.wait_recv()
    keep_north = (tile > 0).astype(f32)
    keep_south = (tile < 7).astype(f32)
    keep_west = (inst > 0).astype(f32)
    keep_east = (inst < 15).astype(f32)
    pad[0, 8:40, :] = pad[0, 8:40, :] * keep_north
    pad[33, 8:40, :] = pad[33, 8:40, :] * keep_south
    for p in range(SIDE):
        pad[1 + p, 7:8, :] = side_in[0, p : p + 1, :] * keep_west
        pad[1 + p, 40:41, :] = side_in[1, p : p + 1, :] * keep_east
    pad[0, 7:8, :] = corner_in[0] * (keep_north * keep_west)
    pad[0, 40:41, :] = corner_in[1] * (keep_north * keep_east)
    pad[33, 7:8, :] = corner_in[2] * (keep_south * keep_west)
    pad[33, 40:41, :] = corner_in[3] * (keep_south * keep_east)

    lats = 4

    def encode(i, carry):
        spread = jnp.zeros((lats, SIDE, CH), f32)
        density = jnp.zeros((lats, SIDE, CH), f32)
        near = pl.ds(lats * i, lats + 2)
        for b in (-1, 0, 1):
            sums = pad[near, 8 + b : 40 + b, :CH]
            counts = counts_of(pad[near, 8 + b : 40 + b, CH:])
            for a in (-1, 0, 1):
                j = 3 * (a + 1) + (b + 1)
                weight = kern[j : j + 1, :].reshape(1, 1, CH)
                spread = spread + weight * sums[1 + a : 1 + a + lats]
                density = density + weight * counts[1 + a : 1 + a + lats]
        share = 1.0 / (1.0 + density)
        value = spread * share
        here = pl.ds(lats * i, lats)
        inv[here] = share
        enc32[here] = value
        enc[aligned(i, lats * SIDE), :] = value.reshape(lats * SIDE, CH).astype(bf16)
        return carry

    lax.fori_loop(0, SIDE // lats, encode, 0)
    for copy in halo_copies:
        copy.wait_send()
    for source, k in ((packed, 0), (tags_out, 1)):
        pltpu.make_async_copy(source.at[others], source.at[others], sems.at[k]).wait()

    give, keep = lands.at[:, :HALF], lands.at[:, HALF : 2 * HALF]
    g = lands.at[:, 2 * HALF : 2 * HALF + WIDTH]
    bufs = (core_in, core_sum, in0, in1, out0)
    outs = (o_down, o_up, o_in)
    streams = [
        Stream(k, at, give, keep, outs, bufs, send_sem, recv_sem) for k in range(len(STREAMS))
    ]
    core = at["core"]

    def forward(i, carry):
        rows = aligned(i, block)
        h = jnp.dot(enc[rows, :], w_in[...], preferred_element_type=f32)
        h0[rows, :] = h
        r = lax.rsqrt(jnp.mean(h * h, axis=-1, keepdims=True) + 1e-06)
        rinv[rows, :] = jnp.broadcast_to(r, (block, CH))
        u_here = (h * r * gain[...]).astype(bf16)
        u[rows, :] = u_here
        for n in range(WIDTH // block):
            cols = slice(n * block, (n + 1) * block)
            act = jnp.dot(u_here, w_up[:, cols], preferred_element_type=f32)
            square = act * act
            tanh = jnp.tanh(TANH_SCALE * act * (1.0 + CUBIC * square))
            cdf = 0.5 + 0.5 * tanh
            slope = cdf + act * (0.5 - 0.5 * tanh * tanh) * (
                TANH_SCALE + (3.0 * CUBIC * TANH_SCALE) * square
            )
            g[rows, cols] = (act * cdf).astype(bf16)
            dact[rows, cols] = (slope * back[rows, cols]).astype(bf16)
        return carry

    lax.fori_loop(0, CELLS // block, forward, 0)

    def weight_grad(left, right_side, into, part, first):
        cols_in = aligned(part, 512)

        def body(i, carry):
            cols = aligned(i, 512)
            into[cols, first : first + 512] = tn_dot(left[:, cols], right_side[:, cols_in]).astype(
                bf16
            )
            return carry

        lax.fori_loop(0, WIDTH // 512, body, 0)

    gain_sum[...] = jnp.zeros_like(gain_sum)

    def backward(i, carry):
        rows = pl.ds(i * block, block)
        du = nt_dot(dact[rows, :], w_up[...])
        h = h0[rows, :]
        r = rinv[rows, :1]
        gain_sum[...] += jnp.sum(du * h * r, axis=0, keepdims=True)
        scaled = du * gain[...]
        mean = jnp.mean(scaled * h, axis=-1, keepdims=True)
        dh = (r * scaled - h * (r * r * r * mean) + dyb[rows, :].astype(f32)).astype(bf16)
        u[rows, :] = dh
        denc = nt_dot(dh, w_in[...])
        eight = pl.ds(i * 8, 8)
        ds[eight] = denc.reshape(8, SIDE, CH) * inv[eight]
        return carry

    def in_grad(i, carry):
        cols = aligned(i, block)
        part = tn_dot(enc[...], u[:, cols]).T
        give[cols, 1024:] = jnp.where(core == 1, part, 0.0).astype(bf16)
        keep[cols, 1024:] = jnp.where(core == 0, part, 0.0).astype(bf16)
        return carry

    def filter_grad(i, totals):
        near, here = pl.ds(lats * i, lats + 2), pl.ds(lats * i, lats)
        slope = ds[here]
        dz[pl.ds(lats * i + 2, lats), 16:48] = slope
        both = slope * enc32[here]
        new = list(totals)
        for b in (-1, 0, 1):
            sums = pad[near, 8 + b : 40 + b, :CH]
            counts = counts_of(pad[near, 8 + b : 40 + b, CH:])
            for a in (-1, 0, 1):
                j = 3 * (a + 1) + (b + 1)
                part = slope * sums[1 + a : 1 + a + lats] - both * counts[1 + a : 1 + a + lats]
                new[j] = new[j] + jnp.sum(part.reshape(lats * 4, 8, CH), axis=0)
        return tuple(new)

    def spread_back(i, carry):
        value = jnp.zeros((2, 48, CH), f32)
        for b in (-1, 0, 1):
            slab = dz[pl.ds(2 * i, 4), 8 - b : 56 - b, :]
            for a in (-1, 0, 1):
                j = 3 * (a + 1) + (b + 1)
                value = value + kern[j : j + 1, :].reshape(1, 1, CH) * slab[1 - a : 3 - a]
        kinds = pad[pl.ds(2 * i, 2), :, CH:]
        rows = aligned(i, 96)
        for part, k in ((value, 0), (kinds, 1)):
            part = part.reshape(96, CH)
            top = part.astype(bf16)
            two[k, rows, :CH] = top
            two[k, rows, CH:] = (part - top.astype(f32)).astype(bf16)
        return carry

    def forecast(i):
        rows = pl.ds(i * half, half)
        y = h0[rows, :] + jnp.dot(g[rows, :], w_down[...], preferred_element_type=f32)
        dact[rows, :] = y.astype(bf16)

    totals = {}

    def take_filter():
        zeros = jnp.zeros((8, CH), f32)
        totals["filter"] = lax.fori_loop(0, SIDE // lats, filter_grad, (zeros,) * 9)

    def take_small():
        lax.fori_loop(0, 17, spread_back, 0)
        quarters = tn_dot(two[1], two[0])
        bias_sum = (quarters[:16, :CH] + quarters[:16, CH:]) + (
            quarters[CH : CH + 16, :CH] + quarters[CH : CH + 16, CH:]
        )
        totals["small"] = jnp.concatenate(
            [gain_sum[:, k * CH : (k + 1) * CH] for k in range(8)]
            + [jnp.sum(part, axis=0, keepdims=True) for part in totals["filter"]]
            + [jnp.zeros((7, CH), f32), bias_sum],
            axis=0,
        )

    all_small, small_levels = [], ("x", "y", "z", "core")

    def pass_small():
        level = totals.get("level", 0)
        if level:
            total = small_total(small_levels[level - 1], level - 1, boxes, totals["copies"])
        else:
            total = totals["small"]
        if level == 4:
            o_small[...] = total
            return
        totals["copies"] = small_reduce(
            at, small_levels[level], level, total, boxes, small_send, small_recv
        )
        all_small.extend(totals["copies"])
        totals["level"] = level + 1

    stores = []

    def store(source, landing):
        stores.append(pltpu.make_async_copy(source, landing, load_sem.at[4 + len(stores)]))
        stores[-1].start()

    def last_forecast():
        forecast(1)
        store(dact, y_hbm)

    tasks = {
        "gd0": lambda: weight_grad(g, dyb, give, 1 - core, 0),
        "gd1": lambda: weight_grad(g, dyb, keep, core, 0),
        "gu0": lambda: weight_grad(u, dact, give, 1 - core, 512),
        "gu1": lambda: weight_grad(u, dact, keep, core, 512),
        "b0": lambda: backward(0, 0),
        "b1": lambda: backward(1, 0),
        "b2": lambda: backward(2, 0),
        "b3": lambda: backward(3, 0),
        "i": lambda: lax.fori_loop(0, WIDTH // block, in_grad, 0),
        "f": take_filter,
        "t": take_small,
        "s": pass_small,
        "y0": lambda: forecast(0),
        "y1": last_forecast,
    }
    for task in PLAN:
        if task in tasks:
            tasks[task]()
            continue
        streams[task].advance()
        if streams[0].done == 7 and streams[1].done == 7 and task in (0, 1):
            store(o_down, down_hbm)
        if all(streams[k].done == 7 for k in (2, 3, 4)) and task in (2, 3, 4):
            store(o_up, up_hbm)
    store(o_in, in_hbm)
    for s in streams:
        s.finish()
    for copy in all_small:
        copy.wait_send()
    for copy in stores:
        copy.wait()


def step(values, instr, target, cell, bias, kern, gain, w_in, w_up, w_down, cot):
    vmem, hbm = pl.BlockSpec(memory_space=pltpu.VMEM), pl.BlockSpec(memory_space=pl.ANY)
    return pl.pallas_call(
        step_kernel,
        out_shape=(
            jax.ShapeDtypeStruct((CELLS, WIDTH), bf16),
            jax.ShapeDtypeStruct((WIDTH, WIDTH), bf16),
            jax.ShapeDtypeStruct((WIDTH, WIDTH), bf16),
            jax.ShapeDtypeStruct((WIDTH, 2 * CH), bf16),
            jax.ShapeDtypeStruct((40, CH), f32),
        ),
        in_specs=[vmem] * 7 + [hbm] * 4,
        out_specs=[hbm] * 4 + [vmem],
        scratch_shapes=[
            pltpu.VMEM((OBS_HERE, CH), bf16),
            pltpu.VMEM((1, OBS_HERE), jnp.int32),
            pltpu.VMEM((DEVICES, SLOTS, CH), bf16),
            pltpu.VMEM((DEVICES, 1, CH), f32),
            pltpu.VMEM((DEVICES, SLOTS, CH), bf16),
            pltpu.VMEM((DEVICES, 1, CH), f32),
            pltpu.VMEM((CELLS, DEVICES * SLOTS), bf16),
            pltpu.VMEM((DEVICES * SLOTS, 2 * CH), bf16),
            pltpu.VMEM((3, SIDE, CH), f32),
            pltpu.VMEM((34, 48, 2 * CH), f32),
            pltpu.VMEM((2, SIDE, 2 * CH), f32),
            pltpu.VMEM((2, SIDE, 2 * CH), f32),
            pltpu.VMEM((4, 1, 2 * CH), f32),
            pltpu.VMEM((4, 1, 2 * CH), f32),
            pltpu.SemaphoreType.DMA((4,)),
            pltpu.SemaphoreType.DMA((8,)),
            pltpu.SemaphoreType.DMA((8,)),
            pltpu.SemaphoreType.REGULAR,
            pltpu.VMEM((WIDTH, WIDTH), bf16),
            pltpu.VMEM((WIDTH, WIDTH), bf16),
            pltpu.VMEM((WIDTH, 2 * CH), bf16),
            pltpu.VMEM((CELLS, CH), bf16),
            pltpu.VMEM((SIDE, SIDE, CH), f32),
            pltpu.VMEM((SIDE, SIDE, CH), f32),
            pltpu.VMEM((CH, WIDTH), bf16),
            pltpu.VMEM((WIDTH, WIDTH), bf16),
            pltpu.VMEM((WIDTH, WIDTH), bf16),
            pltpu.VMEM((CELLS, WIDTH), bf16),
            pltpu.VMEM((CELLS, WIDTH), f32),
            pltpu.VMEM((CELLS, WIDTH), f32),
            pltpu.VMEM((CELLS, CH), f32),
            pltpu.VMEM((CELLS, WIDTH), bf16),
            pltpu.VMEM((CELLS, WIDTH), bf16),
            pltpu.VMEM((SIDE, SIDE, CH), f32),
            pltpu.VMEM((36, 64, CH), f32),
            pltpu.VMEM((2, 34 * 48, 2 * CH), bf16),
            pltpu.VMEM((1, WIDTH), f32),
            pltpu.VMEM((4, 4, 40, CH), f32),
            pltpu.SemaphoreType.DMA((8,)),
            pltpu.SemaphoreType.DMA((12,)),
            pltpu.SemaphoreType.DMA((12,)),
        ]
        + reduce_scratch(),
        compiler_params=pltpu.CompilerParams(
            collective_id=0, has_side_effects=True, vmem_limit_bytes=62 << 20
        ),
    )(values, instr, target, cell, bias, kern, gain, w_in, w_up, w_down, cot)


def widen_kernel(
    y, down, up, into, small, y_out, down_out, up_out, in_out, gain, kern, bias, *scratch
):
    y_in, down_in, up_in, in_in, down_wide, up_wide, in_wide, sems, out_sems = scratch
    size, parts = 256, 4
    rows = [pl.ds(k * size, size) for k in range(parts)]
    loads = [pltpu.make_async_copy(into, in_in, sems.at[0])]
    for k in range(parts):
        for which, (source, landing) in enumerate(((down, down_in), (up, up_in), (y, y_in))):
            loads.append(
                pltpu.make_async_copy(
                    source.at[rows[k]], landing.at[rows[k]], sems.at[1 + 3 * k + which]
                )
            )
    for load in loads:
        load.start()
    stores = []
    gain[...] = small[:8]
    kern[...] = small[8:17]
    bias[...] = small[24:40]
    loads[0].wait()
    for k in range(parts):
        in_wide[:, k * size : (k + 1) * size] = in_in[rows[k], :CH].astype(f32).T
    stores.append(pltpu.make_async_copy(in_wide, in_out, out_sems.at[0]))
    stores[0].start()
    for k in range(parts):
        for which, (narrow, wide, landing) in enumerate(
            ((down_in, down_wide, down_out), (up_in, up_wide, up_out), (y_in, y_in, y_out))
        ):
            loads[1 + 3 * k + which].wait()
            if which < 2:
                wide[rows[k], :] = narrow[rows[k], :].astype(f32)
            stores.append(
                pltpu.make_async_copy(
                    wide.at[rows[k]], landing.at[rows[k]], out_sems.at[1 + 3 * k + which]
                )
            )
            stores[-1].start()
    for store in stores:
        store.wait()


def widen(y, down, up, into, small):
    vmem, hbm = pl.BlockSpec(memory_space=pltpu.VMEM), pl.BlockSpec(memory_space=pl.ANY)
    return pl.pallas_call(
        widen_kernel,
        out_shape=(
            jax.ShapeDtypeStruct((CELLS, WIDTH), bf16),
            jax.ShapeDtypeStruct((WIDTH, WIDTH), f32),
            jax.ShapeDtypeStruct((WIDTH, WIDTH), f32),
            jax.ShapeDtypeStruct((CH, WIDTH), f32),
            jax.ShapeDtypeStruct((8, CH), f32),
            jax.ShapeDtypeStruct((9, CH), f32),
            jax.ShapeDtypeStruct((16, CH), f32),
        ),
        in_specs=[hbm] * 4 + [vmem],
        out_specs=[hbm] * 4 + [vmem] * 3,
        scratch_shapes=[
            pltpu.VMEM((CELLS, WIDTH), bf16),
            pltpu.VMEM((WIDTH, WIDTH), bf16),
            pltpu.VMEM((WIDTH, WIDTH), bf16),
            pltpu.VMEM((WIDTH, 2 * CH), bf16),
            pltpu.VMEM((WIDTH, WIDTH), f32),
            pltpu.VMEM((WIDTH, WIDTH), f32),
            pltpu.VMEM((CH, WIDTH), f32),
            pltpu.SemaphoreType.DMA((13,)),
            pltpu.SemaphoreType.DMA((13,)),
        ],
        compiler_params=pltpu.CompilerParams(vmem_limit_bytes=60 << 20),
    )(y, down, up, into, small)


def shards(
    obs_values,
    obs_instrument,
    obs_target,
    obs_cell,
    inst_bias,
    kernel,
    w_in,
    norm_gain,
    w_up,
    w_down,
    cotangent,
):
    y, down, up, into, small = step(
        obs_values,
        obs_instrument.reshape(1, OBS_HERE),
        obs_target.reshape(1, OBS_HERE),
        obs_cell.reshape(1, OBS_HERE),
        inst_bias,
        kernel,
        norm_gain.reshape(1, WIDTH),
        w_in,
        w_up,
        w_down,
        cotangent.reshape(CELLS, WIDTH),
    )
    y, down, up, into, gain, filters, bias = widen(y, down, up, into, small)
    return (y.reshape(cotangent.shape), into, up, down, gain.reshape(WIDTH), filters, bias)


def solution(mesh):
    return jax.shard_map(
        shards,
        mesh=mesh,
        in_specs=(
            P(("inst", "tile"), None),
            P(("inst", "tile")),
            P(("inst", "tile"), None),
            P(("inst", "tile")),
            P(),
            P(),
            P(),
            P(),
            P(),
            P(),
            P("tile", "inst", None),
        ),
        out_specs=(P("tile", "inst", None), P(), P(), P(), P(), P(), P()),
        check_vma=False,
    )
```

```python
import functools

import jax
import jax.numpy as jnp
from jax import lax
from jax.experimental import pallas as pl
from jax.experimental.pallas import tpu as pltpu
from jax.sharding import PartitionSpec as P

offsets = [(a, b) for a in (-1, 0, 1) for b in (-1, 0, 1)]
f32, bf16 = jnp.float32, jnp.bfloat16


MESH = pl.DeviceIdType.MESH
HALF = 1152
ROWS = 1024
STREAMS = (
    (0, 256, "x", "yz", 0, 0),
    (256, 256, "y", "zx", 0, 256),
    (512, 256, "z", "xy", 1, 0),
    (768, 128, "x", "yz", 1, 256),
    (896, 128, "y", "zx", 1, 384),
    (1024, 128, "z", "xy", 2, 0),
)


PLAN = (
    "gd0", 0, 1, "gd1", 0, 1, "gu0", 2, 3, 4, "gu1", 2, 3, 4, "b0", "b1", "b2", "b3", "i", 5, 0,
    1, 2, 3, 4, "f", 5, "t", "s", 0, 1, 2, 3, 4, "y0", 5, 0, 1, 2, 3, 4, "s", "y1", 5, 0, 1, 2,
    3, 4, "s", 5, 0, 1, 2, 3, 4, "s", 5, 0, 1, 2, 3, 4, 5, "s", 5,
)


def place():
    inst, tile = lax.axis_index("inst"), lax.axis_index("tile")
    return {"z": inst // 4, "x": inst % 4, "y": tile // 2, "core": tile % 2}


def device_at(at):
    return (at["z"] * 4 + at["x"], at["y"] * 2 + at["core"])


def moved(at, axis, step):
    size = 2 if axis == "core" else 4
    return {**at, axis: lax.rem(at[axis] + step, size)}


def send_to(source, landing, send_sem, recv_sem, to):
    copy = pltpu.make_async_remote_copy(
        src_ref=source,
        dst_ref=landing,
        send_sem=send_sem,
        recv_sem=recv_sem,
        device_id=to,
        device_id_type=MESH,
    )
    copy.start()
    return copy


def aligned(index, size):
    return pl.ds(pl.multiple_of(index * size, size), size)


class Stream:
    def __init__(self, number, at, give, keep, outs, bufs, send_sem, recv_sem):
        first, wide, self.axis, self.plane, output, first_out = STREAMS[number]
        self.cols = pl.ds(first, wide)
        self.at, self.give, self.keep, self.o = at, give, keep, outs[output]
        half = self.o.shape[1] // 2
        self.out_cols = pl.ds(pl.multiple_of(at["core"] * half + first_out, 128), wide)
        self.core_in, self.core_sum, self.axis_in, self.axis_sum, self.next_in, self.last_in = bufs
        self.sends, self.recvs = send_sem.at[number], recv_sem.at[number]
        self.done = 0

    def go(self, source, target, slot, at):
        send_to(source, target, self.sends.at[slot], self.recvs.at[slot], device_at(at))

    def to_axis(self, axis, slot, refs):
        for step in (1, 2, 3):
            peer = moved(self.at, axis, step)
            self.go(*refs(step, peer), slot, peer)

    def arrived(self, slot, ref):
        pltpu.make_async_copy(ref, ref, self.recvs.at[slot]).wait()

    def rows_of(self, count):
        return self.o.at[pl.ds(0, count), self.out_cols]

    def my_rows(self, size):
        start = self.at[self.axis] * 256
        if size == 64:
            start = start + self.at[self.plane[0]] * 64
        return pl.ds(pl.multiple_of(start, size), size)

    def step0(self):
        other = moved(self.at, "core", 1)
        self.go(self.give.at[:, self.cols], self.core_in.at[:, self.cols], 0, other)

    def step1(self):
        self.arrived(0, self.core_in.at[:, self.cols])
        for step in (1, 2, 3, 0):
            peer = moved(self.at, self.axis, step)
            rows = aligned(peer[self.axis], 256)
            total = self.keep[rows, self.cols].astype(f32) + self.core_in[rows, self.cols].astype(f32)
            self.core_sum[rows, self.cols] = total.astype(bf16)
            if step:
                landing = self.axis_in.at[step - 1, :, self.cols]
                self.go(self.core_sum.at[rows, self.cols], landing, 1, peer)

    def step2(self):
        self.arrived(1, self.axis_in.at[:, :, self.cols])
        for step in (1, 2, 3, 0):
            peer = moved(self.at, self.plane[0], step)
            part = peer[self.plane[0]]
            rows = aligned(part, 64)
            own = pl.ds(pl.multiple_of(self.at[self.axis] * 256 + part * 64, 64), 64)
            total = self.core_sum[own, self.cols].astype(f32)
            for j in range(3):
                total = total + self.axis_in[j, rows, self.cols].astype(f32)
            self.axis_sum[rows, self.cols] = total.astype(bf16)
            if step:
                landing = self.next_in.at[step - 1, :, self.cols]
                self.go(self.axis_sum.at[rows, self.cols], landing, 2, peer)

    def step3(self):
        self.arrived(2, self.next_in.at[:, :, self.cols])
        total = self.axis_sum[aligned(self.at[self.plane[0]], 64), self.cols].astype(f32)
        for j in range(3):
            total = total + self.next_in[j, :, self.cols].astype(f32)
        mine = self.at[self.plane[1]]
        self.last_in[mine, :, self.cols] = total.astype(bf16)
        part = self.last_in.at[mine, :, self.cols]
        self.to_axis(self.plane[1], 3, lambda step, peer: (part, part))

    def step4(self):
        self.arrived(3, self.rows_of(192))
        total = self.last_in[0, :, self.cols].astype(f32)
        for j in range(1, 4):
            total = total + self.last_in[j, :, self.cols].astype(f32)
        self.o[self.my_rows(64), self.out_cols] = total.astype(bf16)
        part = self.o.at[self.my_rows(64), self.out_cols]
        self.to_axis(self.plane[0], 4, lambda step, peer: (part, part))

    def step5(self):
        self.arrived(4, self.rows_of(192))
        part = self.o.at[self.my_rows(256), self.out_cols]
        self.to_axis(self.axis, 5, lambda step, peer: (part, part))

    def step6(self):
        self.arrived(5, self.rows_of(768))
        part = self.o.at[:, self.out_cols]
        self.go(part, part, 6, moved(self.at, "core", 1))

    def step7(self):
        self.arrived(6, self.rows_of(ROWS))

    def advance(self):
        getattr(self, "step" + str(self.done))()
        self.done += 1

    def finish(self):
        for slot, rows in enumerate((ROWS, 768, 192, 192, 192, 768, ROWS)):
            ref = self.rows_of(rows)
            pltpu.make_async_copy(ref, ref, self.sends.at[slot]).wait()


def reduce_scratch():
    return [
        pltpu.VMEM((ROWS, HALF), bf16),
        pltpu.VMEM((ROWS, HALF), bf16),
        pltpu.VMEM((3, 256, HALF), bf16),
        pltpu.VMEM((256, HALF), bf16),
        pltpu.VMEM((3, 64, HALF), bf16),
        pltpu.VMEM((4, 64, HALF), bf16),
        pltpu.SemaphoreType.DMA((len(STREAMS), 7)),
        pltpu.SemaphoreType.DMA((len(STREAMS), 7)),
    ]


DEVICES, SLOTS, CH = 128, 32, 128
SIDE = 32
OBS_HERE = 2048


def iota(shape, axis):
    return lax.broadcasted_iota(jnp.int32, shape, axis)


def nt_dot(left, right):
    return lax.dot_general(left, right, (((1,), (1,)), ((), ())), preferred_element_type=f32)


def tn_dot(left, right):
    return lax.dot_general(left, right, (((0,), (0,)), ((), ())), preferred_element_type=f32)


WIDTH = 1024
CELLS = SIDE * SIDE
TANH_SCALE = 0.7978845608028654
CUBIC = 0.044715
SCALE = 1.0 / (CELLS * DEVICES) ** 0.5


def small_reduce(at, axis, level, mine, boxes, send_sem, recv_sem):
    size = 2 if axis == "core" else 4
    boxes[level, at[axis]] = mine
    copies = []
    for step in range(1, size):
        box = boxes.at[level, at[axis]]
        k = 3 * level + step - 1
        copies.append(
            send_to(box, box, send_sem.at[k], recv_sem.at[k], device_at(moved(at, axis, step)))
        )
    return copies


def small_total(axis, level, boxes, copies):
    for copy in copies:
        copy.wait_recv()
    total = boxes[level, 0]
    for k in range(1, 2 if axis == "core" else 4):
        total = total + boxes[level, k]
    return total


def counts_of(kinds):
    shape = kinds.shape
    flat = kinds.reshape(-1, CH)
    lane = iota(flat.shape, 1)
    return jnp.where(lane < 16, pltpu.roll(flat, CH // 2, 1), flat).reshape(shape)


def step_kernel(
    values,
    instr,
    target,
    cell,
    bias,
    kern,
    gain,
    w_in_hbm,
    w_up_hbm,
    w_down_hbm,
    cot_hbm,
    y_hbm,
    down_hbm,
    up_hbm,
    in_hbm,
    o_small,
    feat,
    places,
    packed,
    tags_out,
    tags_in,
    lands,
    right,
    spots,
    pad,
    side_out,
    side_in,
    corner_out,
    corner_in,
    sems,
    halo_send,
    halo_recv,
    rows_in,
    o_down,
    o_up,
    o_in,
    enc,
    enc32,
    inv,
    w_in,
    w_up,
    w_down,
    dyb,
    back,
    h0,
    rinv,
    u,
    dact,
    ds,
    dz,
    two,
    gain_sum,
    boxes,
    load_sem,
    small_send,
    small_recv,
    core_in,
    core_sum,
    axis_in,
    axis_sum,
    next_in,
    last_in,
    send_sem,
    recv_sem,
):
    at = place()
    inst, tile = lax.axis_index("inst"), lax.axis_index("tile")
    me = inst * 8 + tile
    barrier = pltpu.get_barrier_semaphore()
    loads = [
        pltpu.make_async_copy(source, landing, load_sem.at[k])
        for k, (source, landing) in enumerate(
            ((cot_hbm, dyb), (w_down_hbm, w_down), (w_in_hbm, w_in), (w_up_hbm, w_up))
        )
    ]
    for load in loads:
        load.start()

    def greet_row(i, carry):
        peer = (inst, lax.rem(tile + i, 8))
        pl.semaphore_signal(barrier, inc=1, device_id=peer, device_id_type=MESH)
        return carry

    def greet_column(i, carry):
        peer = (lax.rem(inst + i, 16), tile)
        pl.semaphore_signal(barrier, inc=1, device_id=peer, device_id_type=MESH)
        return carry

    def tell_column(i, carry):
        peer = (lax.rem(inst + i, 16), tile)
        pl.semaphore_signal(rows_in, inc=1, device_id=peer, device_id_type=MESH)
        return carry

    lax.fori_loop(1, 8, greet_row, 0)
    lax.fori_loop(1, 16, greet_column, 0)

    def clear(p, carry):
        pad[p] = jnp.zeros((48, 2 * CH), f32)
        dz[p] = jnp.zeros((64, CH), f32)
        return carry

    lax.fori_loop(0, 34, clear, 0)
    for k in (34, 35):
        dz[k] = jnp.zeros((64, CH), f32)

    block = 256
    upper = (iota((block, block), 0) < iota((block, block), 1)).astype(bf16)
    ahead = jnp.zeros((DEVICES, 1), f32)
    tags = jnp.zeros((DEVICES, CH), f32)
    for b in range(OBS_HERE // block):
        cols = slice(b * block, (b + 1) * block)
        to = target[:, cols]
        hit = (to == iota((DEVICES, block), 0)).astype(f32)
        hit16 = hit.astype(bf16)
        before = jnp.dot(hit16, upper, preferred_element_type=f32) + ahead
        slot = jnp.sum(hit * before, axis=0, keepdims=True)
        ahead = ahead + jnp.sum(hit, axis=1, keepdims=True)
        slot = slot.astype(jnp.int32)
        places[:, cols] = to * SLOTS + slot
        mine = (slot == iota((SLOTS, block), 0)).astype(f32)
        where = cell[:, cols]
        notes = jnp.concatenate(
            [
                mine * (where // SIDE + 1).astype(f32),
                mine * (where % SIDE + 1).astype(f32),
                mine * (instr[:, cols] + 1).astype(f32),
                jnp.zeros((SLOTS, block), f32),
            ],
            axis=0,
        ).astype(bf16)
        tags = tags + nt_dot(hit16, notes)
    for t in range(DEVICES):
        tags_out[t] = tags[t : t + 1, :]

    pl.semaphore_wait(barrier, 22)
    lax.fori_loop(1, 16, tell_column, 0)

    hi = bias[...].astype(bf16)
    rest_part = bias[...] - hi.astype(f32)
    mid = rest_part.astype(bf16)
    low = (rest_part - mid.astype(f32)).astype(bf16)
    bias3 = jnp.concatenate([hi, mid, low], axis=0)
    for b in range(OBS_HERE // block):
        cols = slice(b * block, (b + 1) * block)
        pick = (instr[:, cols] == iota((16, block), 0)).astype(f32)
        pick3 = jnp.concatenate([pick, pick, pick], axis=0).T.astype(bf16)
        offset = jnp.dot(pick3, bias3, preferred_element_type=f32)
        feat[cols, :] = (values[cols, :].astype(f32) + offset).astype(bf16)

    pl.semaphore_wait(rows_in, 15)

    my_place = pl.ds(pl.multiple_of(lax.rem(me, SIDE) * CH + me // SIDE * SLOTS, SLOTS), SLOTS)

    def send_slot(source, landing, k, to_inst, to_tile):
        t = to_inst * 8 + to_tile
        pltpu.make_async_remote_copy(
            src_ref=source.at[t],
            dst_ref=landing,
            send_sem=sems.at[k],
            recv_sem=sems.at[2 + k],
            device_id=(to_inst, to_tile),
            device_id_type=MESH,
        ).start()

    def send_tags(i, carry):
        peer = lax.rem(me + i * 37, DEVICES)
        send_slot(tags_out, tags_in.at[me], 1, peer // 8, lax.rem(peer, 8))
        return carry

    group = 8 * SLOTS

    def pack_and_send(i, carry):
        turn = lax.rem(i * 7, 16)
        to_inst = lax.rem(at["z"] + turn // 4, 4) * 4 + lax.rem(at["x"] + lax.rem(turn, 4), 4)
        spot = jnp.clip(places[...] - to_inst * group, -1, group).astype(f32).astype(bf16)
        number = iota((group, OBS_HERE), 0).astype(f32).astype(bf16)
        choose = jnp.where(spot == number, jnp.bfloat16(1), jnp.bfloat16(0))
        rows = jnp.dot(choose, feat[...], preferred_element_type=f32).astype(bf16)
        packed[pl.ds(pl.multiple_of(to_inst * 8, 8), 8)] = rows.reshape(8, SLOTS, CH)

        def send_one(j, inner_carry):
            to_tile = lax.rem(tile + j * 3, 8)

            @pl.when(to_inst * 8 + to_tile != me)
            def _():
                send_slot(packed, right.at[my_place, :CH], 0, to_inst, to_tile)

            return inner_carry

        lax.fori_loop(0, 8, send_one, 0)
        lax.fori_loop(
            jnp.minimum((i - 1) * 16 + 1, DEVICES), jnp.minimum(i * 16 + 1, DEVICES), send_tags, 0
        )
        return carry

    lax.fori_loop(1, 17, pack_and_send, 0)
    right[my_place, :CH] = packed[me]
    tags_in[me] = tags_out[me]
    others = pl.ds(0, DEVICES - 1)
    pltpu.make_async_copy(tags_in.at[others], tags_in.at[others], sems.at[3]).wait()
    every = tags_in[...].reshape(DEVICES, CH)
    for k in range(3):
        spots[k] = jnp.concatenate(
            [every[SIDE * m : SIDE * (m + 1), 32 * k : 32 * (k + 1)] for m in range(4)], axis=1
        )

    def place_group(g, carry):
        row = pl.ds(g, 1)
        lat, lon, kind = (spots[k, row, :] for k in range(3))
        number = iota((SIDE, CH), 0).astype(f32) + 1.0
        at_lon = (lon == number).astype(f32)
        cols = aligned(g, CH)
        for p in range(SIDE):
            lands[p * SIDE : (p + 1) * SIDE, cols] = jnp.where(
                lat == float(p + 1), at_lon, 0.0
            ).astype(bf16)
        which = iota((CH, CH), 0)
        kinds = jnp.where(
            which < 16, (kind == which.astype(f32) + 1.0).astype(f32), (kind > 0.0).astype(f32)
        )
        right[cols, CH:] = kinds.T.astype(bf16)
        return carry

    lax.fori_loop(0, SIDE, place_group, 0)

    half = CELLS // 2

    def go_back(i):
        rows = pl.ds(i * half, half)
        dy_here = (dyb[rows, :].astype(f32) * SCALE).astype(bf16)
        dyb[rows, :] = dy_here
        back[rows, :] = nt_dot(dy_here, w_down[...])

    loads[0].wait()
    loads[1].wait()
    go_back(0)
    landed = right.at[pl.ds(0, (DEVICES - 1) * SLOTS), :CH]
    pltpu.make_async_copy(landed, landed, sems.at[2]).wait()

    def sum_block(i, carry):
        total = jnp.dot(lands[aligned(i, half), :], right[...], preferred_element_type=f32)
        pad[pl.ds(1 + 16 * i, 16), 8:40, :] = total.reshape(16, SIDE, 2 * CH)
        return carry

    lax.fori_loop(0, 2, sum_block, 0)

    for p in range(SIDE):
        side_out[0, p : p + 1, :] = pad[1 + p, 8:9, :]
        side_out[1, p : p + 1, :] = pad[1 + p, 39:40, :]
    for k, (p, q) in enumerate(((1, 8), (1, 39), (32, 8), (32, 39))):
        corner_out[k] = pad[p, q : q + 1, :]
    north, south = lax.rem(tile + 7, 8), lax.rem(tile + 1, 8)
    west, east = lax.rem(inst + 15, 16), lax.rem(inst + 1, 16)
    halo = (
        (pad.at[1, 8:40], pad.at[33, 8:40], (inst, north)),
        (pad.at[32, 8:40], pad.at[0, 8:40], (inst, south)),
        (side_out.at[0], side_in.at[1], (west, tile)),
        (side_out.at[1], side_in.at[0], (east, tile)),
        (corner_out.at[0], corner_in.at[3], (west, north)),
        (corner_out.at[1], corner_in.at[2], (east, north)),
        (corner_out.at[2], corner_in.at[1], (west, south)),
        (corner_out.at[3], corner_in.at[0], (east, south)),
    )
    halo_copies = [
        send_to(source, landing, halo_send.at[k], halo_recv.at[k], to)
        for k, (source, landing, to) in enumerate(halo)
    ]
    go_back(1)
    for load in loads[2:]:
        load.wait()
    for copy in halo_copies:
        copy.wait_recv()
    keep_north = (tile > 0).astype(f32)
    keep_south = (tile < 7).astype(f32)
    keep_west = (inst > 0).astype(f32)
    keep_east = (inst < 15).astype(f32)
    pad[0, 8:40, :] = pad[0, 8:40, :] * keep_north
    pad[33, 8:40, :] = pad[33, 8:40, :] * keep_south
    for p in range(SIDE):
        pad[1 + p, 7:8, :] = side_in[0, p : p + 1, :] * keep_west
        pad[1 + p, 40:41, :] = side_in[1, p : p + 1, :] * keep_east
    pad[0, 7:8, :] = corner_in[0] * (keep_north * keep_west)
    pad[0, 40:41, :] = corner_in[1] * (keep_north * keep_east)
    pad[33, 7:8, :] = corner_in[2] * (keep_south * keep_west)
    pad[33, 40:41, :] = corner_in[3] * (keep_south * keep_east)

    lats = 4

    def encode(i, carry):
        spread = jnp.zeros((lats, SIDE, CH), f32)
        density = jnp.zeros((lats, SIDE, CH), f32)
        near = pl.ds(lats * i, lats + 2)
        for b in (-1, 0, 1):
            sums = pad[near, 8 + b : 40 + b, :CH]
            counts = counts_of(pad[near, 8 + b : 40 + b, CH:])
            for a in (-1, 0, 1):
                j = 3 * (a + 1) + (b + 1)
                weight = kern[j : j + 1, :].reshape(1, 1, CH)
                spread = spread + weight * sums[1 + a : 1 + a + lats]
                density = density + weight * counts[1 + a : 1 + a + lats]
        share = 1.0 / (1.0 + density)
        value = spread * share
        here = pl.ds(lats * i, lats)
        inv[here] = share
        enc32[here] = value
        enc[aligned(i, lats * SIDE), :] = value.reshape(lats * SIDE, CH).astype(bf16)
        return carry

    lax.fori_loop(0, SIDE // lats, encode, 0)
    for copy in halo_copies:
        copy.wait_send()
    for source, k in ((packed, 0), (tags_out, 1)):
        pltpu.make_async_copy(source.at[others], source.at[others], sems.at[k]).wait()

    give, keep = lands.at[:, :HALF], lands.at[:, HALF : 2 * HALF]
    g = lands.at[:, 2 * HALF : 2 * HALF + WIDTH]
    bufs = (core_in, core_sum, axis_in, axis_sum, next_in, last_in)
    outs = (o_down, o_up, o_in)
    streams = [
        Stream(k, at, give, keep, outs, bufs, send_sem, recv_sem) for k in range(len(STREAMS))
    ]
    core = at["core"]

    def forward(i, carry):
        rows = aligned(i, block)
        h = jnp.dot(enc[rows, :], w_in[...], preferred_element_type=f32)
        h0[rows, :] = h
        r = lax.rsqrt(jnp.mean(h * h, axis=-1, keepdims=True) + 1e-06)
        rinv[rows, :] = jnp.broadcast_to(r, (block, CH))
        u_here = (h * r * gain[...]).astype(bf16)
        u[rows, :] = u_here
        for n in range(WIDTH // block):
            cols = slice(n * block, (n + 1) * block)
            act = jnp.dot(u_here, w_up[:, cols], preferred_element_type=f32)
            square = act * act
            tanh = jnp.tanh(TANH_SCALE * act * (1.0 + CUBIC * square))
            cdf = 0.5 + 0.5 * tanh
            slope = cdf + act * (0.5 - 0.5 * tanh * tanh) * (
                TANH_SCALE + (3.0 * CUBIC * TANH_SCALE) * square
            )
            g[rows, cols] = (act * cdf).astype(bf16)
            dact[rows, cols] = (slope * back[rows, cols]).astype(bf16)
        return carry

    lax.fori_loop(0, CELLS // block, forward, 0)

    def weight_grad(left, right_side, into, part, first):
        cols_in = aligned(part, 512)

        def body(i, carry):
            cols = aligned(i, 512)
            into[cols, first : first + 512] = tn_dot(left[:, cols], right_side[:, cols_in]).astype(
                bf16
            )
            return carry

        lax.fori_loop(0, WIDTH // 512, body, 0)

    gain_sum[...] = jnp.zeros_like(gain_sum)

    def backward(i, carry):
        rows = pl.ds(i * block, block)
        du = nt_dot(dact[rows, :], w_up[...])
        h = h0[rows, :]
        r = rinv[rows, :1]
        gain_sum[...] += jnp.sum(du * h * r, axis=0, keepdims=True)
        scaled = du * gain[...]
        mean = jnp.mean(scaled * h, axis=-1, keepdims=True)
        dh = (r * scaled - h * (r * r * r * mean) + dyb[rows, :].astype(f32)).astype(bf16)
        u[rows, :] = dh
        denc = nt_dot(dh, w_in[...])
        eight = pl.ds(i * 8, 8)
        ds[eight] = denc.reshape(8, SIDE, CH) * inv[eight]
        return carry

    def in_grad(i, carry):
        cols = aligned(i, block)
        part = tn_dot(enc[...], u[:, cols]).T
        give[cols, 1024:] = jnp.where(core == 1, part, 0.0).astype(bf16)
        keep[cols, 1024:] = jnp.where(core == 0, part, 0.0).astype(bf16)
        return carry

    def filter_grad(i, totals):
        near, here = pl.ds(lats * i, lats + 2), pl.ds(lats * i, lats)
        slope = ds[here]
        dz[pl.ds(lats * i + 2, lats), 16:48] = slope
        both = slope * enc32[here]
        new = list(totals)
        for b in (-1, 0, 1):
            sums = pad[near, 8 + b : 40 + b, :CH]
            counts = counts_of(pad[near, 8 + b : 40 + b, CH:])
            for a in (-1, 0, 1):
                j = 3 * (a + 1) + (b + 1)
                part = slope * sums[1 + a : 1 + a + lats] - both * counts[1 + a : 1 + a + lats]
                new[j] = new[j] + jnp.sum(part.reshape(lats * 4, 8, CH), axis=0)
        return tuple(new)

    def spread_back(i, carry):
        value = jnp.zeros((2, 48, CH), f32)
        for b in (-1, 0, 1):
            slab = dz[pl.ds(2 * i, 4), 8 - b : 56 - b, :]
            for a in (-1, 0, 1):
                j = 3 * (a + 1) + (b + 1)
                value = value + kern[j : j + 1, :].reshape(1, 1, CH) * slab[1 - a : 3 - a]
        kinds = pad[pl.ds(2 * i, 2), :, CH:]
        rows = aligned(i, 96)
        for part, k in ((value, 0), (kinds, 1)):
            part = part.reshape(96, CH)
            top = part.astype(bf16)
            two[k, rows, :CH] = top
            two[k, rows, CH:] = (part - top.astype(f32)).astype(bf16)
        return carry

    def forecast(i):
        rows = pl.ds(i * half, half)
        y = h0[rows, :] + jnp.dot(g[rows, :], w_down[...], preferred_element_type=f32)
        dact[rows, :] = y.astype(bf16)

    totals = {}

    def take_filter():
        zeros = jnp.zeros((8, CH), f32)
        totals["filter"] = lax.fori_loop(0, SIDE // lats, filter_grad, (zeros,) * 9)

    def take_small():
        lax.fori_loop(0, 17, spread_back, 0)
        quarters = tn_dot(two[1], two[0])
        bias_sum = (quarters[:16, :CH] + quarters[:16, CH:]) + (
            quarters[CH : CH + 16, :CH] + quarters[CH : CH + 16, CH:]
        )
        totals["small"] = jnp.concatenate(
            [gain_sum[:, k * CH : (k + 1) * CH] for k in range(8)]
            + [jnp.sum(part, axis=0, keepdims=True) for part in totals["filter"]]
            + [jnp.zeros((7, CH), f32), bias_sum],
            axis=0,
        )

    all_small, small_levels = [], ("x", "y", "z", "core")

    def pass_small():
        level = totals.get("level", 0)
        if level:
            total = small_total(small_levels[level - 1], level - 1, boxes, totals["copies"])
        else:
            total = totals["small"]
        if level == 4:
            o_small[...] = total
            return
        totals["copies"] = small_reduce(
            at, small_levels[level], level, total, boxes, small_send, small_recv
        )
        all_small.extend(totals["copies"])
        totals["level"] = level + 1

    stores = []

    def store(source, landing):
        stores.append(pltpu.make_async_copy(source, landing, load_sem.at[4 + len(stores)]))
        stores[-1].start()

    def last_forecast():
        forecast(1)
        store(dact, y_hbm)

    tasks = {
        "gd0": lambda: weight_grad(g, dyb, give, 1 - core, 0),
        "gd1": lambda: weight_grad(g, dyb, keep, core, 0),
        "gu0": lambda: weight_grad(u, dact, give, 1 - core, 512),
        "gu1": lambda: weight_grad(u, dact, keep, core, 512),
        "b0": lambda: backward(0, 0),
        "b1": lambda: backward(1, 0),
        "b2": lambda: backward(2, 0),
        "b3": lambda: backward(3, 0),
        "i": lambda: lax.fori_loop(0, WIDTH // block, in_grad, 0),
        "f": take_filter,
        "t": take_small,
        "s": pass_small,
        "y0": lambda: forecast(0),
        "y1": last_forecast,
    }
    for task in PLAN:
        if task in tasks:
            tasks[task]()
            continue
        streams[task].advance()
        if streams[0].done == 8 and streams[1].done == 8 and task in (0, 1):
            store(o_down, down_hbm)
        if all(streams[k].done == 8 for k in (2, 3, 4)) and task in (2, 3, 4):
            store(o_up, up_hbm)
    store(o_in, in_hbm)
    for s in streams:
        s.finish()
    for copy in all_small:
        copy.wait_send()
    for copy in stores:
        copy.wait()


def step(values, instr, target, cell, bias, kern, gain, w_in, w_up, w_down, cot):
    vmem, hbm = pl.BlockSpec(memory_space=pltpu.VMEM), pl.BlockSpec(memory_space=pl.ANY)
    return pl.pallas_call(
        step_kernel,
        out_shape=(
            jax.ShapeDtypeStruct((CELLS, WIDTH), bf16),
            jax.ShapeDtypeStruct((WIDTH, WIDTH), bf16),
            jax.ShapeDtypeStruct((WIDTH, WIDTH), bf16),
            jax.ShapeDtypeStruct((WIDTH, 2 * CH), bf16),
            jax.ShapeDtypeStruct((40, CH), f32),
        ),
        in_specs=[vmem] * 7 + [hbm] * 4,
        out_specs=[hbm] * 4 + [vmem],
        scratch_shapes=[
            pltpu.VMEM((OBS_HERE, CH), bf16),
            pltpu.VMEM((1, OBS_HERE), jnp.int32),
            pltpu.VMEM((DEVICES, SLOTS, CH), bf16),
            pltpu.VMEM((DEVICES, 1, CH), f32),
            pltpu.VMEM((DEVICES, 1, CH), f32),
            pltpu.VMEM((CELLS, DEVICES * SLOTS), bf16),
            pltpu.VMEM((DEVICES * SLOTS, 2 * CH), bf16),
            pltpu.VMEM((3, SIDE, CH), f32),
            pltpu.VMEM((34, 48, 2 * CH), f32),
            pltpu.VMEM((2, SIDE, 2 * CH), f32),
            pltpu.VMEM((2, SIDE, 2 * CH), f32),
            pltpu.VMEM((4, 1, 2 * CH), f32),
            pltpu.VMEM((4, 1, 2 * CH), f32),
            pltpu.SemaphoreType.DMA((4,)),
            pltpu.SemaphoreType.DMA((8,)),
            pltpu.SemaphoreType.DMA((8,)),
            pltpu.SemaphoreType.REGULAR,
            pltpu.VMEM((WIDTH, WIDTH), bf16),
            pltpu.VMEM((WIDTH, WIDTH), bf16),
            pltpu.VMEM((WIDTH, 2 * CH), bf16),
            pltpu.VMEM((CELLS, CH), bf16),
            pltpu.VMEM((SIDE, SIDE, CH), f32),
            pltpu.VMEM((SIDE, SIDE, CH), f32),
            pltpu.VMEM((CH, WIDTH), bf16),
            pltpu.VMEM((WIDTH, WIDTH), bf16),
            pltpu.VMEM((WIDTH, WIDTH), bf16),
            pltpu.VMEM((CELLS, WIDTH), bf16),
            pltpu.VMEM((CELLS, WIDTH), f32),
            pltpu.VMEM((CELLS, WIDTH), f32),
            pltpu.VMEM((CELLS, CH), f32),
            pltpu.VMEM((CELLS, WIDTH), bf16),
            pltpu.VMEM((CELLS, WIDTH), bf16),
            pltpu.VMEM((SIDE, SIDE, CH), f32),
            pltpu.VMEM((36, 64, CH), f32),
            pltpu.VMEM((2, 34 * 48, 2 * CH), bf16),
            pltpu.VMEM((1, WIDTH), f32),
            pltpu.VMEM((4, 4, 40, CH), f32),
            pltpu.SemaphoreType.DMA((8,)),
            pltpu.SemaphoreType.DMA((12,)),
            pltpu.SemaphoreType.DMA((12,)),
        ]
        + reduce_scratch(),
        compiler_params=pltpu.CompilerParams(
            collective_id=0, has_side_effects=True, vmem_limit_bytes=62 << 20
        ),
    )(values, instr, target, cell, bias, kern, gain, w_in, w_up, w_down, cot)


def widen_kernel(
    y, down, up, into, small, y_out, down_out, up_out, in_out, gain, kern, bias, *scratch
):
    y_in, down_in, up_in, in_in, down_wide, up_wide, in_wide, sems, out_sems = scratch
    size, parts = 256, 4
    rows = [pl.ds(k * size, size) for k in range(parts)]
    loads = [pltpu.make_async_copy(into, in_in, sems.at[0])]
    for k in range(parts):
        for which, (source, landing) in enumerate(((down, down_in), (up, up_in), (y, y_in))):
            loads.append(
                pltpu.make_async_copy(
                    source.at[rows[k]], landing.at[rows[k]], sems.at[1 + 3 * k + which]
                )
            )
    for load in loads:
        load.start()
    stores = []
    gain[...] = small[:8]
    kern[...] = small[8:17]
    bias[...] = small[24:40]
    loads[0].wait()
    for k in range(parts):
        in_wide[:, k * size : (k + 1) * size] = in_in[rows[k], :CH].astype(f32).T
    stores.append(pltpu.make_async_copy(in_wide, in_out, out_sems.at[0]))
    stores[0].start()
    for k in range(parts):
        for which, (narrow, wide, landing) in enumerate(
            ((down_in, down_wide, down_out), (up_in, up_wide, up_out), (y_in, y_in, y_out))
        ):
            loads[1 + 3 * k + which].wait()
            if which < 2:
                wide[rows[k], :] = narrow[rows[k], :].astype(f32)
            stores.append(
                pltpu.make_async_copy(
                    wide.at[rows[k]], landing.at[rows[k]], out_sems.at[1 + 3 * k + which]
                )
            )
            stores[-1].start()
    for store in stores:
        store.wait()


def widen(y, down, up, into, small):
    vmem, hbm = pl.BlockSpec(memory_space=pltpu.VMEM), pl.BlockSpec(memory_space=pl.ANY)
    return pl.pallas_call(
        widen_kernel,
        out_shape=(
            jax.ShapeDtypeStruct((CELLS, WIDTH), bf16),
            jax.ShapeDtypeStruct((WIDTH, WIDTH), f32),
            jax.ShapeDtypeStruct((WIDTH, WIDTH), f32),
            jax.ShapeDtypeStruct((CH, WIDTH), f32),
            jax.ShapeDtypeStruct((8, CH), f32),
            jax.ShapeDtypeStruct((9, CH), f32),
            jax.ShapeDtypeStruct((16, CH), f32),
        ),
        in_specs=[hbm] * 4 + [vmem],
        out_specs=[hbm] * 4 + [vmem] * 3,
        scratch_shapes=[
            pltpu.VMEM((CELLS, WIDTH), bf16),
            pltpu.VMEM((WIDTH, WIDTH), bf16),
            pltpu.VMEM((WIDTH, WIDTH), bf16),
            pltpu.VMEM((WIDTH, 2 * CH), bf16),
            pltpu.VMEM((WIDTH, WIDTH), f32),
            pltpu.VMEM((WIDTH, WIDTH), f32),
            pltpu.VMEM((CH, WIDTH), f32),
            pltpu.SemaphoreType.DMA((13,)),
            pltpu.SemaphoreType.DMA((13,)),
        ],
        compiler_params=pltpu.CompilerParams(vmem_limit_bytes=60 << 20),
    )(y, down, up, into, small)


def shards(
    obs_values,
    obs_instrument,
    obs_target,
    obs_cell,
    inst_bias,
    kernel,
    w_in,
    norm_gain,
    w_up,
    w_down,
    cotangent,
):
    y, down, up, into, small = step(
        obs_values,
        obs_instrument.reshape(1, OBS_HERE),
        obs_target.reshape(1, OBS_HERE),
        obs_cell.reshape(1, OBS_HERE),
        inst_bias,
        kernel,
        norm_gain.reshape(1, WIDTH),
        w_in,
        w_up,
        w_down,
        cotangent.reshape(CELLS, WIDTH),
    )
    y, down, up, into, gain, filters, bias = widen(y, down, up, into, small)
    return (y.reshape(cotangent.shape), into, up, down, gain.reshape(WIDTH), filters, bias)


def solution(mesh):
    return jax.shard_map(
        shards,
        mesh=mesh,
        in_specs=(
            P(("inst", "tile"), None),
            P(("inst", "tile")),
            P(("inst", "tile"), None),
            P(("inst", "tile")),
            P(),
            P(),
            P(),
            P(),
            P(),
            P(),
            P("tile", "inst", None),
        ),
        out_specs=(P("tile", "inst", None), P(), P(), P(), P(), P(), P()),
        check_vma=False,
    )
```

```python
import functools

import jax
import jax.numpy as jnp
from jax import lax
from jax.experimental import pallas as pl
from jax.experimental.pallas import tpu as pltpu
from jax.sharding import PartitionSpec as P

offsets = [(a, b) for a in (-1, 0, 1) for b in (-1, 0, 1)]
f32, bf16 = jnp.float32, jnp.bfloat16


MESH = pl.DeviceIdType.MESH
HALF = 1152
ROWS = 1024
STREAMS = (
    (0, 256, "x", "yz", 0, 0),
    (256, 256, "y", "zx", 0, 256),
    (512, 256, "z", "xy", 1, 0),
    (768, 128, "x", "yz", 1, 256),
    (896, 128, "y", "zx", 1, 384),
    (1024, 128, "z", "xy", 2, 0),
)


PLAN = (
    "gd0", 0, 1, "gd1", 0, 1, "gu0", 2, 3, 4, "gu1", 2, 3, 4, "b0", "b1", "i", 5, 0,
    1, 2, 3, 4, "f", 5, "t", "s", 0, 1, 2, 3, 4, "y0", 5, 0, 1, 2, 3, 4, "s", "y1", 5, 0, 1, 2,
    3, 4, "s", 5, 0, 1, 2, 3, 4, "s", 5, 0, 1, 2, 3, 4, 5, "s", 5,
)


def place():
    inst, tile = lax.axis_index("inst"), lax.axis_index("tile")
    return {"z": inst // 4, "x": inst % 4, "y": tile // 2, "core": tile % 2}


def device_at(at):
    return (at["z"] * 4 + at["x"], at["y"] * 2 + at["core"])


def moved(at, axis, step):
    size = 2 if axis == "core" else 4
    return {**at, axis: lax.rem(at[axis] + step, size)}


def send_to(source, landing, send_sem, recv_sem, to):
    copy = pltpu.make_async_remote_copy(
        src_ref=source,
        dst_ref=landing,
        send_sem=send_sem,
        recv_sem=recv_sem,
        device_id=to,
        device_id_type=MESH,
    )
    copy.start()
    return copy


def aligned(index, size):
    return pl.ds(pl.multiple_of(index * size, size), size)


class Stream:
    def __init__(self, number, at, give, keep, outs, bufs, send_sem, recv_sem):
        first, wide, self.axis, self.plane, output, first_out = STREAMS[number]
        self.cols = pl.ds(first, wide)
        self.at, self.give, self.keep, self.o = at, give, keep, outs[output]
        half = self.o.shape[1] // 2
        self.out_cols = pl.ds(pl.multiple_of(at["core"] * half + first_out, 128), wide)
        self.core_in, self.core_sum, self.axis_in, self.axis_sum, self.next_in, self.last_in = bufs
        self.sends, self.recvs = send_sem.at[number], recv_sem.at[number]
        self.done = 0

    def go(self, source, target, slot, at):
        send_to(source, target, self.sends.at[slot], self.recvs.at[slot], device_at(at))

    def to_axis(self, axis, slot, refs):
        for step in (1, 2, 3):
            peer = moved(self.at, axis, step)
            self.go(*refs(step, peer), slot, peer)

    def arrived(self, slot, ref):
        pltpu.make_async_copy(ref, ref, self.recvs.at[slot]).wait()

    def rows_of(self, count):
        return self.o.at[pl.ds(0, count), self.out_cols]

    def my_rows(self, size):
        start = self.at[self.axis] * 256
        if size == 64:
            start = start + self.at[self.plane[0]] * 64
        return pl.ds(pl.multiple_of(start, size), size)

    def step0(self):
        other = moved(self.at, "core", 1)
        self.go(self.give.at[:, self.cols], self.core_in.at[:, self.cols], 0, other)

    def step1(self):
        self.arrived(0, self.core_in.at[:, self.cols])
        for step in (1, 2, 3, 0):
            peer = moved(self.at, self.axis, step)
            rows = aligned(peer[self.axis], 256)
            total = self.keep[rows, self.cols].astype(f32) + self.core_in[rows, self.cols].astype(f32)
            self.core_sum[rows, self.cols] = total.astype(bf16)
            if step:
                landing = self.axis_in.at[step - 1, :, self.cols]
                self.go(self.core_sum.at[rows, self.cols], landing, 1, peer)

    def step2(self):
        self.arrived(1, self.axis_in.at[:, :, self.cols])
        for step in (1, 2, 3, 0):
            peer = moved(self.at, self.plane[0], step)
            part = peer[self.plane[0]]
            rows = aligned(part, 64)
            own = pl.ds(pl.multiple_of(self.at[self.axis] * 256 + part * 64, 64), 64)
            total = self.core_sum[own, self.cols].astype(f32)
            for j in range(3):
                total = total + self.axis_in[j, rows, self.cols].astype(f32)
            self.axis_sum[rows, self.cols] = total.astype(bf16)
            if step:
                landing = self.next_in.at[step - 1, :, self.cols]
                self.go(self.axis_sum.at[rows, self.cols], landing, 2, peer)

    def step3(self):
        self.arrived(2, self.next_in.at[:, :, self.cols])
        total = self.axis_sum[aligned(self.at[self.plane[0]], 64), self.cols].astype(f32)
        for j in range(3):
            total = total + self.next_in[j, :, self.cols].astype(f32)
        mine = self.at[self.plane[1]]
        self.last_in[mine, :, self.cols] = total.astype(bf16)
        part = self.last_in.at[mine, :, self.cols]
        self.to_axis(self.plane[1], 3, lambda step, peer: (part, part))

    def step4(self):
        self.arrived(3, self.rows_of(192))
        total = self.last_in[0, :, self.cols].astype(f32)
        for j in range(1, 4):
            total = total + self.last_in[j, :, self.cols].astype(f32)
        self.o[self.my_rows(64), self.out_cols] = total.astype(bf16)
        part = self.o.at[self.my_rows(64), self.out_cols]
        self.to_axis(self.plane[0], 4, lambda step, peer: (part, part))

    def step5(self):
        self.arrived(4, self.rows_of(192))
        part = self.o.at[self.my_rows(256), self.out_cols]
        self.to_axis(self.axis, 5, lambda step, peer: (part, part))

    def step6(self):
        self.arrived(5, self.rows_of(768))
        part = self.o.at[:, self.out_cols]
        self.go(part, part, 6, moved(self.at, "core", 1))

    def step7(self):
        self.arrived(6, self.rows_of(ROWS))

    def advance(self):
        getattr(self, "step" + str(self.done))()
        self.done += 1

    def finish(self):
        for slot, rows in enumerate((ROWS, 768, 192, 192, 192, 768, ROWS)):
            ref = self.rows_of(rows)
            pltpu.make_async_copy(ref, ref, self.sends.at[slot]).wait()


def reduce_scratch():
    return [
        pltpu.VMEM((ROWS, HALF), bf16),
        pltpu.VMEM((ROWS, HALF), bf16),
        pltpu.VMEM((3, 256, HALF), bf16),
        pltpu.VMEM((256, HALF), bf16),
        pltpu.VMEM((3, 64, HALF), bf16),
        pltpu.VMEM((4, 64, HALF), bf16),
        pltpu.SemaphoreType.DMA((len(STREAMS), 7)),
        pltpu.SemaphoreType.DMA((len(STREAMS), 7)),
    ]


DEVICES, SLOTS, CH = 128, 32, 128
SIDE = 32
OBS_HERE = 2048


def iota(shape, axis):
    return lax.broadcasted_iota(jnp.int32, shape, axis)


def nt_dot(left, right):
    return lax.dot_general(left, right, (((1,), (1,)), ((), ())), preferred_element_type=f32)


def tn_dot(left, right):
    return lax.dot_general(left, right, (((0,), (0,)), ((), ())), preferred_element_type=f32)


WIDTH = 1024
CELLS = SIDE * SIDE
TANH_SCALE = 0.7978845608028654
CUBIC = 0.044715
SCALE = 1.0 / (CELLS * DEVICES) ** 0.5


def small_reduce(at, axis, level, mine, boxes, send_sem, recv_sem):
    size = 2 if axis == "core" else 4
    boxes[level, at[axis]] = mine
    copies = []
    for step in range(1, size):
        box = boxes.at[level, at[axis]]
        k = 3 * level + step - 1
        copies.append(
            send_to(box, box, send_sem.at[k], recv_sem.at[k], device_at(moved(at, axis, step)))
        )
    return copies


def small_total(axis, level, boxes, copies):
    for copy in copies:
        copy.wait_recv()
    total = boxes[level, 0]
    for k in range(1, 2 if axis == "core" else 4):
        total = total + boxes[level, k]
    return total


def counts_of(kinds):
    shape = kinds.shape
    flat = kinds.reshape(-1, CH)
    lane = iota(flat.shape, 1)
    return jnp.where(lane < 16, pltpu.roll(flat, CH // 2, 1), flat).reshape(shape)


def step_kernel(
    values,
    instr,
    target,
    cell,
    bias,
    kern,
    gain,
    w_in_hbm,
    w_up_hbm,
    w_down_hbm,
    cot_hbm,
    y_hbm,
    down_hbm,
    up_hbm,
    in_hbm,
    o_small,
    feat,
    places,
    packed,
    tags_out,
    tags_in,
    lands,
    right,
    spots,
    pad,
    side_out,
    side_in,
    corner_out,
    corner_in,
    sems,
    halo_send,
    halo_recv,
    rows_in,
    o_down,
    o_up,
    o_in,
    enc,
    enc32,
    inv,
    w_in,
    w_up,
    w_down,
    dyb,
    back,
    h0,
    rinv,
    u,
    dact,
    ds,
    dz,
    two,
    gain_sum,
    boxes,
    load_sem,
    small_send,
    small_recv,
    core_in,
    core_sum,
    axis_in,
    axis_sum,
    next_in,
    last_in,
    send_sem,
    recv_sem,
):
    at = place()
    inst, tile = lax.axis_index("inst"), lax.axis_index("tile")
    me = inst * 8 + tile
    barrier = pltpu.get_barrier_semaphore()
    loads = [
        pltpu.make_async_copy(source, landing, load_sem.at[k])
        for k, (source, landing) in enumerate(
            ((cot_hbm, dyb), (w_down_hbm, w_down), (w_in_hbm, w_in), (w_up_hbm, w_up))
        )
    ]
    for load in loads:
        load.start()

    def greet_row(i, carry):
        peer = (inst, lax.rem(tile + i, 8))
        pl.semaphore_signal(barrier, inc=1, device_id=peer, device_id_type=MESH)
        return carry

    def greet_column(i, carry):
        peer = (lax.rem(inst + i, 16), tile)
        pl.semaphore_signal(barrier, inc=1, device_id=peer, device_id_type=MESH)
        return carry

    def tell_column(i, carry):
        peer = (lax.rem(inst + i, 16), tile)
        pl.semaphore_signal(rows_in, inc=1, device_id=peer, device_id_type=MESH)
        return carry

    lax.fori_loop(1, 8, greet_row, 0)
    lax.fori_loop(1, 16, greet_column, 0)

    def clear(p, carry):
        pad[p] = jnp.zeros((48, 2 * CH), f32)
        dz[p] = jnp.zeros((64, CH), f32)
        return carry

    lax.fori_loop(0, 34, clear, 0)
    for k in (34, 35):
        dz[k] = jnp.zeros((64, CH), f32)

    block = 256
    upper = (iota((block, block), 0) < iota((block, block), 1)).astype(bf16)
    ahead = jnp.zeros((DEVICES, 1), f32)
    tags = jnp.zeros((DEVICES, CH), f32)
    for b in range(OBS_HERE // block):
        cols = slice(b * block, (b + 1) * block)
        to = target[:, cols]
        hit = (to == iota((DEVICES, block), 0)).astype(f32)
        hit16 = hit.astype(bf16)
        before = jnp.dot(hit16, upper, preferred_element_type=f32) + ahead
        slot = jnp.sum(hit * before, axis=0, keepdims=True)
        ahead = ahead + jnp.sum(hit, axis=1, keepdims=True)
        slot = slot.astype(jnp.int32)
        places[:, cols] = to * SLOTS + slot
        mine = (slot == iota((SLOTS, block), 0)).astype(f32)
        where = cell[:, cols]
        notes = jnp.concatenate(
            [
                mine * (where // SIDE + 1).astype(f32),
                mine * (where % SIDE + 1).astype(f32),
                mine * (instr[:, cols] + 1).astype(f32),
                jnp.zeros((SLOTS, block), f32),
            ],
            axis=0,
        ).astype(bf16)
        tags = tags + nt_dot(hit16, notes)
    for t in range(DEVICES):
        tags_out[t] = tags[t : t + 1, :]

    pl.semaphore_wait(barrier, 22)
    lax.fori_loop(1, 16, tell_column, 0)

    hi = bias[...].astype(bf16)
    rest_part = bias[...] - hi.astype(f32)
    mid = rest_part.astype(bf16)
    low = (rest_part - mid.astype(f32)).astype(bf16)
    bias3 = jnp.concatenate([hi, mid, low], axis=0)
    for b in range(OBS_HERE // block):
        cols = slice(b * block, (b + 1) * block)
        pick = (instr[:, cols] == iota((16, block), 0)).astype(f32)
        pick3 = jnp.concatenate([pick, pick, pick], axis=0).T.astype(bf16)
        offset = jnp.dot(pick3, bias3, preferred_element_type=f32)
        feat[cols, :] = (values[cols, :].astype(f32) + offset).astype(bf16)

    pl.semaphore_wait(rows_in, 15)

    my_place = pl.ds(pl.multiple_of(lax.rem(me, SIDE) * CH + me // SIDE * SLOTS, SLOTS), SLOTS)

    def send_slot(source, landing, k, to_inst, to_tile):
        t = to_inst * 8 + to_tile
        pltpu.make_async_remote_copy(
            src_ref=source.at[t],
            dst_ref=landing,
            send_sem=sems.at[k],
            recv_sem=sems.at[2 + k],
            device_id=(to_inst, to_tile),
            device_id_type=MESH,
        ).start()

    def send_tags(i, carry):
        peer = lax.rem(me + i * 37, DEVICES)
        send_slot(tags_out, tags_in.at[me], 1, peer // 8, lax.rem(peer, 8))
        return carry

    group = 8 * SLOTS

    def pack_and_send(i, carry):
        turn = lax.rem(i * 7, 16)
        to_inst = lax.rem(at["z"] + turn // 4, 4) * 4 + lax.rem(at["x"] + lax.rem(turn, 4), 4)
        spot = jnp.clip(places[...] - to_inst * group, -1, group).astype(f32).astype(bf16)
        number = iota((group, OBS_HERE), 0).astype(f32).astype(bf16)
        choose = jnp.where(spot == number, jnp.bfloat16(1), jnp.bfloat16(0))
        rows = jnp.dot(choose, feat[...], preferred_element_type=f32).astype(bf16)
        packed[pl.ds(pl.multiple_of(to_inst * 8, 8), 8)] = rows.reshape(8, SLOTS, CH)

        def send_one(j, inner_carry):
            to_tile = lax.rem(tile + j * 3, 8)

            @pl.when(to_inst * 8 + to_tile != me)
            def _():
                send_slot(packed, right.at[my_place, :CH], 0, to_inst, to_tile)

            return inner_carry

        lax.fori_loop(0, 8, send_one, 0)
        lax.fori_loop(
            jnp.minimum((i - 1) * 16 + 1, DEVICES), jnp.minimum(i * 16 + 1, DEVICES), send_tags, 0
        )
        return carry

    lax.fori_loop(1, 17, pack_and_send, 0)
    right[my_place, :CH] = packed[me]
    tags_in[me] = tags_out[me]
    others = pl.ds(0, DEVICES - 1)
    pltpu.make_async_copy(tags_in.at[others], tags_in.at[others], sems.at[3]).wait()
    every = tags_in[...].reshape(DEVICES, CH)
    for k in range(3):
        spots[k] = jnp.concatenate(
            [every[SIDE * m : SIDE * (m + 1), 32 * k : 32 * (k + 1)] for m in range(4)], axis=1
        )

    def place_group(g, carry):
        row = pl.ds(g, 1)
        lat, lon, kind = (spots[k, row, :] for k in range(3))
        number = iota((SIDE, CH), 0).astype(f32) + 1.0
        at_lon = (lon == number).astype(f32)
        cols = aligned(g, CH)
        for p in range(SIDE):
            lands[p * SIDE : (p + 1) * SIDE, cols] = jnp.where(
                lat == float(p + 1), at_lon, 0.0
            ).astype(bf16)
        which = iota((CH, CH), 0)
        kinds = jnp.where(
            which < 16, (kind == which.astype(f32) + 1.0).astype(f32), (kind > 0.0).astype(f32)
        )
        right[cols, CH:] = kinds.T.astype(bf16)
        return carry

    lax.fori_loop(0, SIDE, place_group, 0)

    half = CELLS // 2

    def go_back(i):
        rows = pl.ds(i * half, half)
        dy_here = (dyb[rows, :].astype(f32) * SCALE).astype(bf16)
        dyb[rows, :] = dy_here
        back[rows, :] = nt_dot(dy_here, w_down[...])

    loads[0].wait()
    loads[1].wait()
    go_back(0)
    landed = right.at[pl.ds(0, (DEVICES - 1) * SLOTS), :CH]
    pltpu.make_async_copy(landed, landed, sems.at[2]).wait()

    def sum_block(i, carry):
        total = jnp.dot(lands[aligned(i, half), :], right[...], preferred_element_type=f32)
        pad[pl.ds(1 + 16 * i, 16), 8:40, :] = total.reshape(16, SIDE, 2 * CH)
        return carry

    lax.fori_loop(0, 2, sum_block, 0)

    for p in range(SIDE):
        side_out[0, p : p + 1, :] = pad[1 + p, 8:9, :]
        side_out[1, p : p + 1, :] = pad[1 + p, 39:40, :]
    for k, (p, q) in enumerate(((1, 8), (1, 39), (32, 8), (32, 39))):
        corner_out[k] = pad[p, q : q + 1, :]
    north, south = lax.rem(tile + 7, 8), lax.rem(tile + 1, 8)
    west, east = lax.rem(inst + 15, 16), lax.rem(inst + 1, 16)
    halo = (
        (pad.at[1, 8:40], pad.at[33, 8:40], (inst, north)),
        (pad.at[32, 8:40], pad.at[0, 8:40], (inst, south)),
        (side_out.at[0], side_in.at[1], (west, tile)),
        (side_out.at[1], side_in.at[0], (east, tile)),
        (corner_out.at[0], corner_in.at[3], (west, north)),
        (corner_out.at[1], corner_in.at[2], (east, north)),
        (corner_out.at[2], corner_in.at[1], (west, south)),
        (corner_out.at[3], corner_in.at[0], (east, south)),
    )
    halo_copies = [
        send_to(source, landing, halo_send.at[k], halo_recv.at[k], to)
        for k, (source, landing, to) in enumerate(halo)
    ]
    go_back(1)
    for load in loads[2:]:
        load.wait()
    for copy in halo_copies:
        copy.wait_recv()
    keep_north = (tile > 0).astype(f32)
    keep_south = (tile < 7).astype(f32)
    keep_west = (inst > 0).astype(f32)
    keep_east = (inst < 15).astype(f32)
    pad[0, 8:40, :] = pad[0, 8:40, :] * keep_north
    pad[33, 8:40, :] = pad[33, 8:40, :] * keep_south
    for p in range(SIDE):
        pad[1 + p, 7:8, :] = side_in[0, p : p + 1, :] * keep_west
        pad[1 + p, 40:41, :] = side_in[1, p : p + 1, :] * keep_east
    pad[0, 7:8, :] = corner_in[0] * (keep_north * keep_west)
    pad[0, 40:41, :] = corner_in[1] * (keep_north * keep_east)
    pad[33, 7:8, :] = corner_in[2] * (keep_south * keep_west)
    pad[33, 40:41, :] = corner_in[3] * (keep_south * keep_east)

    lats = 4

    def encode(i, carry):
        spread = jnp.zeros((lats, SIDE, CH), f32)
        density = jnp.zeros((lats, SIDE, CH), f32)
        near = pl.ds(lats * i, lats + 2)
        for b in (-1, 0, 1):
            sums = pad[near, 8 + b : 40 + b, :CH]
            counts = counts_of(pad[near, 8 + b : 40 + b, CH:])
            for a in (-1, 0, 1):
                j = 3 * (a + 1) + (b + 1)
                weight = kern[j : j + 1, :].reshape(1, 1, CH)
                spread = spread + weight * sums[1 + a : 1 + a + lats]
                density = density + weight * counts[1 + a : 1 + a + lats]
        share = 1.0 / (1.0 + density)
        value = spread * share
        here = pl.ds(lats * i, lats)
        inv[here] = share
        enc32[here] = value
        enc[aligned(i, lats * SIDE), :] = value.reshape(lats * SIDE, CH).astype(bf16)
        return carry

    lax.fori_loop(0, SIDE // lats, encode, 0)
    for copy in halo_copies:
        copy.wait_send()
    for source, k in ((packed, 0), (tags_out, 1)):
        pltpu.make_async_copy(source.at[others], source.at[others], sems.at[k]).wait()

    give, keep = lands.at[:, :HALF], lands.at[:, HALF : 2 * HALF]
    g = lands.at[:, 2 * HALF : 2 * HALF + WIDTH]
    bufs = (core_in, core_sum, axis_in, axis_sum, next_in, last_in)
    outs = (o_down, o_up, o_in)
    streams = [
        Stream(k, at, give, keep, outs, bufs, send_sem, recv_sem) for k in range(len(STREAMS))
    ]
    core = at["core"]

    def forward(i, carry):
        rows = aligned(i, half)
        h = jnp.dot(enc[rows, :], w_in[...], preferred_element_type=f32)
        h0[rows, :] = h
        r = lax.rsqrt(jnp.mean(h * h, axis=-1, keepdims=True) + 1e-06)
        rinv[rows, :] = jnp.broadcast_to(r, (half, CH))
        u_here = (h * r * gain[...]).astype(bf16)
        u[rows, :] = u_here
        for n in range(WIDTH // block):
            cols = slice(n * block, (n + 1) * block)
            act = jnp.dot(u_here, w_up[:, cols], preferred_element_type=f32)
            square = act * act
            tanh = jnp.tanh(TANH_SCALE * act * (1.0 + CUBIC * square))
            cdf = 0.5 + 0.5 * tanh
            slope = cdf + act * (0.5 - 0.5 * tanh * tanh) * (
                TANH_SCALE + (3.0 * CUBIC * TANH_SCALE) * square
            )
            g[rows, cols] = (act * cdf).astype(bf16)
            dact[rows, cols] = (slope * back[rows, cols]).astype(bf16)
        return carry

    lax.fori_loop(0, CELLS // half, forward, 0)

    def weight_grad(left, right_side, into, part, first):
        cols_in = aligned(part, 512)

        def body(i, carry):
            cols = aligned(i, 512)
            into[cols, first : first + 512] = tn_dot(left[:, cols], right_side[:, cols_in]).astype(
                bf16
            )
            return carry

        lax.fori_loop(0, WIDTH // 512, body, 0)

    gain_sum[...] = jnp.zeros_like(gain_sum)

    def backward(i, carry):
        rows = pl.ds(i * half, half)
        du = nt_dot(dact[rows, :], w_up[...])
        h = h0[rows, :]
        r = rinv[rows, :1]
        gain_sum[...] += jnp.sum(du * h * r, axis=0, keepdims=True)
        scaled = du * gain[...]
        mean = jnp.mean(scaled * h, axis=-1, keepdims=True)
        dh = (r * scaled - h * (r * r * r * mean) + dyb[rows, :].astype(f32)).astype(bf16)
        u[rows, :] = dh
        denc = nt_dot(dh, w_in[...])
        lat = pl.ds(i * 16, 16)
        ds[lat] = denc.reshape(16, SIDE, CH) * inv[lat]
        return carry

    def in_grad(i, carry):
        cols = aligned(i, block)
        part = tn_dot(enc[...], u[:, cols]).T
        give[cols, 1024:] = jnp.where(core == 1, part, 0.0).astype(bf16)
        keep[cols, 1024:] = jnp.where(core == 0, part, 0.0).astype(bf16)
        return carry

    def filter_grad(i, totals):
        near, here = pl.ds(lats * i, lats + 2), pl.ds(lats * i, lats)
        slope = ds[here]
        dz[pl.ds(lats * i + 2, lats), 16:48] = slope
        both = slope * enc32[here]
        new = list(totals)
        for b in (-1, 0, 1):
            sums = pad[near, 8 + b : 40 + b, :CH]
            counts = counts_of(pad[near, 8 + b : 40 + b, CH:])
            for a in (-1, 0, 1):
                j = 3 * (a + 1) + (b + 1)
                part = slope * sums[1 + a : 1 + a + lats] - both * counts[1 + a : 1 + a + lats]
                new[j] = new[j] + jnp.sum(part.reshape(lats * 4, 8, CH), axis=0)
        return tuple(new)

    def spread_back(i, carry):
        value = jnp.zeros((2, 48, CH), f32)
        for b in (-1, 0, 1):
            slab = dz[pl.ds(2 * i, 4), 8 - b : 56 - b, :]
            for a in (-1, 0, 1):
                j = 3 * (a + 1) + (b + 1)
                value = value + kern[j : j + 1, :].reshape(1, 1, CH) * slab[1 - a : 3 - a]
        kinds = pad[pl.ds(2 * i, 2), :, CH:]
        rows = aligned(i, 96)
        for part, k in ((value, 0), (kinds, 1)):
            part = part.reshape(96, CH)
            top = part.astype(bf16)
            two[k, rows, :CH] = top
            two[k, rows, CH:] = (part - top.astype(f32)).astype(bf16)
        return carry

    def forecast(i):
        rows = pl.ds(i * half, half)
        y = h0[rows, :] + jnp.dot(g[rows, :], w_down[...], preferred_element_type=f32)
        dact[rows, :] = y.astype(bf16)

    totals = {}

    def take_filter():
        zeros = jnp.zeros((8, CH), f32)
        totals["filter"] = lax.fori_loop(0, SIDE // lats, filter_grad, (zeros,) * 9)

    def take_small():
        lax.fori_loop(0, 17, spread_back, 0)
        quarters = tn_dot(two[1], two[0])
        bias_sum = (quarters[:16, :CH] + quarters[:16, CH:]) + (
            quarters[CH : CH + 16, :CH] + quarters[CH : CH + 16, CH:]
        )
        totals["small"] = jnp.concatenate(
            [gain_sum[:, k * CH : (k + 1) * CH] for k in range(8)]
            + [jnp.sum(part, axis=0, keepdims=True) for part in totals["filter"]]
            + [jnp.zeros((7, CH), f32), bias_sum],
            axis=0,
        )

    all_small, small_levels = [], ("x", "y", "z", "core")

    def pass_small():
        level = totals.get("level", 0)
        if level:
            total = small_total(small_levels[level - 1], level - 1, boxes, totals["copies"])
        else:
            total = totals["small"]
        if level == 4:
            o_small[...] = total
            return
        totals["copies"] = small_reduce(
            at, small_levels[level], level, total, boxes, small_send, small_recv
        )
        all_small.extend(totals["copies"])
        totals["level"] = level + 1

    stores = []

    def store(source, landing):
        stores.append(pltpu.make_async_copy(source, landing, load_sem.at[4 + len(stores)]))
        stores[-1].start()

    def last_forecast():
        forecast(1)
        store(dact, y_hbm)

    tasks = {
        "gd0": lambda: weight_grad(g, dyb, give, 1 - core, 0),
        "gd1": lambda: weight_grad(g, dyb, keep, core, 0),
        "gu0": lambda: weight_grad(u, dact, give, 1 - core, 512),
        "gu1": lambda: weight_grad(u, dact, keep, core, 512),
        "b0": lambda: backward(0, 0),
        "b1": lambda: backward(1, 0),
        "i": lambda: lax.fori_loop(0, WIDTH // block, in_grad, 0),
        "f": take_filter,
        "t": take_small,
        "s": pass_small,
        "y0": lambda: forecast(0),
        "y1": last_forecast,
    }
    for task in PLAN:
        if task in tasks:
            tasks[task]()
            continue
        streams[task].advance()
        if streams[0].done == 8 and streams[1].done == 8 and task in (0, 1):
            store(o_down, down_hbm)
        if all(streams[k].done == 8 for k in (2, 3, 4)) and task in (2, 3, 4):
            store(o_up, up_hbm)
    store(o_in, in_hbm)
    for s in streams:
        s.finish()
    for copy in all_small:
        copy.wait_send()
    for copy in stores:
        copy.wait()


def step(values, instr, target, cell, bias, kern, gain, w_in, w_up, w_down, cot):
    vmem, hbm = pl.BlockSpec(memory_space=pltpu.VMEM), pl.BlockSpec(memory_space=pl.ANY)
    return pl.pallas_call(
        step_kernel,
        out_shape=(
            jax.ShapeDtypeStruct((CELLS, WIDTH), bf16),
            jax.ShapeDtypeStruct((WIDTH, WIDTH), bf16),
            jax.ShapeDtypeStruct((WIDTH, WIDTH), bf16),
            jax.ShapeDtypeStruct((WIDTH, 2 * CH), bf16),
            jax.ShapeDtypeStruct((40, CH), f32),
        ),
        in_specs=[vmem] * 7 + [hbm] * 4,
        out_specs=[hbm] * 4 + [vmem],
        scratch_shapes=[
            pltpu.VMEM((OBS_HERE, CH), bf16),
            pltpu.VMEM((1, OBS_HERE), jnp.int32),
            pltpu.VMEM((DEVICES, SLOTS, CH), bf16),
            pltpu.VMEM((DEVICES, 1, CH), f32),
            pltpu.VMEM((DEVICES, 1, CH), f32),
            pltpu.VMEM((CELLS, DEVICES * SLOTS), bf16),
            pltpu.VMEM((DEVICES * SLOTS, 2 * CH), bf16),
            pltpu.VMEM((3, SIDE, CH), f32),
            pltpu.VMEM((34, 48, 2 * CH), f32),
            pltpu.VMEM((2, SIDE, 2 * CH), f32),
            pltpu.VMEM((2, SIDE, 2 * CH), f32),
            pltpu.VMEM((4, 1, 2 * CH), f32),
            pltpu.VMEM((4, 1, 2 * CH), f32),
            pltpu.SemaphoreType.DMA((4,)),
            pltpu.SemaphoreType.DMA((8,)),
            pltpu.SemaphoreType.DMA((8,)),
            pltpu.SemaphoreType.REGULAR,
            pltpu.VMEM((WIDTH, WIDTH), bf16),
            pltpu.VMEM((WIDTH, WIDTH), bf16),
            pltpu.VMEM((WIDTH, 2 * CH), bf16),
            pltpu.VMEM((CELLS, CH), bf16),
            pltpu.VMEM((SIDE, SIDE, CH), f32),
            pltpu.VMEM((SIDE, SIDE, CH), f32),
            pltpu.VMEM((CH, WIDTH), bf16),
            pltpu.VMEM((WIDTH, WIDTH), bf16),
            pltpu.VMEM((WIDTH, WIDTH), bf16),
            pltpu.VMEM((CELLS, WIDTH), bf16),
            pltpu.VMEM((CELLS, WIDTH), f32),
            pltpu.VMEM((CELLS, WIDTH), f32),
            pltpu.VMEM((CELLS, CH), f32),
            pltpu.VMEM((CELLS, WIDTH), bf16),
            pltpu.VMEM((CELLS, WIDTH), bf16),
            pltpu.VMEM((SIDE, SIDE, CH), f32),
            pltpu.VMEM((36, 64, CH), f32),
            pltpu.VMEM((2, 34 * 48, 2 * CH), bf16),
            pltpu.VMEM((1, WIDTH), f32),
            pltpu.VMEM((4, 4, 40, CH), f32),
            pltpu.SemaphoreType.DMA((8,)),
            pltpu.SemaphoreType.DMA((12,)),
            pltpu.SemaphoreType.DMA((12,)),
        ]
        + reduce_scratch(),
        compiler_params=pltpu.CompilerParams(
            collective_id=0, has_side_effects=True, vmem_limit_bytes=62 << 20
        ),
    )(values, instr, target, cell, bias, kern, gain, w_in, w_up, w_down, cot)


def widen_kernel(
    y, down, up, into, small, y_out, down_out, up_out, in_out, gain, kern, bias, *scratch
):
    y_in, down_in, up_in, in_in, down_wide, up_wide, in_wide, sems, out_sems = scratch
    size, parts = 256, 4
    rows = [pl.ds(k * size, size) for k in range(parts)]
    loads = [pltpu.make_async_copy(into, in_in, sems.at[0])]
    for k in range(parts):
        for which, (source, landing) in enumerate(((down, down_in), (up, up_in), (y, y_in))):
            loads.append(
                pltpu.make_async_copy(
                    source.at[rows[k]], landing.at[rows[k]], sems.at[1 + 3 * k + which]
                )
            )
    for load in loads:
        load.start()
    stores = []
    gain[...] = small[:8]
    kern[...] = small[8:17]
    bias[...] = small[24:40]
    loads[0].wait()
    for k in range(parts):
        in_wide[:, k * size : (k + 1) * size] = in_in[rows[k], :CH].astype(f32).T
    stores.append(pltpu.make_async_copy(in_wide, in_out, out_sems.at[0]))
    stores[0].start()
    for k in range(parts):
        for which, (narrow, wide, landing) in enumerate(
            ((down_in, down_wide, down_out), (up_in, up_wide, up_out), (y_in, y_in, y_out))
        ):
            loads[1 + 3 * k + which].wait()
            if which < 2:
                wide[rows[k], :] = narrow[rows[k], :].astype(f32)
            stores.append(
                pltpu.make_async_copy(
                    wide.at[rows[k]], landing.at[rows[k]], out_sems.at[1 + 3 * k + which]
                )
            )
            stores[-1].start()
    for store in stores:
        store.wait()


def widen(y, down, up, into, small):
    vmem, hbm = pl.BlockSpec(memory_space=pltpu.VMEM), pl.BlockSpec(memory_space=pl.ANY)
    return pl.pallas_call(
        widen_kernel,
        out_shape=(
            jax.ShapeDtypeStruct((CELLS, WIDTH), bf16),
            jax.ShapeDtypeStruct((WIDTH, WIDTH), f32),
            jax.ShapeDtypeStruct((WIDTH, WIDTH), f32),
            jax.ShapeDtypeStruct((CH, WIDTH), f32),
            jax.ShapeDtypeStruct((8, CH), f32),
            jax.ShapeDtypeStruct((9, CH), f32),
            jax.ShapeDtypeStruct((16, CH), f32),
        ),
        in_specs=[hbm] * 4 + [vmem],
        out_specs=[hbm] * 4 + [vmem] * 3,
        scratch_shapes=[
            pltpu.VMEM((CELLS, WIDTH), bf16),
            pltpu.VMEM((WIDTH, WIDTH), bf16),
            pltpu.VMEM((WIDTH, WIDTH), bf16),
            pltpu.VMEM((WIDTH, 2 * CH), bf16),
            pltpu.VMEM((WIDTH, WIDTH), f32),
            pltpu.VMEM((WIDTH, WIDTH), f32),
            pltpu.VMEM((CH, WIDTH), f32),
            pltpu.SemaphoreType.DMA((13,)),
            pltpu.SemaphoreType.DMA((13,)),
        ],
        compiler_params=pltpu.CompilerParams(vmem_limit_bytes=60 << 20),
    )(y, down, up, into, small)


def shards(
    obs_values,
    obs_instrument,
    obs_target,
    obs_cell,
    inst_bias,
    kernel,
    w_in,
    norm_gain,
    w_up,
    w_down,
    cotangent,
):
    y, down, up, into, small = step(
        obs_values,
        obs_instrument.reshape(1, OBS_HERE),
        obs_target.reshape(1, OBS_HERE),
        obs_cell.reshape(1, OBS_HERE),
        inst_bias,
        kernel,
        norm_gain.reshape(1, WIDTH),
        w_in,
        w_up,
        w_down,
        cotangent.reshape(CELLS, WIDTH),
    )
    y, down, up, into, gain, filters, bias = widen(y, down, up, into, small)
    return (y.reshape(cotangent.shape), into, up, down, gain.reshape(WIDTH), filters, bias)


def solution(mesh):
    return jax.shard_map(
        shards,
        mesh=mesh,
        in_specs=(
            P(("inst", "tile"), None),
            P(("inst", "tile")),
            P(("inst", "tile"), None),
            P(("inst", "tile")),
            P(),
            P(),
            P(),
            P(),
            P(),
            P(),
            P("tile", "inst", None),
        ),
        out_specs=(P("tile", "inst", None), P(), P(), P(), P(), P(), P()),
        check_vma=False,
    )
```
